32 devices in a mesh: atoms: 8 (over z, y), grp: 4 (over x, core).
Axes of the slice: x: 2, y: 2, z: 4, core: 2. Of those that a mesh axis runs over, the one named last changes fastest.
Arguments:
- params: float32 [89344], replicated
- first_moment: float32 [89344], replicated, may hold values from -2.2888184e-05 to 2.2888184e-05
- second_moment: float32 [89344], replicated, may hold values from 1.1192694e-12 to 4.4770776e-12
- average: float32 [89344], replicated
- edge_vectors: float32 [3, 4, 8192], P(None, 'grp', 'atoms'), as said below
- owner_rank: int32 [4, 8192, 1], P('grp', 'atoms'), may hold values from 0 to 7; in each aligned block of 1024 rows (0 to 1023, 1024 to 2047, ..., all dimensions but the last counted through in order) at most 256 rows name the same one
- neighbour_local: int32 [4, 8192], P('grp', 'atoms'), may hold values from 0 to 31
- centre_species: int32 [4, 256], P('grp', 'atoms'), may hold values from 0 to 4
- neighbour_species: int32 [4, 8192], P('grp', 'atoms'), may hold values from 0 to 4
- live_atoms: int32 [4, 8], P('grp', 'atoms'), may hold values from 1 to 32, as said below
- target_forces: float32 [3, 4, 256], P(None, 'grp', 'atoms'), may hold values from -6 to 6
Outputs:
- loss_sum: float32 [], replicated
- count: float32 [], replicated
- grad_norm: float32 [], replicated
- forces: float32 [3, 4, 256], P(None, 'grp', 'atoms')
- new_first: float32 [89344], replicated
- new_second: float32 [89344], replicated
- new_params: float32 [89344], replicated
- low_params: bfloat16 [89344], replicated
- new_average: float32 [89344], replicated
The draws below stay inside these ranges and needn't reach their ends.
Inputs may be any that keep to these rules, and one draw needn't show every extreme that they name: `owner_rank`: among the 1024 edges of one device, at most 256 have their neighbour on any one owner, a bound that some block reaches. `live_atoms`: A device's true atoms are its first ones; some device has all 32. `edge_vectors`: edge lengths lie between 0.9 and 4.8.
All inputs are finite; a program needn't handle non-finite values.
Results may differ from the reference program's by a relative error of at most 0.001.
Values sent between devices are 32-bit elements; how exact they have to be, the bound alone decides.
No kernel may reach another device: no remote copies, remote signals or barrier semaphores. Data moves between devices by JAX's collectives and lax.ppermute only.
A program may use at most 128 MiB of HBM per device.

```python
import math
import jax
import jax.numpy as jnp
import numpy as np
from jax import lax

LATENT = 64
UNITS = 128
CHANNELS = 32
BASES = 8
SPECIES = 5
LAYERS = 3
STEP = 10
NEI = 32
A_DEV = 32
E_DEV = 1024
ATOMS_G = 256
EDGES_G = 8192
CAP = 256
NPARAM = 89344
N_ATOMS = 8
N_GRP = 4


def layered_scales():
    fans = [(BASES + 2 * SPECIES, (BASES + 2 * SPECIES) * LATENT), (LATENT, LAYERS * LATENT * 2 * CHANNELS), (3 * CHANNELS, LAYERS * 3 * CHANNELS * LATENT), (LATENT, LAYERS * LATENT * UNITS), (UNITS, LAYERS * UNITS * LATENT), (LATENT, LATENT * UNITS), (UNITS, UNITS)]
    return jnp.concatenate([jnp.full((amount,), fan ** (-0.5), jnp.float32) for fan, amount in fans])


def layered_values(key):
    scales = layered_scales()
    values = jax.random.normal(key, scales.shape, jnp.float32)
    return values * scales


def draw_params(key, part):
    key = jax.random.fold_in(key, 3)
    return layered_values(key)


def draw_average(key, part):
    key = jax.random.fold_in(key, 7)
    return layered_values(key)


def draw_edge_vectors(key, part):
    key = jax.random.fold_in(key, 11)
    first, second, third = jax.random.split(key, 3)
    shape = (N_GRP, EDGES_G)
    distance = jax.random.uniform(first, shape, jnp.float32, 0.9, 4.8)
    cosine = jax.random.uniform(second, shape, jnp.float32, -1.0, 1.0)
    azimuth = jax.random.uniform(third, shape, jnp.float32, -math.pi, math.pi)
    sine = jnp.sqrt(jnp.maximum(1.0 - cosine * cosine, 0.0))
    return jnp.stack([distance * sine * jnp.cos(azimuth), distance * sine * jnp.sin(azimuth), distance * cosine])


def draw_live_atoms(key, part):
    key = jax.random.fold_in(key, 5)
    total = N_GRP * N_ATOMS
    places = jnp.arange(total, dtype=jnp.int32)
    lowest = A_DEV // 3
    rising = lowest + (A_DEV - lowest) * places // (total - 1)
    removed = jax.random.randint(key, (total,), 0, A_DEV // 4 + 1)
    live = jnp.where(places == total - 1, A_DEV, jnp.maximum(rising - removed, 1))
    return live.astype(jnp.int32).reshape(N_GRP, N_ATOMS)


def place_ends(values, stream_key, smallest, top_value):
    dims = values.shape
    spot = [jax.random.randint(jax.random.fold_in(stream_key, axis), (), 0, dims[axis]) for axis in range(len(dims))]
    values = values.at[tuple(spot)].set(smallest)
    longest = dims.index(max(dims))
    spot[longest] = (spot[longest] + 1) % dims[longest]
    return values.at[tuple(spot)].set(top_value)


def shard_levels(rng, shape, shards, smallest, top_value):
    factor_of = 1.0
    for position, shards_of in shards:
        heights = jax.random.uniform(jax.random.fold_in(jax.random.fold_in(rng, 6), position), (shards_of,), jnp.float32, smallest / len(shards), top_value / len(shards))
        factor_of = factor_of * jnp.repeat(jnp.exp(heights), shape[position] // shards_of).reshape((-1,) + (1,) * (len(shape) - 1 - position))
    return factor_of


def assign_block(rng, own, number, rows, count, top, bound, lean):
    order = jax.random.permutation(rng, count)
    heavy_load, common = portions_of(count, rows * top, bound, lean, True), portions_of(count, rows * top, bound, lean, False)
    places = jnp.arange(count)

    def named(lengths, turn):
        used = int((lengths > 0).sum())
        fixed = max(1, used // 4)
        passed = fixed + (places - fixed + turn * (used - fixed)) % max(1, count - fixed)
        return jnp.zeros((count,), jnp.int32).at[order[jnp.where(places < fixed, places, passed)]].set(jnp.asarray(lengths, jnp.int32))

    lengths = jnp.where(number % 4 == 0, named(heavy_load, number // 4), named(common, number - number // 4 - 1))
    mixed = jax.random.permutation(jax.random.fold_in(own, 3), count)
    giver, receiver = mixed[0:count // 2 * 2:2], mixed[1:count // 2 * 2:2]
    margin = jnp.minimum(lengths[giver] - 1, bound - lengths[receiver]) // 2
    margin = jnp.where((giver == order[0]) | (receiver == order[0]) | (lengths[receiver] == 0), 0, jnp.maximum(margin, 0))
    passed = jax.random.randint(jax.random.fold_in(own, 4), (count // 2,), 0, 1 << 20) % (margin + 1)
    lengths = lengths.at[giver].add(-passed).at[receiver].add(passed)
    labels = jnp.searchsorted(jnp.cumsum(lengths), jnp.arange(rows * top), side="right").astype(jnp.int32)
    grid = labels.reshape(top, rows).T
    grid = grid[jax.random.permutation(jax.random.fold_in(own, 1), rows)]
    turn = jax.random.randint(jax.random.fold_in(own, 2), (rows, 1), 0, top)
    return jnp.take_along_axis(grid, (jnp.arange(top)[None, :] + turn) % top, axis=1)


def portions_of(count, total, most, slope, full):
    portions = [(1 << 20) // math.isqrt(grade ** slope) + 1 for grade in range(1, count + 1)]
    largest = most if full else min(most, max(-(-total // count), total * portions[0] // sum(portions)))
    least = 1 if total - largest >= count - 1 else 0
    holding, spare = [largest] + [least] * (count - 1), total - largest - least * (count - 1)
    while spare > 0:
        movable = [i for i in range(1, count) if holding[i] < largest] or [i for i in range(1, count) if holding[i] < most]
        whole, remaining = sum([portions[i] for i in movable]), spare
        for i in movable:
            extra = min(most - holding[i], max(1, remaining * portions[i] // whole), spare)
            holding[i] = holding[i] + extra
            spare = spare - extra
    return np.array(holding)


def noise(key, shape, scale, bound, cuts=(), kind=jnp.bfloat16):
    values = scale * jax.random.normal(key, shape, jnp.float32)
    if cuts:
        values = values * shard_levels(key, shape, cuts, -0.22, 0.18)
    return jnp.clip(values, -bound, bound).astype(kind)


def setup_inputs(seed: int = 0) -> dict:
    streams_of = jax.random.split(jax.random.key(seed), 12)
    params = draw_params(jax.random.fold_in(streams_of[11], 71), 0)
    first_moment = noise(streams_of[1], (NPARAM,), (0.0011 * NPARAM ** -0.5), 2.288818359375e-05, (), jnp.float32)
    second_moment = jnp.clip(jnp.exp(jax.random.uniform(streams_of[2], (NPARAM,), jnp.float32, math.log(1.119269390711941e-12), math.log(4.477077562847764e-12))), 1.119269390711941e-12, 4.477077562847764e-12)
    average = draw_average(jax.random.fold_in(streams_of[11], 71), 0)
    edge_vectors = draw_edge_vectors(jax.random.fold_in(streams_of[11], 71), 0)
    owner_rank_keys = jax.random.split(jax.random.fold_in(streams_of[5], 1), N_GRP * EDGES_G // E_DEV)
    owner_rank_turns = jax.random.permutation(jax.random.fold_in(streams_of[5], 3), N_GRP * EDGES_G // E_DEV)
    owner_rank = jax.vmap(lambda own, number: assign_block(jax.random.fold_in(streams_of[5], 2), own, number, E_DEV, N_ATOMS, 1, CAP, 2))(owner_rank_keys, owner_rank_turns).reshape((N_GRP, EDGES_G, 1))
    neighbour_local = place_ends(jax.random.randint(streams_of[6], (N_GRP, EDGES_G), 0, A_DEV), jax.random.fold_in(streams_of[6], 1), 0, A_DEV - 1).astype(jnp.int32)
    centre_species = place_ends(jax.random.randint(streams_of[7], (N_GRP, ATOMS_G), 0, SPECIES), jax.random.fold_in(streams_of[7], 1), 0, SPECIES - 1).astype(jnp.int32)
    neighbour_species = place_ends(jax.random.randint(streams_of[8], (N_GRP, EDGES_G), 0, SPECIES), jax.random.fold_in(streams_of[8], 1), 0, SPECIES - 1).astype(jnp.int32)
    live_atoms = draw_live_atoms(jax.random.fold_in(streams_of[11], 71), 0)
    target_forces = noise(streams_of[10], (3, N_GRP, ATOMS_G), 1.0, 6.0, ((1, 4), (2, 8)), jnp.float32)
    return {"params": params, "first_moment": first_moment, "second_moment": second_moment, "average": average, "edge_vectors": edge_vectors, "owner_rank": owner_rank, "neighbour_local": neighbour_local, "centre_species": centre_species, "neighbour_species": neighbour_species, "live_atoms": live_atoms, "target_forces": target_forces}


@jax.custom_vjp
def low(v):
    return lax.optimization_barrier(v.astype(jnp.bfloat16)).astype(jnp.float32)

@jax.custom_vjp
def low_back(v):
    return v

def low_keep(v):
    return (low(v), None)

def low_pass(kept, grad):
    return (grad,)

def back_keep(v):
    return (v, None)

def back_low(kept, grad):
    return (low(grad),)
low.defvjp(low_keep, low_pass)
low_back.defvjp(back_keep, back_low)
cutoff_radius = 5.0
clip_level = 0.01
learn_rate = 0.1
beta_one = 0.9
beta_two = 0.999
epsilon_adam = 1e-08
decay_rate = 0.01
average_keep = 0.99

def dense(left, right):
    return jnp.dot(left, right, precision=lax.Precision.HIGHEST)

def unpack(flat):
    shapes = [(BASES + 2 * SPECIES, LATENT), (LAYERS, LATENT, 2 * CHANNELS), (LAYERS, 3 * CHANNELS, LATENT), (LAYERS, LATENT, UNITS), (LAYERS, UNITS, LATENT), (LATENT, UNITS), (UNITS,)]
    pieces = []
    offset = 0
    for shape_now in shapes:
        amount = math.prod(shape_now)
        pieces.append(flat[offset:offset + amount].reshape(shape_now))
        offset = offset + amount
    return pieces

def edge_energy(flat, vectors, centre_kind, neighbour_kind):
    embed_w, env_w, inv_w, first_w, second_w, head_w, head_v = unpack(flat)
    edges = vectors.shape[1]
    atoms = centre_kind.shape[0]
    along_x, along_y, along_z = (vectors[0], vectors[1], vectors[2])
    distance = jnp.sqrt(along_x * along_x + along_y * along_y + along_z * along_z)
    unit_x, unit_y, unit_z = (along_x / distance, along_y / distance, along_z / distance)
    scaled = distance / cutoff_radius
    envelope = 1.0 - 28.0 * scaled ** 6 + 48.0 * scaled ** 7 - 21.0 * scaled ** 8
    orders = jnp.arange(1, BASES + 1).astype(vectors.dtype)
    bessel = math.sqrt(2.0 / cutoff_radius) * jnp.sin(orders[:, None] * math.pi * scaled[None, :]) / distance[None, :]
    kinds = jnp.arange(SPECIES, dtype=jnp.int32)
    centre_edge = jnp.repeat(centre_kind, NEI)
    centre_hot = (centre_edge[None, :] == kinds[:, None]).astype(vectors.dtype)
    neighbour_hot = (neighbour_kind[None, :] == kinds[:, None]).astype(vectors.dtype)
    features = jnp.concatenate([bessel * envelope[None, :], centre_hot, neighbour_hot], 0)
    latent = jax.nn.silu(dense(features.T, embed_w))
    root_three, root_five, root_fifteen = (math.sqrt(3.0), math.sqrt(5.0), math.sqrt(15.0))
    harmonics = jnp.stack([jnp.ones_like(unit_x), root_three * unit_x, root_three * unit_y, root_three * unit_z, root_fifteen * unit_x * unit_y, root_fifteen * unit_y * unit_z, 0.5 * root_five * (3.0 * unit_z * unit_z - 1.0), root_fifteen * unit_x * unit_z, 0.5 * root_fifteen * (unit_x * unit_x - unit_y * unit_y)], 1)
    tensor = jnp.broadcast_to(harmonics[:, :, None], (edges, 9, CHANNELS))
    for level in range(LAYERS):
        mixed = dense(latent, env_w[level])
        weights_env = mixed[:, :CHANNELS] * envelope[:, None]
        weights_edge = mixed[:, CHANNELS:]
        spread = weights_env[:, None, :] * harmonics[:, :, None]
        environment = spread.reshape(atoms, NEI, 9, CHANNELS).sum(1) / math.sqrt(NEI)
        environment = jnp.repeat(environment, NEI, axis=0)
        weighted = weights_edge[:, None, :] * tensor
        product = weighted * environment
        invariants = jnp.concatenate([product[:, 0], product[:, 1:4].sum(1), product[:, 4:].sum(1)], 1)
        tensor = 0.7071 * (weighted * environment[:, 0:1] + environment * weighted[:, 0:1])
        inner = latent + dense(invariants, inv_w[level])
        latent = latent + envelope[:, None] * dense(jax.nn.silu(dense(inner, first_w[level])), second_w[level])
    energies = dense(jax.nn.silu(dense(latent, head_w)), head_v) * envelope
    return jnp.sum(energies)

def adam_update(weights, moment_one, moment_two, smoothed, gradient):
    moment_one = beta_one * moment_one + (1.0 - beta_one) * gradient
    moment_two = beta_two * moment_two + (1.0 - beta_two) * gradient * gradient
    corrected_one = moment_one / (1.0 - beta_one ** STEP)
    corrected_two = moment_two / (1.0 - beta_two ** STEP)
    weights = weights - learn_rate * (corrected_one / (jnp.sqrt(corrected_two) + epsilon_adam) + decay_rate * weights)
    smoothed = average_keep * smoothed + (1.0 - average_keep) * weights
    return (weights, moment_one, moment_two, smoothed)

def reference(params, first_moment, second_moment, average, edge_vectors, owner_rank, neighbour_local, centre_species, neighbour_species, live_atoms, target_forces):
    blocks = N_GRP * N_ATOMS
    vectors = edge_vectors.reshape(3, blocks, E_DEV).transpose(1, 0, 2)
    centre_blocks = centre_species.reshape(blocks, A_DEV)
    neighbour_blocks = neighbour_species.reshape(blocks, E_DEV)
    group_ids = jnp.arange(N_GRP, dtype=jnp.int32)[:, None]
    target_index = (group_ids * ATOMS_G + owner_rank[:, :, 0] * A_DEV + neighbour_local).reshape(-1)
    atom_local = jnp.arange(ATOMS_G, dtype=jnp.int32) % A_DEV
    atom_block = jnp.arange(ATOMS_G, dtype=jnp.int32) // A_DEV
    mask = (atom_local[None, :] < live_atoms[:, atom_block]).astype(jnp.float32)
    count = 3.0 * jnp.sum(live_atoms).astype(jnp.float32)

    def loss_of(flat):

        def block(inputs):
            return jax.grad(edge_energy, argnums=1)(flat, inputs[0], inputs[1], inputs[2])
        slopes = lax.map(jax.checkpoint(block), (vectors, centre_blocks, neighbour_blocks))
        centre_part = slopes.reshape(blocks, 3, A_DEV, NEI).sum(3).transpose(1, 0, 2).reshape(3, N_GRP * ATOMS_G)
        edge_part = slopes.transpose(1, 0, 2).reshape(3, N_GRP * EDGES_G)
        total = centre_part + jnp.zeros_like(centre_part).at[:, target_index].add(-edge_part)
        total = total.reshape(3, N_GRP, ATOMS_G)
        error = total - target_forces
        return (jnp.sum(mask[None] * error * error), total)
    loss_sum, pullback, forces = jax.vjp(loss_of, params, has_aux=True)
    grads = pullback(jnp.ones_like(loss_sum))[0] / count
    grad_norm = jnp.sqrt(jnp.sum(grads * grads))
    clipped = grads * (clip_level / jnp.maximum(grad_norm, clip_level))
    new_params, new_first, new_second, new_average = adam_update(params, first_moment, second_moment, average, clipped)
    return (loss_sum, count, grad_norm, forces, new_first, new_second, new_params, new_params.astype(jnp.bfloat16), new_average)
```

```python
import functools
import math

import jax
import jax.numpy as jnp
from jax import lax
from jax.experimental import pallas as pl
from jax.experimental.pallas import tpu as pltpu
from jax.sharding import Mesh
from jax.sharding import PartitionSpec as P

LATENT = 64
UNITS = 128
CHANNELS = 32
BASES = 8
SPECIES = 5
LAYERS = 3
STEP = 10
NEI = 32
NPARAM = 89344

cutoff_radius = 5.0
clip_level = 0.01
learn_rate = 0.1
beta_one = 0.9
beta_two = 0.999
epsilon_adam = 1e-08
decay_rate = 0.01
average_keep = 0.99
mix = 0.7071

f32 = jnp.float32
bf16 = jnp.bfloat16

ATOMS = 32
EDGES = 1024
TILES = 8
CH = 256
CHUNKS = EDGES // CH
FEAT = 32

AT_EMBED = 0
AT_ENV = 9
AT_INV = AT_ENV + 96
AT_ONE = AT_INV + 144
AT_TWO = AT_ONE + 192
AT_HEAD = AT_TWO + 192
AT_VEC = AT_HEAD + 64
ROWS = AT_VEC + 1
PADDED = 768
HALF = PADDED // 2

STATE = [
    ("wf_emb", (LATENT, 3 * FEAT), bf16),
    ("wf_env", (3, 64, 192), bf16),
    ("wb_env", (3, 64, 192), bf16),
    ("wf_inv", (3, 64, 288), bf16),
    ("wb_inv", (3, 96, 192), bf16),
    ("wf_one", (3, 128, 192), bf16),
    ("wb_one", (3, 64, 384), bf16),
    ("wf_two", (3, 64, 384), bf16),
    ("wb_two", (3, 128, 192), bf16),
    ("wf_head", (128, 192), bf16),
    ("wb_head", (64, 384), bf16),
    ("whcol", (128, 128), f32),
    ("place", (3, 8, 128), f32),
    ("owner", (8, 128), jnp.int32),
    ("hot", (ATOMS, EDGES), bf16),
    ("geo", (10, 8, 128), f32),
    ("bes", (2, BASES, EDGES), f32),
    ("phi", (2 * FEAT, EDGES), bf16),
    ("latx", (4, 128, EDGES), bf16),
    ("pq", (3, 64, EDGES), f32),
    ("vv", (3, 64, EDGES), f32),
    ("ivx", (3, 192, EDGES), bf16),
    ("inx", (3, 128, EDGES), bf16),
    ("sx", (3, 256, EDGES), bf16),
    ("s1", (3, 128, EDGES), f32),
    ("t2", (3, 128, EDGES), f32),
    ("oo", (3, 64, EDGES), f32),
    ("lb", (3, 64, EDGES), f32),
    ("ob", (3, 128, EDGES), bf16),
    ("hb", (3, 256, EDGES), bf16),
    ("ib", (3, 128, EDGES), bf16),
    ("vb", (3, 96, EDGES), f32),
    ("ab", (3, 32, EDGES), f32),
    ("pb", (3, 128, EDGES), bf16),
    ("qq", (3, 32, EDGES), f32),
    ("qb", (3, 32, EDGES), f32),
    ("z1", (64, EDGES), f32),
    ("tz", (64, EDGES), f32),
    ("zb", (128, EDGES), bf16),
    ("sh", (128, EDGES), f32),
    ("h1", (128, EDGES), f32),
    ("h2", (128, EDGES), f32),
    ("hhb", (256, EDGES), bf16),
    ("env", (3, 9, 32, 128), f32),
    ("eh", (3, 8, 32, 128), f32),
    ("bb", (3, 3, 32, 128), f32),
    ("eb", (3, 9, 32, 128), f32),
    ("cot", (3, 11, 32, 128), f32),
]

SCRATCH_A = [
    ("tmp", (128, 128), f32),
    ("run", (64, EDGES), f32),
    ("ybar", (9, 8, 8, 128), f32),
    ("dbar", (8, 8, 128), f32),
]

SCRATCH_B = [
    ("tmp", (128, 128), f32),
    ("run", (64, EDGES), f32),
    ("cdir", (3, 8, 128), f32),
    ("gd", (10, 8, 128), f32),
    ("phid", (2 * FEAT, EDGES), bf16),
    ("zd", (64, EDGES), f32),
    ("latd", (4, 128, EDGES), bf16),
    ("pqd", (3, 64, EDGES), f32),
    ("vvd", (3, 64, EDGES), f32),
    ("qd", (3, 32, EDGES), f32),
    ("ivd", (3, 192, EDGES), bf16),
    ("ind", (3, 128, EDGES), bf16),
    ("hd", (3, 128, EDGES), f32),
    ("sd", (3, 256, EDGES), bf16),
    ("envd", (3, 9, 32, 128), f32),
    ("ehd", (3, 8, 32, 128), f32),
    ("bd", (3, 3, 32, 128), f32),
    ("hht", (256, EDGES), bf16),
    ("ot", (128, EDGES), bf16),
    ("ht", (256, EDGES), bf16),
    ("it", (128, EDGES), bf16),
    ("vt", (96, EDGES), f32),
    ("qt", (3, 32, EDGES), f32),
    ("pt", (128, EDGES), bf16),
    ("zt", (128, EDGES), bf16),
    ("et", (3, 9, 32, 128), f32),
    ("cott", (11, 32, 128), f32),
    ("grad", (PADDED, 128), f32),
]


class Refs:
    def __init__(self, entries, refs):
        for (name, _, _), ref in zip(entries, refs, strict=True):
            setattr(self, name, ref)


def split(x):
    high = x.astype(bf16)
    return high, (x - high.astype(f32)).astype(bf16)


def product(weights, high, low):
    return jnp.dot(
        weights, jnp.concatenate([high, low, high], 0), preferred_element_type=f32
    )


def put(ref, rows, columns, value, lead=()):
    high, low = split(value)
    half = ref.shape[-2] // 2
    ref[(*lead, slice(rows, rows + value.shape[0]), columns)] = high
    ref[(*lead, slice(half + rows, half + rows + value.shape[0]), columns)] = low
    return high, low


def pair(ref, columns, lead=()):
    half = ref.shape[-2] // 2
    return ref[(*lead, slice(0, half), columns)], ref[(*lead, slice(half, 2 * half), columns)]


def spin(x, amount):
    return pltpu.roll(x, amount % 128, 1)


def group_sum(x):
    x = x + spin(x, 64)
    return x + spin(x, 32)


def lanes(shape):
    return lax.broadcasted_iota(jnp.int32, shape, len(shape) - 1)


def rows_of(shape):
    return lax.broadcasted_iota(jnp.int32, shape, len(shape) - 2)


def silu_parts(h):
    gate = 1.0 / (1.0 + jnp.exp(-h))
    slope = gate * (1.0 - gate)
    return h * gate, gate + h * slope, slope * (2.0 + h * (1.0 - 2.0 * gate))


def geometry(x, y, z):
    d = jnp.sqrt(x * x + y * y + z * z)
    u, v, w = x / d, y / d, z / d
    s = d / cutoff_radius
    s2 = s * s
    s6 = s2 * s2 * s2
    f = 1.0 - 28.0 * s6 + 48.0 * (s6 * s) - 21.0 * (s6 * s2)
    r3, r5, r15 = math.sqrt(3.0), math.sqrt(5.0), math.sqrt(15.0)
    harmonics = [
        r3 * u,
        r3 * v,
        r3 * w,
        r15 * u * v,
        r15 * v * w,
        0.5 * r5 * (3.0 * w * w - 1.0),
        r15 * u * w,
        0.5 * r15 * (u * u - v * v),
    ]
    return d, f, harmonics


def dots(left, right):
    total = left[0] * right[0]
    for a, b in zip(left[1:], right[1:], strict=True):
        total = total + a * b
    return total


def degree(m):
    return 1 if m <= 3 else 2


def atom_terms(envs):
    if len(envs) == 1:
        (one,) = envs
        zero = jnp.zeros_like(one[0])
        return [one[0], zero, zero], one[1:]
    if len(envs) == 2:
        one, two = envs
        return (
            [2.0 * one[0] * two[0], dots(one[1:4], two[1:4]), dots(one[4:], two[4:])],
            [one[0] * two[m] for m in range(1, 9)],
        )
    one, two, three = envs
    both = one[0] * two[0]
    twice = 2.0 * one[0]
    part = [two[0] * one[m] + twice * two[m] for m in range(1, 9)]
    return (
        [4.0 * both * three[0], dots(part[:3], three[1:4]), dots(part[3:], three[4:])],
        [both * three[m] for m in range(1, 9)],
    )


def atom_back(envs, cots):
    return jax.vjp(atom_terms, envs)[1](cots)[0]


def tile(t):
    return slice(128 * t, 128 * t + 128)


def chunk(c):
    return slice(CH * c, CH * c + CH)


def wide(ref, index, c):
    per = CH // 128
    return jnp.concatenate([ref[index, t : t + 1, :] for t in range(per * c, per * c + per)], 1)


def fold(value):
    total = value[0:8]
    for r in range(8, value.shape[0], 8):
        total = total + value[r : r + 8]
    return total


def unpack(packed, count, tmp):
    half = count // 2
    tmp[pl.ds(0, half, stride=2), :] = packed
    tmp[pl.ds(1, half, stride=2), :] = spin(packed, 64)
    value = tmp[0:count, :]
    return jnp.where(lanes(value.shape) < 64, value, spin(value, 64))


def store_64(ref, lead, doubled):
    high, low = split(doubled)
    ref[(*lead, slice(None), slice(0, 128))] = high
    ref[(*lead, slice(None), slice(128, 192))] = low[:, 0:64]


def store_128(ref, lead, value):
    high, low = split(value)
    ref[(*lead, slice(None), slice(0, 128))] = high
    ref[(*lead, slice(None), slice(128, 256))] = high
    ref[(*lead, slice(None), slice(256, 384))] = low


def store_96(ref, lead, value):
    high = value.astype(bf16).astype(f32)
    low = value - high
    high_on, low_on = spin(high, 96), spin(low, 64)
    lane = lanes(value.shape)
    ref[(*lead, slice(None), slice(0, 128))] = jnp.where(lane < 96, high, high_on).astype(bf16)
    ref[(*lead, slice(None), slice(128, 256))] = jnp.where(lane < 64, high_on, low_on).astype(bf16)
    ref[(*lead, slice(None), slice(256, 288))] = low_on[:, 0:32].astype(bf16)


def prepare(par, st, wb_emb, tmp):
    for k in range(LAYERS):
        w = unpack(par[AT_ENV + 32 * k : AT_ENV + 32 * k + 32, :], 64, tmp)
        store_64(st.wb_env, (k,), w)
        store_64(st.wf_env, (k,), jnp.concatenate([w, w], 0).T[0:64])
        w = unpack(par[AT_INV + 48 * k : AT_INV + 48 * k + 48, :], 96, tmp)
        store_64(st.wb_inv, (k,), w)
        store_96(st.wf_inv, (k,), jnp.concatenate([w, jnp.zeros((32, 128), f32)], 0).T[0:64])
        w = par[AT_ONE + 64 * k : AT_ONE + 64 * k + 64, :]
        store_128(st.wb_one, (k,), w)
        store_64(st.wf_one, (k,), jnp.concatenate([w, w], 0).T)
        w = unpack(par[AT_TWO + 64 * k : AT_TWO + 64 * k + 64, :], 128, tmp)
        store_64(st.wb_two, (k,), w)
        store_128(st.wf_two, (k,), w.T[0:64])
    w = par[AT_HEAD : AT_HEAD + 64, :]
    store_128(st.wb_head, (), w)
    store_64(st.wf_head, (), jnp.concatenate([w, w], 0).T)
    w = unpack(par[0:9, :], 18, tmp)
    w = jnp.concatenate([w[0:16], jnp.where(rows_of((16, 128)) < 2, tmp_rows(w, 16), 0.0)], 0)
    store_64(wb_emb, (), w[0:16])
    high = w.astype(bf16).astype(f32)
    low = w - high
    turned = jnp.concatenate([high, high, low, jnp.zeros((32, 128), f32)], 0).T[0:64]
    st.wf_emb[...] = turned[:, 0 : 3 * FEAT].astype(bf16)
    st.whcol[...] = jnp.broadcast_to(par[AT_VEC : AT_VEC + 1, :], (128, 128)).T


def tmp_rows(w, start):
    return jnp.concatenate([w[start : start + 2], jnp.zeros((14, 128), f32)], 0)


def sine_parts(turns):
    whole = jnp.round(turns)
    rest = (turns - whole) * math.pi
    odd = whole - 2.0 * jnp.floor(whole * 0.5)
    sign = 1.0 - 2.0 * odd
    r2 = rest * rest
    sine = 0.0
    for n in (13, 11, 9, 7, 5, 3, 1):
        sine = sine * r2 + (-1.0) ** (n // 2) / math.factorial(n)
    cosine = 0.0
    for n in (14, 12, 10, 8, 6, 4, 2, 0):
        cosine = cosine * r2 + (-1.0) ** (n // 2) / math.factorial(n)
    return sign * rest * sine, sign * cosine


def first_kernel(ranks, axis, par, vec, own, loc, nsp, cen, live, tgt, pay, *refs):
    st = Refs(STATE, refs[: len(STATE)])
    wb_emb, payload, scatter = refs[len(STATE) : len(STATE) + 3]
    sc = Refs(SCRATCH_A, refs[len(STATE) + 3 :])
    me = lax.axis_index(axis)
    prepare(par, st, wb_emb, sc.tmp)

    code = ((own[...] * 32 + loc[...]) * 8 + nsp[...]).astype(f32)
    for q, value in enumerate((vec[0], vec[1], vec[2], code)):
        for a in range(4):
            sc.tmp[pl.ds(32 * q + a, 8, stride=4), :] = spin(value, -32 * a)
    turned = sc.tmp[...].T
    lane = lanes((8, 128))

    def picked(q):
        out = spin(turned[0:8], -32 * q)
        for g in range(1, 4):
            out = jnp.where(lane // 32 == g, spin(turned[8 * g : 8 * g + 8], 32 * (g - q)), out)
        return out

    xyz = [picked(q) for q in range(3)]
    codes = picked(3).astype(jnp.int32)
    for q in range(3):
        st.place[q] = xyz[q]
    local = lax.shift_right_logical(codes, 3) & 31
    owner = lax.shift_right_logical(codes, 8)
    kind = codes & 7
    st.owner[...] = owner
    sc.tmp[0:8, :] = jnp.zeros((8, 128), f32)
    sc.tmp[0:1, 0:32] = cen[...].astype(f32)
    centre_kind = group_sum(sc.tmp[0:8, :])[0:1].astype(jnp.int32)

    d, f, harmonics = geometry(*xyz)
    st.geo[0] = f
    for m in range(8):
        st.geo[m + 1] = harmonics[m]
    st.geo[9] = f * (1.0 / math.sqrt(NEI))
    geo = st.geo

    orders = (rows_of((8, 128)) + 1).astype(f32)
    inv_d = 1.0 / d
    scale = math.sqrt(2.0 / cutoff_radius)
    for t in range(TILES):
        row_inv = inv_d[t : t + 1]
        sine, cosine = sine_parts(orders * (d[t : t + 1] / cutoff_radius))
        b = (scale * sine) * row_inv
        slope = (scale * math.pi / cutoff_radius) * orders * cosine * row_inv - b * row_inv
        st.bes[0, :, tile(t)] = b
        st.bes[1, :, tile(t)] = slope
        row = rows_of((FEAT - 8, 128)) + 8
        hot = (row == centre_kind + 8) | (row == kind[t : t + 1] + 13)
        features = jnp.concatenate([b * f[t : t + 1], hot.astype(f32)], 0)
        put(st.phi, 0, tile(t), features)
        st.hot[:, tile(t)] = (rows_of((ATOMS, 128)) == local[t : t + 1]).astype(f32).astype(bf16)

    for c in range(CHUNKS):
        cs = chunk(c)
        s, s1, s2 = silu_parts(product(st.wf_emb[...], *pair(st.phi, cs)))
        st.z1[:, cs] = s1
        st.tz[:, cs] = s2
        sc.run[:, cs] = s
        put(st.latx, 0, cs, s, (0,))

    for k in range(LAYERS):
        for c in range(CHUNKS):
            cs = chunk(c)
            st.pq[k, :, cs] = product(st.wf_env[k], *pair(st.latx, cs, (k,)))
        for r in range(0, 32, 16):
            rs = slice(r, r + 16)
            sums = None
            for t in range(TILES):
                a = st.pq[k, rs, tile(t)] * geo[9, t : t + 1, :]
                terms = [a] + [a * geo[m, t : t + 1, :] for m in range(1, 9)]
                sums = terms if sums is None else [x + y for x, y in zip(sums, terms, strict=True)]
            for m in range(9):
                st.env[k, m, rs, :] = group_sum(sums[m])
        for r in range(0, 32, 8):
            rs = slice(r, r + 8)
            envs = [[st.env[j, m, rs, :] for m in range(9)] for j in range(k + 1)]
            base, factors = atom_terms(envs)
            for l in range(3):
                st.bb[k, l, rs, :] = base[l]
            for m in range(8):
                st.eh[k, m, rs, :] = factors[m]
        for r in range(0, 32, 16):
            rs = slice(r, r + 16)
            for t in range(TILES):
                ts = tile(t)
                q = st.pq[k, 32 + r : 48 + r, ts]
                if k > 0:
                    q = mix * st.qq[k - 1, rs, ts] * q
                st.qq[k, rs, ts] = q
                values = [st.bb[k, l, rs, :] for l in range(3)]
                for m in range(1, 9):
                    l = degree(m)
                    values[l] = values[l] + geo[m, t : t + 1, :] * st.eh[k, m - 1, rs, :]
                st.vv[k, rs, ts] = values[1]
                st.vv[k, 32 + r : 48 + r, ts] = values[2]
                for l in range(3):
                    put(st.ivx, 32 * l + r, ts, q * values[l], (k,))
        for c in range(CHUNKS):
            cs = chunk(c)
            inner = sc.run[:, cs] + product(st.wf_inv[k], *pair(st.ivx, cs, (k,)))
            h = product(st.wf_one[k], *put(st.inx, 0, cs, inner, (k,)))
            s, s1, s2 = silu_parts(h)
            st.s1[k, :, cs] = s1
            st.t2[k, :, cs] = s2
            o = product(st.wf_two[k], *put(st.sx, 0, cs, s, (k,)))
            st.oo[k, :, cs] = o
            latent = sc.run[:, cs] + wide(geo, 0, c) * o
            sc.run[:, cs] = latent
            put(st.latx, 0, cs, latent, (k + 1,))

    per = CH // 128
    for c in range(CHUNKS):
        cs = chunk(c)
        s, s1, s2 = silu_parts(product(st.wf_head[...], *pair(st.latx, cs, (3,))))
        st.sh[:, cs] = s
        st.h1[:, cs] = s1
        st.h2[:, cs] = s2
        whcol = jnp.concatenate([st.whcol[...]] * per, 1)
        energy = whcol * s
        for j in range(per):
            sc.ybar[0, per * c + j] = fold(energy[:, 128 * j : 128 * j + 128])
        back = put(st.hhb, 0, cs, wide(geo, 0, c) * whcol * s1)
        st.lb[2, :, cs] = product(st.wb_head[...], *back)

    for k in reversed(range(LAYERS)):
        for c in range(CHUNKS):
            cs = chunk(c)
            lb = st.lb[k, :, cs]
            share = st.oo[k, :, cs] * lb
            for j in range(per):
                sc.ybar[0, per * c + j] += fold(share[:, 128 * j : 128 * j + 128])
            sb = product(st.wb_two[k], *put(st.ob, 0, cs, wide(geo, 0, c) * lb, (k,)))
            st.t2[k, :, cs] = st.t2[k, :, cs] * sb
            ib = product(st.wb_one[k], *put(st.hb, 0, cs, st.s1[k, :, cs] * sb, (k,)))
            st.vb[k, :, cs] = product(st.wb_inv[k], *put(st.ib, 0, cs, ib, (k,)))
            sc.run[:, cs] = lb + ib
        for r in range(0, 32, 16):
            rs = slice(r, r + 16)
            sums = None
            for t in range(TILES):
                ts = tile(t)
                q = st.qq[k, rs, ts]
                vb = [st.vb[k, 32 * l + r : 32 * l + r + 16, ts] for l in range(3)]
                qb = (
                    vb[0] * st.bb[k, 0, rs, :]
                    + vb[1] * st.vv[k, rs, ts]
                    + vb[2] * st.vv[k, 32 + r : 48 + r, ts]
                )
                if k < LAYERS - 1:
                    qb = qb + mix * st.pq[k + 1, 32 + r : 48 + r, ts] * st.qb[k + 1, rs, ts]
                st.qb[k, rs, ts] = qb
                back = [x * q for x in vb]
                terms = list(back)
                for m in range(1, 9):
                    terms.append(back[degree(m)] * geo[m, t : t + 1, :])
                    share = fold(back[degree(m)] * st.eh[k, m - 1, rs, :])
                    if k == LAYERS - 1 and r == 0:
                        sc.ybar[m, t] = share
                    else:
                        sc.ybar[m, t] += share
                sums = terms if sums is None else [x + y for x, y in zip(sums, terms, strict=True)]
            for n in range(11):
                st.cot[k, n, rs, :] = group_sum(sums[n])
        for r in range(0, 32, 8):
            rs = slice(r, r + 8)
            envs = [[st.env[j, m, rs, :] for m in range(9)] for j in range(k + 1)]
            cots = [st.cot[k, n, rs, :] for n in range(11)]
            back = atom_back(envs, (cots[:3], cots[3:]))
            for j in range(k + 1):
                for m in range(9):
                    if k == LAYERS - 1:
                        st.eb[j, m, rs, :] = back[j][m]
                    else:
                        st.eb[j, m, rs, :] += back[j][m]
        for r in range(0, 32, 16):
            rs = slice(r, r + 16)
            for t in range(TILES):
                ts = tile(t)
                p = st.pq[k, rs, ts]
                fs = geo[9, t : t + 1, :]
                a = p * fs
                ab = st.eb[k, 0, rs, :]
                for m in range(1, 9):
                    e = st.eb[k, m, rs, :]
                    ab = ab + geo[m, t : t + 1, :] * e
                    sc.ybar[m, t] += fold(a * e)
                st.ab[k, rs, ts] = ab
                sc.ybar[0, t] += fold((1.0 / math.sqrt(NEI)) * ab * p)
                put(st.pb, r, ts, ab * fs, (k,))
                qb = st.qb[k, rs, ts]
                if k > 0:
                    qb = mix * st.qq[k - 1, rs, ts] * qb
                put(st.pb, 32 + r, ts, qb, (k,))
        for c in range(CHUNKS):
            cs = chunk(c)
            lb = sc.run[:, cs] + product(st.wb_env[k], *pair(st.pb, cs, (k,)))
            if k > 0:
                st.lb[k - 1, :, cs] = lb
                continue
            st.tz[:, cs] = st.tz[:, cs] * lb
            pb = product(wb_emb[...], *put(st.zb, 0, cs, st.z1[:, cs] * lb))[0:8]
            for j in range(per):
                t = per * c + j
                part = pb[:, 128 * j : 128 * j + 128]
                sc.ybar[0, t] += st.bes[0, :, tile(t)] * part
                sc.dbar[t] = geo[0, t : t + 1, :] * st.bes[1, :, tile(t)] * part

    bars = [jnp.sum(sc.ybar[m], axis=1) for m in range(9)]
    slopes = jax.vjp(geometry, *xyz)[1]((jnp.sum(sc.dbar[...], axis=1), bars[0], bars[1:]))

    for t in range(TILES):
        mine = rows_of((ranks, 128)) == owner[t : t + 1]
        parts = jnp.concatenate([jnp.where(mine, s[t : t + 1], 0.0) for s in slopes], 0)
        high = parts.astype(bf16).astype(f32)
        scatter[:, tile(t)] = jnp.concatenate([high, parts - high], 0).astype(bf16)
    sums = lax.dot_general(
        scatter[...], st.hot[...], (((1,), (1,)), ((), ())), preferred_element_type=f32
    )
    payload[...] = jnp.zeros(payload.shape, f32)
    for q in range(3):
        at = ranks * q
        total = jnp.broadcast_to(jnp.sum(slopes[q], axis=0, keepdims=True), (8, 128))
        total = group_sum(total)[0:1, 0:32]
        part = -(sums[at : at + ranks] + sums[3 * ranks + at : 4 * ranks + at])
        payload[at : at + ranks, 0:32] = part + jnp.where(
            rows_of((ranks, 32)) == me, total, 0.0
        )
    payload[3 * ranks : 3 * ranks + 3, 0:32] = tgt[...]
    payload[3 * ranks + 3 : 3 * ranks + 4, 0:32] = (lanes((1, 32)) < live[0, 0]).astype(f32)

    def spread(j, carry):
        pay[j] = payload[...]
        return carry

    lax.fori_loop(0, ranks, spread, 0)


def outer(*pairs):
    full = None
    for x, y in pairs:
        part = lax.dot_general(x, y, (((1,), (1,)), ((), ())), preferred_element_type=f32)
        full = part if full is None else full + part
    rows, columns = full.shape[0] // 2, full.shape[1] // 2
    if columns == 64:
        return full[:rows] + (spin(full[:rows], 64) + full[rows:])
    return full[:rows, :columns] + (full[:rows, columns:] + full[rows:, :columns])


def pack(value, tmp):
    count = value.shape[0]
    tmp[0:count, :] = value
    even, odd = tmp[pl.ds(0, count // 2, stride=2), :], tmp[pl.ds(1, count // 2, stride=2), :]
    return jnp.where(lanes(even.shape) < 64, even, spin(odd, 64))


def second_kernel(ranks, axis, pick, live, got, *refs):
    st = Refs(STATE, refs[: len(STATE)])
    keep, give, forces, tm, aim = refs[len(STATE) : len(STATE) + 5]
    sc = Refs(SCRATCH_B, refs[len(STATE) + 5 :])
    me = lax.axis_index(axis)
    geo, gd = st.geo, sc.gd

    total = got[0, 0 : 3 * ranks, :]
    for j in range(1, ranks):
        total = total + got[j, 0 : 3 * ranks, :]
    for j in range(ranks):
        for q in range(4):
            tm[q * ranks + j : q * ranks + j + 1, :] = got[j, 3 * ranks + q : 3 * ranks + q + 1, :]
    mask = tm[3 * ranks : 4 * ranks, :]
    mine = rows_of((ranks, 128)) == me
    loss = jnp.zeros((ranks, 128), f32)
    centre = []
    for q in range(3):
        at = slice(q * ranks, q * ranks + ranks)
        error = mask * (total[at] - tm[at, :])
        loss = loss + jnp.where(mine, error * error, 0.0)
        forces[q : q + 1, :] = jnp.sum(jnp.where(mine, total[at], 0.0), axis=0, keepdims=True)[:, 0:32]
        error = 2.0 * error
        aim[at, :] = error
        own = jnp.sum(jnp.where(mine, error, 0.0), axis=0, keepdims=True)
        centre.append(group_sum(jnp.broadcast_to(own, (8, 128)))[0:1])
    aims = aim[...]
    high = aims.astype(bf16).astype(f32)
    stacked = jnp.concatenate([high, aims - high], 0).astype(bf16)[:, 0:32]
    seen = jnp.dot(stacked, st.hot[...], preferred_element_type=f32)
    seen = seen[0 : 3 * ranks] + seen[3 * ranks :]
    for t in range(TILES):
        at_owner = rows_of((ranks, 128)) == st.owner[t : t + 1, :]
        for q in range(3):
            there = jnp.where(at_owner, seen[q * ranks : q * ranks + ranks, tile(t)], 0.0)
            sc.cdir[q, t : t + 1, :] = centre[q] - jnp.sum(there, axis=0, keepdims=True)

    xyz = tuple(st.place[q] for q in range(3))
    ways = tuple(sc.cdir[q] for q in range(3))
    _, (dd, fd, yd) = jax.jvp(geometry, xyz, ways)
    gd[0] = fd
    for m in range(8):
        gd[m + 1] = yd[m]
    gd[9] = fd * (1.0 / math.sqrt(NEI))
    for t in range(TILES):
        b, slope = st.bes[0, :, tile(t)], st.bes[1, :, tile(t)]
        row = fd[t : t + 1] * b + (geo[0, t : t + 1, :] * dd[t : t + 1]) * slope
        put(sc.phid, 0, tile(t), jnp.concatenate([row, jnp.zeros((FEAT - 8, 128), f32)], 0))

    for c in range(CHUNKS):
        cs = chunk(c)
        zd = product(st.wf_emb[...], *pair(sc.phid, cs))
        sc.zd[:, cs] = zd
        ld = st.z1[:, cs] * zd
        sc.run[:, cs] = ld
        put(sc.latd, 0, cs, ld, (0,))

    for k in range(LAYERS):
        for c in range(CHUNKS):
            cs = chunk(c)
            sc.pqd[k, :, cs] = product(st.wf_env[k], *pair(sc.latd, cs, (k,)))
        for r in range(0, 32, 16):
            rs = slice(r, r + 16)
            sums = None
            for t in range(TILES):
                ts = tile(t)
                p = st.pq[k, rs, ts]
                a = p * geo[9, t : t + 1, :]
                ad = sc.pqd[k, rs, ts] * geo[9, t : t + 1, :] + p * gd[9, t : t + 1, :]
                terms = [ad] + [
                    ad * geo[m, t : t + 1, :] + a * gd[m, t : t + 1, :] for m in range(1, 9)
                ]
                sums = terms if sums is None else [x + y for x, y in zip(sums, terms, strict=True)]
            for m in range(9):
                sc.envd[k, m, rs, :] = group_sum(sums[m])
        for r in range(0, 32, 8):
            rs = slice(r, r + 8)
            envs = [[st.env[j, m, rs, :] for m in range(9)] for j in range(k + 1)]
            envds = [[sc.envd[j, m, rs, :] for m in range(9)] for j in range(k + 1)]
            _, (base, factors) = jax.jvp(atom_terms, (envs,), (envds,))
            for l in range(3):
                sc.bd[k, l, rs, :] = base[l]
            for m in range(8):
                sc.ehd[k, m, rs, :] = factors[m]
        for r in range(0, 32, 16):
            rs = slice(r, r + 16)
            ru = slice(32 + r, 48 + r)
            for t in range(TILES):
                ts = tile(t)
                qd = sc.pqd[k, ru, ts]
                if k > 0:
                    qd = mix * (
                        sc.qd[k - 1, rs, ts] * st.pq[k, ru, ts] + st.qq[k - 1, rs, ts] * qd
                    )
                sc.qd[k, rs, ts] = qd
                q = st.qq[k, rs, ts]
                values = [st.bb[k, 0, rs, :], st.vv[k, rs, ts], st.vv[k, ru, ts]]
                moves = [sc.bd[k, l, rs, :] for l in range(3)]
                for m in range(1, 9):
                    l = degree(m)
                    moves[l] = (
                        moves[l]
                        + geo[m, t : t + 1, :] * sc.ehd[k, m - 1, rs, :]
                        + gd[m, t : t + 1, :] * st.eh[k, m - 1, rs, :]
                    )
                sc.vvd[k, rs, ts] = moves[1]
                sc.vvd[k, ru, ts] = moves[2]
                for l in range(3):
                    put(sc.ivd, 32 * l + r, ts, qd * values[l] + q * moves[l], (k,))
        for c in range(CHUNKS):
            cs = chunk(c)
            ind = sc.run[:, cs] + product(st.wf_inv[k], *pair(sc.ivd, cs, (k,)))
            hd = product(st.wf_one[k], *put(sc.ind, 0, cs, ind, (k,)))
            sc.hd[k, :, cs] = hd
            od = product(st.wf_two[k], *put(sc.sd, 0, cs, st.s1[k, :, cs] * hd, (k,)))
            ld = sc.run[:, cs] + wide(gd, 0, c) * st.oo[k, :, cs] + wide(geo, 0, c) * od
            sc.run[:, cs] = ld
            put(sc.latd, 0, cs, ld, (k + 1,))

    per = CH // 128
    vector = jnp.zeros((128, 128), f32)
    for c in range(CHUNKS):
        cs = chunk(c)
        hhd = product(st.wf_head[...], *pair(sc.latd, cs, (3,)))
        fw, fdw = wide(geo, 0, c), wide(gd, 0, c)
        h1 = st.h1[:, cs]
        whcol = jnp.concatenate([st.whcol[...]] * per, 1)
        part = fw * h1 * hhd + fdw * st.sh[:, cs]
        for j in range(per):
            vector = vector + part[:, 128 * j : 128 * j + 128]
        back = put(sc.hht, 0, cs, whcol * (fdw * h1 + fw * st.h2[:, cs] * hhd))
        sc.run[:, cs] = product(st.wb_head[...], *back)
    sc.grad[AT_HEAD : AT_HEAD + 64, :] = outer((sc.latd[3], st.hhb[...]), (st.latx[3], sc.hht[...]))
    sc.grad[AT_VEC : AT_VEC + 1, :] = jnp.sum(vector.T, axis=0, keepdims=True)

    for k in reversed(range(LAYERS)):
        for c in range(CHUNKS):
            cs = chunk(c)
            lt = sc.run[:, cs]
            ot = wide(gd, 0, c) * st.lb[k, :, cs] + wide(geo, 0, c) * lt
            tt = product(st.wb_two[k], *put(sc.ot, 0, cs, ot))
            ht = tt * st.s1[k, :, cs] + st.t2[k, :, cs] * sc.hd[k, :, cs]
            it = product(st.wb_one[k], *put(sc.ht, 0, cs, ht))
            sc.vt[:, cs] = product(st.wb_inv[k], *put(sc.it, 0, cs, it))
            sc.run[:, cs] = lt + it
        for r in range(0, 32, 16):
            rs = slice(r, r + 16)
            ru = slice(32 + r, 48 + r)
            sums = None
            for t in range(TILES):
                ts = tile(t)
                q, qd = st.qq[k, rs, ts], sc.qd[k, rs, ts]
                ls = [slice(32 * l + r, 32 * l + r + 16) for l in range(3)]
                vb = [st.vb[k, s, ts] for s in ls]
                vt = [sc.vt[s, ts] for s in ls]
                qt = (
                    vt[0] * st.bb[k, 0, rs, :]
                    + vt[1] * st.vv[k, rs, ts]
                    + vt[2] * st.vv[k, ru, ts]
                    + vb[0] * sc.bd[k, 0, rs, :]
                    + vb[1] * sc.vvd[k, rs, ts]
                    + vb[2] * sc.vvd[k, ru, ts]
                )
                if k < LAYERS - 1:
                    qt = qt + mix * (
                        sc.pqd[k + 1, ru, ts] * st.qb[k + 1, rs, ts]
                        + st.pq[k + 1, ru, ts] * sc.qt[k + 1, rs, ts]
                    )
                sc.qt[k, rs, ts] = qt
                back = [x * q for x in vb]
                turn = [x * q + y * qd for x, y in zip(vt, vb, strict=True)]
                terms = list(turn)
                for m in range(1, 9):
                    l = degree(m)
                    terms.append(turn[l] * geo[m, t : t + 1, :] + back[l] * gd[m, t : t + 1, :])
                sums = terms if sums is None else [x + y for x, y in zip(sums, terms, strict=True)]
            for n in range(11):
                sc.cott[n, rs, :] = group_sum(sums[n])
        for r in range(0, 32, 8):
            rs = slice(r, r + 8)
            envs = [[st.env[j, m, rs, :] for m in range(9)] for j in range(k + 1)]
            envds = [[sc.envd[j, m, rs, :] for m in range(9)] for j in range(k + 1)]
            cots = [st.cot[k, n, rs, :] for n in range(11)]
            cotts = [sc.cott[n, rs, :] for n in range(11)]
            _, back = jax.jvp(
                atom_back,
                (envs, (cots[:3], cots[3:])),
                (envds, (cotts[:3], cotts[3:])),
            )
            for j in range(k + 1):
                for m in range(9):
                    if k == LAYERS - 1:
                        sc.et[j, m, rs, :] = back[j][m]
                    else:
                        sc.et[j, m, rs, :] += back[j][m]
        for r in range(0, 32, 16):
            rs = slice(r, r + 16)
            for t in range(TILES):
                ts = tile(t)
                at = sc.et[k, 0, rs, :]
                for m in range(1, 9):
                    at = (
                        at
                        + geo[m, t : t + 1, :] * sc.et[k, m, rs, :]
                        + gd[m, t : t + 1, :] * st.eb[k, m, rs, :]
                    )
                pt = at * geo[9, t : t + 1, :] + st.ab[k, rs, ts] * gd[9, t : t + 1, :]
                put(sc.pt, r, ts, pt)
                qt = sc.qt[k, rs, ts]
                if k > 0:
                    qt = mix * (sc.qd[k - 1, rs, ts] * st.qb[k, rs, ts] + st.qq[k - 1, rs, ts] * qt)
                put(sc.pt, 32 + r, ts, qt)
        for c in range(CHUNKS):
            cs = chunk(c)
            lt = sc.run[:, cs] + product(st.wb_env[k], *pair(sc.pt, cs))
            sc.run[:, cs] = lt
            if k == 0:
                put(sc.zt, 0, cs, lt * st.z1[:, cs] + st.tz[:, cs] * sc.zd[:, cs])
        at = AT_TWO + 64 * k
        sc.grad[at : at + 64, :] = pack(outer((sc.sd[k], st.ob[k]), (st.sx[k], sc.ot[...])), sc.tmp)
        at = AT_ONE + 64 * k
        sc.grad[at : at + 64, :] = outer((sc.ind[k], st.hb[k]), (st.inx[k], sc.ht[...]))
        at = AT_INV + 48 * k
        sc.grad[at : at + 48, :] = pack(outer((sc.ivd[k], st.ib[k]), (st.ivx[k], sc.it[...])), sc.tmp)
        at = AT_ENV + 32 * k
        sc.grad[at : at + 32, :] = pack(outer((sc.latd[k], st.pb[k]), (st.latx[k], sc.pt[...])), sc.tmp)
    packed = pack(outer((sc.phid[...], st.zb[...]), (st.phi[...], sc.zt[...])), sc.tmp)
    sc.grad[0:9, :] = packed[0:9]
    sc.grad[ROWS:PADDED, :] = jnp.zeros((PADDED - ROWS, 128), f32)
    lane = lanes((1, 128))
    amount = 3.0 * live[0, 0].astype(f32)
    sc.grad[ROWS : ROWS + 1, :] = jnp.where(
        lane == 0, jnp.sum(loss), jnp.where(lane == 1, amount, 0.0)
    )
    half = lax.axis_index(pick)
    keep[...] = sc.grad[pl.ds(pl.multiple_of(half * HALF, HALF), HALF), :]
    give[...] = sc.grad[pl.ds(pl.multiple_of((1 - half) * HALF, HALF), HALF), :]


def third_kernel(pick, mine, other, par, first, second, avg, *outs):
    loss, count, norm, new_first, new_second, new_par, low, new_avg = outs
    half = lax.axis_index(pick)
    lower = jnp.where(half == 0, mine[...], other[...])
    upper = jnp.where(half == 0, other[...], mine[...])
    last = ROWS - HALF
    scalars = upper[last : last + 1]
    loss[...] = scalars[:, 0:1]
    amount = scalars[:, 1:2]
    count[...] = amount
    squares = jnp.sum(lower * lower, keepdims=True) + jnp.sum(
        upper[0:last] * upper[0:last], keepdims=True
    )
    length = jnp.sqrt(squares) / amount
    norm[...] = length
    factor = (clip_level / jnp.maximum(length, clip_level)) / amount
    for start, stop, value in ((0, HALF, lower), (HALF, ROWS, upper[0:last])):
        rows = slice(start, stop)
        gradient = value * factor
        one = beta_one * first[rows, :] + (1.0 - beta_one) * gradient
        two = beta_two * second[rows, :] + (1.0 - beta_two) * gradient * gradient
        fixed_one = one / (1.0 - beta_one**STEP)
        fixed_two = two / (1.0 - beta_two**STEP)
        weights = par[rows, :]
        weights = weights - learn_rate * (
            fixed_one / (jnp.sqrt(fixed_two) + epsilon_adam) + decay_rate * weights
        )
        new_first[rows, :] = one
        new_second[rows, :] = two
        new_par[rows, :] = weights
        low[rows, :] = weights.astype(bf16)
        new_avg[rows, :] = average_keep * avg[rows, :] + (1.0 - average_keep) * weights


VMEM = pl.BlockSpec(memory_space=pltpu.VMEM)
SMEM = pl.BlockSpec(memory_space=pltpu.SMEM)


def scratch(entries):
    return [pltpu.VMEM(shape, dtype) for _, shape, dtype in entries]


def local(
    ranks,
    wide_axes,
    params,
    first_moment,
    second_moment,
    average,
    edge_vectors,
    owner_rank,
    neighbour_local,
    centre_species,
    neighbour_species,
    live_atoms,
    target_forces,
):
    shape = jax.ShapeDtypeStruct
    flat = (ROWS, 128)
    par = params.reshape(flat)
    live = live_atoms.reshape(1, 1)
    tall = 3 * ranks + 8
    parts = len(wide_axes[1])
    state = [shape(s, t) for _, s, t in STATE]
    pay, *kept = pl.pallas_call(
        functools.partial(first_kernel, ranks, "atoms"),
        out_shape=[shape((ranks, tall, 128), f32), *state],
        in_specs=[VMEM] * 6 + [SMEM, VMEM],
        out_specs=[VMEM] * (1 + len(state)),
        scratch_shapes=[
            pltpu.VMEM((16, 192), bf16),
            pltpu.VMEM((tall, 128), f32),
            pltpu.VMEM((6 * ranks, EDGES), bf16),
            *scratch(SCRATCH_A),
        ],
        compiler_params=pltpu.CompilerParams(vmem_limit_bytes=16 * 2**20),
        name="forward",
    )(
        par,
        edge_vectors.reshape(3, 8, 128),
        owner_rank.reshape(8, 128),
        neighbour_local.reshape(8, 128),
        neighbour_species.reshape(8, 128),
        centre_species.reshape(1, ATOMS),
        live,
        target_forces.reshape(3, ATOMS),
    )
    got = lax.all_to_all(pay, "atoms", split_axis=0, concat_axis=0, tiled=True)
    keep, give, forces = pl.pallas_call(
        functools.partial(second_kernel, ranks, "atoms", "low"),
        out_shape=[shape((HALF, 128), f32), shape((HALF, 128), f32), shape((3, ATOMS), f32)],
        in_specs=[SMEM, VMEM] + [VMEM] * len(state),
        out_specs=[VMEM] * 3,
        scratch_shapes=[
            pltpu.VMEM((4 * ranks, 128), f32),
            pltpu.VMEM((3 * ranks, 128), f32),
            *scratch(SCRATCH_B),
        ],
        compiler_params=pltpu.CompilerParams(vmem_limit_bytes=20 * 2**20),
        name="gradient",
    )(live, got, *kept)
    swap = [(0, 1), (1, 0)]
    axes, size = ("atoms", "high"), ranks * 2
    held = keep + lax.ppermute(give, "low", swap)
    pieces = size * 8 * -(-HALF // (8 * size))
    held = jnp.pad(held, ((0, pieces - HALF), (0, 0))).reshape(size, pieces // size, 128)
    summed = lax.all_to_all(held, axes, split_axis=0, concat_axis=0, tiled=True).sum(0)
    summed = jnp.broadcast_to(summed[None], (size, *summed.shape))
    mine = lax.all_to_all(summed, axes, split_axis=0, concat_axis=0, tiled=True)
    mine = mine.reshape(pieces, 128)[:HALF]
    other = lax.ppermute(mine, "low", swap)
    one, vec = shape((1, 1), f32), shape(flat, f32)
    loss, count, norm, new_first, new_second, new_params, low, new_average = pl.pallas_call(
        functools.partial(third_kernel, "low"),
        out_shape=[one, one, one, vec, vec, vec, shape(flat, bf16), vec],
        in_specs=[VMEM] * 6,
        out_specs=[VMEM] * 8,
        compiler_params=pltpu.CompilerParams(vmem_limit_bytes=16 * 2**20),
        name="update",
    )(
        mine,
        other,
        par,
        first_moment.reshape(flat),
        second_moment.reshape(flat),
        average.reshape(flat),
    )
    return (
        loss.reshape(()),
        count.reshape(()),
        norm.reshape(()),
        forces.reshape(3, 1, ATOMS),
        new_first.reshape(-1),
        new_second.reshape(-1),
        new_params.reshape(-1),
        low.reshape(-1),
        new_average.reshape(-1),
    )


def solution(mesh):
    ranks, groups = mesh.shape["atoms"], mesh.shape["grp"]
    fine = Mesh(mesh.devices.reshape(ranks, groups // 2, 2), ("atoms", "high", "low"))
    grp = ("high", "low")
    in_specs = (
        P(),
        P(),
        P(),
        P(),
        P(None, grp, "atoms"),
        P(grp, "atoms", None),
        P(grp, "atoms"),
        P(grp, "atoms"),
        P(grp, "atoms"),
        P(grp, "atoms"),
        P(None, grp, "atoms"),
    )
    out_specs = (P(), P(), P(), P(None, grp, "atoms"), P(), P(), P(), P(), P())
    return jax.shard_map(
        functools.partial(local, ranks, (("atoms", "high"), grp)),
        mesh=fine,
        in_specs=in_specs,
        out_specs=out_specs,
        check_vma=False,
    )
```

```python
import functools
import math

import jax
import jax.numpy as jnp
from jax import lax
from jax.experimental import pallas as pl
from jax.experimental.pallas import tpu as pltpu
from jax.sharding import Mesh
from jax.sharding import PartitionSpec as P

LATENT = 64
UNITS = 128
CHANNELS = 32
BASES = 8
SPECIES = 5
LAYERS = 3
STEP = 10
NEI = 32
NPARAM = 89344

cutoff_radius = 5.0
clip_level = 0.01
learn_rate = 0.1
beta_one = 0.9
beta_two = 0.999
epsilon_adam = 1e-08
decay_rate = 0.01
average_keep = 0.99
mix = 0.7071

f32 = jnp.float32
bf16 = jnp.bfloat16

ATOMS = 32
EDGES = 1024
TILES = 8
FEAT = 32

AT_EMBED = 0
AT_ENV = 9
AT_INV = AT_ENV + 96
AT_ONE = AT_INV + 144
AT_TWO = AT_ONE + 192
AT_HEAD = AT_TWO + 192
AT_VEC = AT_HEAD + 64
ROWS = AT_VEC + 1
PADDED = 768
HALF = PADDED // 2

STATE = [
    ("wf_emb", (LATENT, 3 * FEAT), bf16),
    ("wf_env", (3, 64, 192), bf16),
    ("wb_env", (3, 64, 192), bf16),
    ("wf_inv", (3, 64, 288), bf16),
    ("wf_one", (3, 128, 192), bf16),
    ("wb_one", (3, 64, 384), bf16),
    ("wf_io", (3, 128, 288), bf16),
    ("wb_io", (3, 96, 384), bf16),
    ("wf_two", (3, 64, 384), bf16),
    ("wb_two", (3, 128, 192), bf16),
    ("wf_te", (2, 64, 384), bf16),
    ("wb_te", (2, 128, 192), bf16),
    ("wf_th", (128, 384), bf16),
    ("wb_th", (128, 384), bf16),
    ("wf_head", (128, 192), bf16),
    ("wb_head", (64, 384), bf16),
    ("whcol", (128, 128), f32),
    ("place", (3, 8, 128), f32),
    ("owner", (8, 128), jnp.int32),
    ("hot", (ATOMS, EDGES), bf16),
    ("geo", (10, 8, 128), f32),
    ("bes", (2, BASES, EDGES), f32),
    ("phi", (2 * FEAT, EDGES), bf16),
    ("latx", (4, 128, EDGES), bf16),
    ("pq", (3, 64, EDGES), f32),
    ("vv", (3, 64, EDGES), f32),
    ("ivx", (3, 192, EDGES), bf16),
    ("sx", (3, 256, EDGES), bf16),
    ("s1", (3, 128, EDGES), f32),
    ("t2", (3, 128, EDGES), f32),
    ("oo", (3, 64, EDGES), f32),
    ("ts", (2, 64, EDGES), f32),
    ("th", (128, EDGES), f32),
    ("lb", (3, 64, EDGES), f32),
    ("ob", (3, 128, EDGES), bf16),
    ("hb", (3, 256, EDGES), bf16),
    ("xb", (3, 128, EDGES), f32),
    ("vb", (3, 96, EDGES), f32),
    ("ab", (3, 32, EDGES), f32),
    ("pb", (3, 128, EDGES), bf16),
    ("qq", (3, 32, EDGES), f32),
    ("qb", (3, 32, EDGES), f32),
    ("z1", (64, EDGES), f32),
    ("tz", (64, EDGES), f32),
    ("zb", (128, EDGES), bf16),
    ("sh", (128, EDGES), f32),
    ("h1", (128, EDGES), f32),
    ("h2", (128, EDGES), f32),
    ("hhb", (256, EDGES), bf16),
    ("env", (3, 9, 32, 128), f32),
    ("eh", (3, 8, 32, 128), f32),
    ("bb", (3, 3, 32, 128), f32),
    ("eb", (3, 9, 32, 128), f32),
    ("cot", (3, 11, 32, 128), f32),
]

SCRATCH_A = [
    ("tmp", (11, 128, 128), f32),
    ("wb_emb", (16, 192), bf16),
    ("ybar", (9, 8, 8, 128), f32),
    ("dbar", (8, 8, 128), f32),
]

SCRATCH_B = [
    ("tmp", (8, 128, 128), f32),
    ("part", (320, 256), f32),
    ("cdir", (3, 8, 128), f32),
    ("gd", (10, 8, 128), f32),
    ("phid", (2 * FEAT, EDGES), bf16),
    ("zd", (64, EDGES), f32),
    ("latd", (4, 128, EDGES), bf16),
    ("pqd", (3, 64, EDGES), f32),
    ("vvd", (3, 64, EDGES), f32),
    ("qd", (3, 32, EDGES), f32),
    ("ivd", (3, 192, EDGES), bf16),
    ("hd", (3, 128, EDGES), f32),
    ("sd", (3, 256, EDGES), bf16),
    ("envd", (3, 9, 32, 128), f32),
    ("ehd", (3, 8, 32, 128), f32),
    ("bd", (3, 3, 32, 128), f32),
    ("hht", (256, EDGES), bf16),
    ("ot", (3, 128, EDGES), bf16),
    ("ht", (3, 256, EDGES), bf16),
    ("qt", (3, 32, EDGES), f32),
    ("pt", (3, 128, EDGES), bf16),
    ("zt", (128, EDGES), bf16),
    ("et", (3, 9, 32, 128), f32),
    ("cott", (11, 32, 128), f32),
    ("grad", (PADDED, 128), f32),
]


class Refs:
    def __init__(self, entries, refs):
        for (name, _, _), ref in zip(entries, refs, strict=True):
            setattr(self, name, ref)


def split(x):
    high = x.astype(bf16)
    return high, (x - high.astype(f32)).astype(bf16)


def product(weights, high, low):
    return jnp.dot(
        weights, jnp.concatenate([high, low, high], 0), preferred_element_type=f32
    )


def put(ref, rows, columns, value, lead=()):
    high, low = split(value)
    half = ref.shape[-2] // 2
    ref[(*lead, slice(rows, rows + value.shape[0]), columns)] = high
    ref[(*lead, slice(half + rows, half + rows + value.shape[0]), columns)] = low
    return high, low


def pair(ref, columns, lead=()):
    half = ref.shape[-2] // 2
    return ref[(*lead, slice(0, half), columns)], ref[(*lead, slice(half, 2 * half), columns)]


def spin(x, amount):
    return pltpu.roll(x, amount % 128, 1)


def group_sum(x):
    x = x + spin(x, 64)
    return x + spin(x, 32)


def lanes(shape):
    return lax.broadcasted_iota(jnp.int32, shape, len(shape) - 1)


def rows_of(shape):
    return lax.broadcasted_iota(jnp.int32, shape, len(shape) - 2)


def silu_parts(h):
    gate = 1.0 / (1.0 + jnp.exp(-h))
    slope = gate * (1.0 - gate)
    return h * gate, gate + h * slope, slope * (2.0 + h * (1.0 - 2.0 * gate))


def geometry(x, y, z):
    d = jnp.sqrt(x * x + y * y + z * z)
    u, v, w = x / d, y / d, z / d
    s = d / cutoff_radius
    s2 = s * s
    s6 = s2 * s2 * s2
    f = 1.0 - 28.0 * s6 + 48.0 * (s6 * s) - 21.0 * (s6 * s2)
    r3, r5, r15 = math.sqrt(3.0), math.sqrt(5.0), math.sqrt(15.0)
    harmonics = [
        r3 * u,
        r3 * v,
        r3 * w,
        r15 * u * v,
        r15 * v * w,
        0.5 * r5 * (3.0 * w * w - 1.0),
        r15 * u * w,
        0.5 * r15 * (u * u - v * v),
    ]
    return d, f, harmonics


def dots(left, right):
    total = left[0] * right[0]
    for a, b in zip(left[1:], right[1:], strict=True):
        total = total + a * b
    return total


def degree(m):
    return 1 if m <= 3 else 2


def atom_terms(envs):
    if len(envs) == 1:
        (one,) = envs
        zero = jnp.zeros_like(one[0])
        return [one[0], zero, zero], one[1:]
    if len(envs) == 2:
        one, two = envs
        return (
            [2.0 * one[0] * two[0], dots(one[1:4], two[1:4]), dots(one[4:], two[4:])],
            [one[0] * two[m] for m in range(1, 9)],
        )
    one, two, three = envs
    both = one[0] * two[0]
    twice = 2.0 * one[0]
    part = [two[0] * one[m] + twice * two[m] for m in range(1, 9)]
    return (
        [4.0 * both * three[0], dots(part[:3], three[1:4]), dots(part[3:], three[4:])],
        [both * three[m] for m in range(1, 9)],
    )


def atom_back(envs, cots):
    return jax.vjp(atom_terms, envs)[1](cots)[0]


def tile(t):
    return slice(128 * t, 128 * t + 128)


def fold(value):
    total = value[0:8]
    for r in range(8, value.shape[0], 8):
        total = total + value[r : r + 8]
    return total


def unpack(packed, count, tmp):
    half = count // 2
    tmp[pl.ds(0, half, stride=2), :] = packed
    tmp[pl.ds(1, half, stride=2), :] = spin(packed, 64)
    value = tmp[0:count, :]
    return jnp.where(lanes(value.shape) < 64, value, spin(value, 64))


def store_64(ref, lead, doubled):
    high, low = split(doubled)
    ref[(*lead, slice(None), slice(0, 128))] = high
    ref[(*lead, slice(None), slice(128, 192))] = low[:, 0:64]


def store_128(ref, lead, value):
    high, low = split(value)
    ref[(*lead, slice(None), slice(0, 128))] = high
    ref[(*lead, slice(None), slice(128, 256))] = high
    ref[(*lead, slice(None), slice(256, 384))] = low


def store_96(ref, lead, value):
    high = value.astype(bf16).astype(f32)
    low = value - high
    high_on, low_on = spin(high, 96), spin(low, 64)
    lane = lanes(value.shape)
    ref[(*lead, slice(None), slice(0, 128))] = jnp.where(lane < 96, high, high_on).astype(bf16)
    ref[(*lead, slice(None), slice(128, 256))] = jnp.where(lane < 64, high_on, low_on).astype(bf16)
    ref[(*lead, slice(None), slice(256, 288))] = low_on[:, 0:32].astype(bf16)


def across(ref, index):
    return jnp.concatenate([ref[index, t : t + 1, :] for t in range(TILES)], 1)


def spread_rows(value):
    return jnp.concatenate([value[t : t + 1] for t in range(TILES)], 1)


def joined(grid):
    return jnp.concatenate([jnp.concatenate(row, 1) for row in grid], 0)


def keep_pair(ref, lead, value):
    high, low = split(value)
    half = value.shape[0]
    ref[(*lead, slice(0, half), slice(None))] = high
    ref[(*lead, slice(half, 2 * half), slice(None))] = low
    return high, low


def both(ref, lead=()):
    half = ref.shape[-2] // 2
    return ref[(*lead, slice(0, half), slice(None))], ref[(*lead, slice(half, 2 * half), slice(None))]


def shares(value):
    total = fold(value)
    return [total[:, tile(t)] for t in range(TILES)]


def tmp_rows(w, start):
    return jnp.concatenate([w[start : start + 2], jnp.zeros((14, 128), f32)], 0)


def weights_product(left, right):
    high, low = split(right)
    return product(left, high, low)


def prepare(par, st, sc):
    def turned(value):
        return value.T

    spare = iter(range(11))

    def doubled(at, count):
        return unpack(par[at : at + count // 2, :], count, sc.tmp.at[next(spare)])

    w = doubled(AT_EMBED, 18)
    w = jnp.concatenate([w[0:16], tmp_rows(w, 16)], 0)
    store_64(sc.wb_emb, (), w[0:16])
    high = w.astype(bf16).astype(f32)
    low = w - high
    turn = jnp.concatenate([high, high, low, jnp.zeros((32, 128), f32)], 0).T[0:64]
    st.wf_emb[...] = turn[:, 0 : 3 * FEAT].astype(bf16)
    envs, ones = [], []
    for k in range(LAYERS):
        w = doubled(AT_ENV + 32 * k, 64)
        envs.append(w)
        store_64(st.wb_env, (k,), w)
        store_64(st.wf_env, (k,), jnp.concatenate([w, w], 0).T[0:64])
    head = par[AT_HEAD : AT_HEAD + 64, :]
    for k in range(LAYERS):
        one = par[AT_ONE + 64 * k : AT_ONE + 64 * k + 64, :]
        store_128(st.wb_one, (k,), one)
        store_64(st.wf_one, (k,), jnp.concatenate([one, one], 0).T)
        w = doubled(AT_INV + 48 * k, 96)
        store_96(st.wf_inv, (k,), jnp.concatenate([w, jnp.zeros((32, 128), f32)], 0).T[0:64])
        high, low = split(w)
        left = jnp.concatenate([high, low[:, 0:64]], 1)
        w = weights_product(left, one)
        store_128(st.wb_io, (k,), w)
        store_96(st.wf_io, (k,), jnp.concatenate([w, jnp.zeros((32, 128), f32)], 0).T)
        w = doubled(AT_TWO + 64 * k, 128)
        high, low = split(w)
        left = jnp.concatenate([high, low[:, 0:64]], 1)
        st.wb_two[k] = left
        store_128(st.wf_two, (k,), w.T[0:64])
        if k < LAYERS - 1:
            w = weights_product(left, envs[k + 1])
            store_64(st.wb_te, (k,), w)
            store_128(st.wf_te, (k,), w.T[0:64])
        else:
            w = weights_product(left, head)
            store_128(st.wb_th, (), w)
            store_128(st.wf_th, (), w.T)
    store_128(st.wb_head, (), head)
    store_64(st.wf_head, (), jnp.concatenate([head, head], 0).T)
    st.whcol[...] = jnp.broadcast_to(par[AT_VEC : AT_VEC + 1, :], (128, 128)).T


def sine_parts(turns):
    whole = jnp.round(turns)
    rest = (turns - whole) * math.pi
    odd = whole - 2.0 * jnp.floor(whole * 0.5)
    sign = 1.0 - 2.0 * odd
    r2 = rest * rest
    sine = 0.0
    for n in (13, 11, 9, 7, 5, 3, 1):
        sine = sine * r2 + (-1.0) ** (n // 2) / math.factorial(n)
    cosine = 0.0
    for n in (14, 12, 10, 8, 6, 4, 2, 0):
        cosine = cosine * r2 + (-1.0) ** (n // 2) / math.factorial(n)
    return sign * rest * sine, sign * cosine


def first_kernel(ranks, axis, live, *refs):
    sources = refs[0:7]
    pay = refs[7]
    st = Refs(STATE, refs[8 : 8 + len(STATE)])
    rest = refs[8 + len(STATE) :]
    vec, own, loc, nsp, cen, tgt, par = rest[0:7]
    sems, payload, scatter = rest[7:10]
    sc = Refs(SCRATCH_A, rest[10:])
    me = lax.axis_index(axis)
    copies = [
        pltpu.make_async_copy(source, target, sems.at[n])
        for n, (source, target) in enumerate(zip(sources, rest[0:7], strict=True))
    ]
    for copy in copies:
        copy.start()
    for copy in copies:
        copy.wait()

    order = sc.tmp.at[10]
    code = ((own[...] * 32 + loc[...]) * 8 + nsp[...]).astype(f32)
    for q, value in enumerate((vec[0], vec[1], vec[2], code)):
        for a in range(4):
            order[pl.ds(32 * q + a, 8, stride=4), :] = spin(value, -32 * a)
    turned = order[...].T
    lane = lanes((8, 128))

    def picked(q):
        out = spin(turned[0:8], -32 * q)
        for g in range(1, 4):
            out = jnp.where(lane // 32 == g, spin(turned[8 * g : 8 * g + 8], 32 * (g - q)), out)
        return out

    xyz = [picked(q) for q in range(3)]
    codes = picked(3).astype(jnp.int32)
    for q in range(3):
        st.place[q] = xyz[q]
    local = lax.shift_right_logical(codes, 3) & 31
    owner = lax.shift_right_logical(codes, 8)
    kind = codes & 7
    st.owner[...] = owner
    sc.dbar[0] = jnp.zeros((8, 128), f32)
    sc.dbar[0, 0:1, 0:32] = cen[...].astype(f32)
    centre_kind = group_sum(sc.dbar[0])[0:1].astype(jnp.int32)

    d, f, harmonics = geometry(*xyz)
    geo = st.geo
    geo[0] = f
    for m in range(8):
        geo[m + 1] = harmonics[m]
    geo[9] = f * (1.0 / math.sqrt(NEI))

    orders = (rows_of((8, 128)) + 1).astype(f32)
    inv_d = 1.0 / d
    scale = math.sqrt(2.0 / cutoff_radius)
    tiles = []
    for t in range(TILES):
        row_inv = inv_d[t : t + 1]
        sine, cosine = sine_parts(orders * (d[t : t + 1] / cutoff_radius))
        b = (scale * sine) * row_inv
        slope = (scale * math.pi / cutoff_radius) * orders * cosine * row_inv - b * row_inv
        st.bes[0, :, tile(t)] = b
        st.bes[1, :, tile(t)] = slope
        row = rows_of((FEAT - 8, 128)) + 8
        hot = (row == centre_kind + 8) | (row == kind[t : t + 1] + 13)
        tiles.append(jnp.concatenate([b * f[t : t + 1], hot.astype(f32)], 0))
        st.hot[:, tile(t)] = (rows_of((ATOMS, 128)) == local[t : t + 1]).astype(f32).astype(bf16)
    phi = keep_pair(st.phi, (), jnp.concatenate(tiles, 1))

    prepare(par, st, sc)
    fw = spread_rows(f)

    s, s1, s2 = silu_parts(product(st.wf_emb[...], *phi))
    st.z1[...] = s1
    st.tz[...] = s2
    latent = s
    lat = keep_pair(st.latx, (0,), s)
    pq = product(st.wf_env[0], *lat)
    base = product(st.wf_one[0], *lat)
    ahead = product(st.wf_env[1], *lat)
    st.pq[0] = pq

    for k in range(LAYERS):
        for r in range(0, 32, 16):
            rs = slice(r, r + 16)
            sums = None
            for t in range(TILES):
                a = pq[rs, tile(t)] * geo[9, t : t + 1, :]
                terms = [a] + [a * geo[m, t : t + 1, :] for m in range(1, 9)]
                sums = terms if sums is None else [x + y for x, y in zip(sums, terms, strict=True)]
            for m in range(9):
                st.env[k, m, rs, :] = group_sum(sums[m])
        for r in range(0, 32, 8):
            rs = slice(r, r + 8)
            envs = [[st.env[j, m, rs, :] for m in range(9)] for j in range(k + 1)]
            level, factors = atom_terms(envs)
            for l in range(3):
                st.bb[k, l, rs, :] = level[l]
            for m in range(8):
                st.eh[k, m, rs, :] = factors[m]
        high = [[None] * TILES for _ in range(6)]
        low = [[None] * TILES for _ in range(6)]
        for r in range(0, 32, 16):
            rs = slice(r, r + 16)
            for t in range(TILES):
                ts = tile(t)
                q = pq[32 + r : 48 + r, ts]
                if k > 0:
                    q = mix * st.qq[k - 1, rs, ts] * q
                st.qq[k, rs, ts] = q
                values = [st.bb[k, l, rs, :] for l in range(3)]
                for m in range(1, 9):
                    l = degree(m)
                    values[l] = values[l] + geo[m, t : t + 1, :] * st.eh[k, m - 1, rs, :]
                st.vv[k, rs, ts] = values[1]
                st.vv[k, 32 + r : 48 + r, ts] = values[2]
                for l in range(3):
                    n = 2 * l + r // 16
                    high[n][t], low[n][t] = split(q * values[l])
        high, low = joined(high), joined(low)
        st.ivx[k, 0:96, :] = high
        st.ivx[k, 96:192, :] = low
        h = base + product(st.wf_io[k], high, low)
        s, s1, s2 = silu_parts(h)
        st.s1[k] = s1
        st.t2[k] = s2
        pair_s = keep_pair(st.sx, (k,), s)
        if k < LAYERS - 1:
            step = product(st.wf_te[k], *pair_s)
            st.ts[k] = step
            pq = ahead + fw * step
            st.pq[k + 1] = pq
        else:
            step = product(st.wf_th[...], *pair_s)
            st.th[...] = step
            hh = ahead + fw * step
        o = product(st.wf_two[k], *pair_s)
        st.oo[k] = o
        latent = latent + fw * o
        lat = keep_pair(st.latx, (k + 1,), latent)
        if k < LAYERS - 1:
            base = product(st.wf_one[k + 1], *lat)
            ahead = product(st.wf_env[k + 2] if k + 2 < LAYERS else st.wf_head[...], *lat)

    s, s1, s2 = silu_parts(hh)
    st.sh[...] = s
    st.h1[...] = s1
    st.h2[...] = s2
    whcol = jnp.concatenate([st.whcol[...]] * TILES, 1)
    back = keep_pair(st.hhb, (), fw * whcol * s1)
    for t, share in enumerate(shares(whcol * s)):
        sc.ybar[0, t] = share
    xb = product(st.wb_th[...], *back)
    lb = product(st.wb_head[...], *back)

    for k in reversed(range(LAYERS)):
        st.xb[k] = xb
        sb = fw * xb
        pair_h = keep_pair(st.hb, (k,), st.s1[k] * sb)
        st.t2[k] = st.t2[k] * sb
        vb = product(st.wb_io[k], *pair_h)
        ib = product(st.wb_one[k], *pair_h)
        st.vb[k] = vb
        st.lb[k] = lb
        keep_pair(st.ob, (k,), fw * lb)
        for t, share in enumerate(shares(st.oo[k] * lb)):
            sc.ybar[0, t] += share
        run = lb + ib
        if k > 0:
            ahead = product(st.wb_two[k - 1], *split(run))
        for r in range(0, 32, 16):
            rs = slice(r, r + 16)
            sums = None
            for t in range(TILES):
                ts = tile(t)
                q = st.qq[k, rs, ts]
                vs = [vb[32 * l + r : 32 * l + r + 16, ts] for l in range(3)]
                qb = (
                    vs[0] * st.bb[k, 0, rs, :]
                    + vs[1] * st.vv[k, rs, ts]
                    + vs[2] * st.vv[k, 32 + r : 48 + r, ts]
                )
                if k < LAYERS - 1:
                    qb = qb + mix * st.pq[k + 1, 32 + r : 48 + r, ts] * st.qb[k + 1, rs, ts]
                st.qb[k, rs, ts] = qb
                back = [x * q for x in vs]
                terms = list(back)
                for m in range(1, 9):
                    terms.append(back[degree(m)] * geo[m, t : t + 1, :])
                    share = fold(back[degree(m)] * st.eh[k, m - 1, rs, :])
                    if k == LAYERS - 1 and r == 0:
                        sc.ybar[m, t] = share
                    else:
                        sc.ybar[m, t] += share
                sums = terms if sums is None else [x + y for x, y in zip(sums, terms, strict=True)]
            for n in range(11):
                st.cot[k, n, rs, :] = group_sum(sums[n])
        for r in range(0, 32, 8):
            rs = slice(r, r + 8)
            envs = [[st.env[j, m, rs, :] for m in range(9)] for j in range(k + 1)]
            cots = [st.cot[k, n, rs, :] for n in range(11)]
            back = atom_back(envs, (cots[:3], cots[3:]))
            for j in range(k + 1):
                for m in range(9):
                    if k == LAYERS - 1:
                        st.eb[j, m, rs, :] = back[j][m]
                    else:
                        st.eb[j, m, rs, :] += back[j][m]
        high = [[None] * TILES for _ in range(4)]
        low = [[None] * TILES for _ in range(4)]
        for r in range(0, 32, 16):
            rs = slice(r, r + 16)
            for t in range(TILES):
                ts = tile(t)
                p = st.pq[k, rs, ts]
                fs = geo[9, t : t + 1, :]
                a = p * fs
                ab = st.eb[k, 0, rs, :]
                for m in range(1, 9):
                    e = st.eb[k, m, rs, :]
                    ab = ab + geo[m, t : t + 1, :] * e
                    sc.ybar[m, t] += fold(a * e)
                st.ab[k, rs, ts] = ab
                sc.ybar[0, t] += fold((1.0 / math.sqrt(NEI)) * ab * p)
                qb = st.qb[k, rs, ts]
                if k > 0:
                    qb = mix * st.qq[k - 1, rs, ts] * qb
                high[r // 16][t], low[r // 16][t] = split(ab * fs)
                high[2 + r // 16][t], low[2 + r // 16][t] = split(qb)
        high, low = joined(high), joined(low)
        st.pb[k, 0:64, :] = high
        st.pb[k, 64:128, :] = low
        if k > 0:
            xb = ahead + product(st.wb_te[k - 1], high, low)
        lb = run + product(st.wb_env[k], high, low)

    st.tz[...] = st.tz[...] * lb
    pb = product(sc.wb_emb[...], *keep_pair(st.zb, (), st.z1[...] * lb))[0:8]
    for t in range(TILES):
        part = pb[:, tile(t)]
        sc.ybar[0, t] += st.bes[0, :, tile(t)] * part
        sc.dbar[t] = geo[0, t : t + 1, :] * st.bes[1, :, tile(t)] * part

    bars = [jnp.sum(sc.ybar[m], axis=1) for m in range(9)]
    slopes = jax.vjp(geometry, *xyz)[1]((jnp.sum(sc.dbar[...], axis=1), bars[0], bars[1:]))

    for t in range(TILES):
        mine = rows_of((ranks, 128)) == owner[t : t + 1]
        parts = jnp.concatenate([jnp.where(mine, s[t : t + 1], 0.0) for s in slopes], 0)
        high = parts.astype(bf16).astype(f32)
        scatter[:, tile(t)] = jnp.concatenate([high, parts - high], 0).astype(bf16)
    sums = lax.dot_general(
        scatter[...], st.hot[...], (((1,), (1,)), ((), ())), preferred_element_type=f32
    )
    payload[...] = jnp.zeros(payload.shape, f32)
    for q in range(3):
        at = ranks * q
        total = jnp.broadcast_to(jnp.sum(slopes[q], axis=0, keepdims=True), (8, 128))
        total = group_sum(total)[0:1, 0:32]
        part = -(sums[at : at + ranks] + sums[3 * ranks + at : 4 * ranks + at])
        payload[at : at + ranks, 0:32] = part + jnp.where(
            rows_of((ranks, 32)) == me, total, 0.0
        )
    for q in range(3):
        payload[3 * ranks + q : 3 * ranks + q + 1, 0:32] = tgt[q]
    payload[3 * ranks + 3 : 3 * ranks + 4, 0:32] = (lanes((1, 32)) < live[0, 0]).astype(f32)

    def spread(j, carry):
        pay[j] = payload[...]
        return carry

    lax.fori_loop(0, ranks, spread, 0)


def cross(x, y):
    return lax.dot_general(x, y, (((1,), (1,)), ((), ())), preferred_element_type=f32)


def settle(full):
    rows, columns = full.shape[0] // 2, full.shape[1] // 2
    if columns == 64:
        return full[:rows] + (spin(full[:rows], 64) + full[rows:])
    return full[:rows, :columns] + (full[:rows, columns:] + full[rows:, :columns])


def pack(value, tmp):
    count = value.shape[0]
    tmp[0:count, :] = value
    even, odd = tmp[pl.ds(0, count // 2, stride=2), :], tmp[pl.ds(1, count // 2, stride=2), :]
    return jnp.where(lanes(even.shape) < 64, even, spin(odd, 64))


def second_kernel(ranks, axis, pick, live, got, *refs):
    st = Refs(STATE, refs[: len(STATE)])
    keep, give, forces, tm, aim = refs[len(STATE) : len(STATE) + 5]
    sc = Refs(SCRATCH_B, refs[len(STATE) + 5 :])
    me = lax.axis_index(axis)
    geo, gd = st.geo, sc.gd

    total = got[0, 0 : 3 * ranks, :]
    for j in range(1, ranks):
        total = total + got[j, 0 : 3 * ranks, :]
    for j in range(ranks):
        for q in range(4):
            tm[q * ranks + j : q * ranks + j + 1, :] = got[j, 3 * ranks + q : 3 * ranks + q + 1, :]
    mask = tm[3 * ranks : 4 * ranks, :]
    mine = rows_of((ranks, 128)) == me
    loss = jnp.zeros((ranks, 128), f32)
    centre = []
    for q in range(3):
        at = slice(q * ranks, q * ranks + ranks)
        error = mask * (total[at] - tm[at, :])
        loss = loss + jnp.where(mine, error * error, 0.0)
        forces[q] = jnp.sum(jnp.where(mine, total[at], 0.0), axis=0, keepdims=True)[:, 0:32]
        error = 2.0 * error
        aim[at, :] = error
        own = jnp.sum(jnp.where(mine, error, 0.0), axis=0, keepdims=True)
        centre.append(group_sum(jnp.broadcast_to(own, (8, 128)))[0:1])
    aims = aim[...]
    high = aims.astype(bf16).astype(f32)
    stacked = jnp.concatenate([high, aims - high], 0).astype(bf16)[:, 0:32]
    seen = jnp.dot(stacked, st.hot[...], preferred_element_type=f32)
    seen = seen[0 : 3 * ranks] + seen[3 * ranks :]
    for t in range(TILES):
        at_owner = rows_of((ranks, 128)) == st.owner[t : t + 1, :]
        for q in range(3):
            there = jnp.where(at_owner, seen[q * ranks : q * ranks + ranks, tile(t)], 0.0)
            sc.cdir[q, t : t + 1, :] = centre[q] - jnp.sum(there, axis=0, keepdims=True)

    xyz = tuple(st.place[q] for q in range(3))
    ways = tuple(sc.cdir[q] for q in range(3))
    _, (dd, fd, yd) = jax.jvp(geometry, xyz, ways)
    gd[0] = fd
    for m in range(8):
        gd[m + 1] = yd[m]
    gd[9] = fd * (1.0 / math.sqrt(NEI))
    tiles = []
    for t in range(TILES):
        b, slope = st.bes[0, :, tile(t)], st.bes[1, :, tile(t)]
        row = fd[t : t + 1] * b + (geo[0, t : t + 1, :] * dd[t : t + 1]) * slope
        tiles.append(jnp.concatenate([row, jnp.zeros((FEAT - 8, 128), f32)], 0))
    phid = keep_pair(sc.phid, (), jnp.concatenate(tiles, 1))
    fw, fdw = across(geo, 0), spread_rows(fd)

    zd = product(st.wf_emb[...], *phid)
    sc.zd[...] = zd
    latent = st.z1[...] * zd
    lat = keep_pair(sc.latd, (0,), latent)
    pqd = product(st.wf_env[0], *lat)
    base = product(st.wf_one[0], *lat)
    ahead = product(st.wf_env[1], *lat)
    sc.pqd[0] = pqd

    for k in range(LAYERS):
        for r in range(0, 32, 16):
            rs = slice(r, r + 16)
            sums = None
            for t in range(TILES):
                ts = tile(t)
                p = st.pq[k, rs, ts]
                a = p * geo[9, t : t + 1, :]
                ad = pqd[rs, ts] * geo[9, t : t + 1, :] + p * gd[9, t : t + 1, :]
                terms = [ad] + [
                    ad * geo[m, t : t + 1, :] + a * gd[m, t : t + 1, :] for m in range(1, 9)
                ]
                sums = terms if sums is None else [x + y for x, y in zip(sums, terms, strict=True)]
            for m in range(9):
                sc.envd[k, m, rs, :] = group_sum(sums[m])
        for r in range(0, 32, 8):
            rs = slice(r, r + 8)
            envs = [[st.env[j, m, rs, :] for m in range(9)] for j in range(k + 1)]
            envds = [[sc.envd[j, m, rs, :] for m in range(9)] for j in range(k + 1)]
            _, (level, factors) = jax.jvp(atom_terms, (envs,), (envds,))
            for l in range(3):
                sc.bd[k, l, rs, :] = level[l]
            for m in range(8):
                sc.ehd[k, m, rs, :] = factors[m]
        high = [[None] * TILES for _ in range(6)]
        low = [[None] * TILES for _ in range(6)]
        for r in range(0, 32, 16):
            rs = slice(r, r + 16)
            ru = slice(32 + r, 48 + r)
            for t in range(TILES):
                ts = tile(t)
                qd = pqd[ru, ts]
                if k > 0:
                    qd = mix * (
                        sc.qd[k - 1, rs, ts] * st.pq[k, ru, ts] + st.qq[k - 1, rs, ts] * qd
                    )
                sc.qd[k, rs, ts] = qd
                q = st.qq[k, rs, ts]
                values = [st.bb[k, 0, rs, :], st.vv[k, rs, ts], st.vv[k, ru, ts]]
                moves = [sc.bd[k, l, rs, :] for l in range(3)]
                for m in range(1, 9):
                    l = degree(m)
                    moves[l] = (
                        moves[l]
                        + geo[m, t : t + 1, :] * sc.ehd[k, m - 1, rs, :]
                        + gd[m, t : t + 1, :] * st.eh[k, m - 1, rs, :]
                    )
                sc.vvd[k, rs, ts] = moves[1]
                sc.vvd[k, ru, ts] = moves[2]
                for l in range(3):
                    n = 2 * l + r // 16
                    high[n][t], low[n][t] = split(qd * values[l] + q * moves[l])
        high, low = joined(high), joined(low)
        sc.ivd[k, 0:96, :] = high
        sc.ivd[k, 96:192, :] = low
        hd = base + product(st.wf_io[k], high, low)
        sc.hd[k] = hd
        pair_s = keep_pair(sc.sd, (k,), st.s1[k] * hd)
        if k < LAYERS - 1:
            pqd = ahead + fdw * st.ts[k] + fw * product(st.wf_te[k], *pair_s)
            sc.pqd[k + 1] = pqd
        else:
            hhd = ahead + fdw * st.th[...] + fw * product(st.wf_th[...], *pair_s)
        od = product(st.wf_two[k], *pair_s)
        latent = latent + fdw * st.oo[k] + fw * od
        lat = keep_pair(sc.latd, (k + 1,), latent)
        if k < LAYERS - 1:
            base = product(st.wf_one[k + 1], *lat)
            ahead = product(st.wf_env[k + 2] if k + 2 < LAYERS else st.wf_head[...], *lat)

    whcol = jnp.concatenate([st.whcol[...]] * TILES, 1)
    back = keep_pair(sc.hht, (), whcol * (fdw * st.h1[...] + fw * st.h2[...] * hhd))
    xt = product(st.wb_th[...], *back)
    lt = product(st.wb_head[...], *back)
    part = fw * st.h1[...] * hhd + fdw * st.sh[...]
    vector = part[:, tile(0)]
    for t in range(1, TILES):
        vector = vector + part[:, tile(t)]
    sc.grad[AT_VEC : AT_VEC + 1, :] = jnp.sum(vector.T, axis=0, keepdims=True)

    queue = []
    spare = [0]

    def work(count):
        for _ in range(min(count, len(queue))):
            queue.pop(0)()

    def single(rows, columns, first, second, finish):
        def begin():
            sc.part[0:rows, 0:columns] = cross(*first())

        def end():
            finish(settle(sc.part[0:rows, 0:columns] + cross(*second())))

        queue.extend((begin, end))

    def plain(at, count):
        def finish(value):
            sc.grad[at : at + count, :] = value

        return finish

    def packed(at, count):
        def finish(value):
            spare[0] = (spare[0] + 1) % 8
            sc.grad[at : at + count, :] = pack(value, sc.tmp.at[spare[0]])[0:count]

        return finish

    def middle(k):
        def finish(value):
            moved = value[0:96]
            high, low = split(moved)
            at = AT_ONE + 64 * k
            sc.grad[at : at + 64, :] = value[96:160] + product(st.wf_inv[k], high, low)
            inv = cross(jnp.concatenate([high, low, high], 1), st.wb_one[k])
            inv = jnp.concatenate([inv, jnp.zeros((96, 64), f32)], 1)
            packed(AT_INV + 48 * k, 48)(inv)

        return finish

    def stack(lat, inv):
        return jnp.concatenate([inv[0:96, :], lat[0:64, :], inv[96:192, :], lat[64:128, :]], 0)

    single(
        128,
        256,
        lambda: (sc.latd[3], st.hhb[...]),
        lambda: (st.latx[3], sc.hht[...]),
        plain(AT_HEAD, 64),
    )

    for k in reversed(range(LAYERS)):
        ht = (fdw * st.xb[k] + fw * xt) * st.s1[k] + st.t2[k] * sc.hd[k]
        pair_h = keep_pair(sc.ht, (k,), ht)
        vt = product(st.wb_io[k], *pair_h)
        it = product(st.wb_one[k], *pair_h)
        keep_pair(sc.ot, (k,), fdw * st.lb[k] + fw * lt)
        run = lt + it
        if k > 0:
            ahead = product(st.wb_two[k - 1], *split(run))
        work(2)
        single(
            320,
            256,
            lambda k=k: (stack(sc.latd[k], sc.ivd[k]), st.hb[k]),
            lambda k=k: (stack(st.latx[k], st.ivx[k]), sc.ht[k]),
            middle(k),
        )
        single(
            256,
            128,
            lambda k=k: (sc.sd[k], st.ob[k]),
            lambda k=k: (st.sx[k], sc.ot[k]),
            packed(AT_TWO + 64 * k, 64),
        )
        for r in range(0, 32, 16):
            rs = slice(r, r + 16)
            ru = slice(32 + r, 48 + r)
            sums = None
            for t in range(TILES):
                ts = tile(t)
                q, qd = st.qq[k, rs, ts], sc.qd[k, rs, ts]
                ls = [slice(32 * l + r, 32 * l + r + 16) for l in range(3)]
                vb = [st.vb[k, s, ts] for s in ls]
                vs = [vt[s, ts] for s in ls]
                qt = (
                    vs[0] * st.bb[k, 0, rs, :]
                    + vs[1] * st.vv[k, rs, ts]
                    + vs[2] * st.vv[k, ru, ts]
                    + vb[0] * sc.bd[k, 0, rs, :]
                    + vb[1] * sc.vvd[k, rs, ts]
                    + vb[2] * sc.vvd[k, ru, ts]
                )
                if k < LAYERS - 1:
                    qt = qt + mix * (
                        sc.pqd[k + 1, ru, ts] * st.qb[k + 1, rs, ts]
                        + st.pq[k + 1, ru, ts] * sc.qt[k + 1, rs, ts]
                    )
                sc.qt[k, rs, ts] = qt
                back = [x * q for x in vb]
                twist = [x * q + y * qd for x, y in zip(vs, vb, strict=True)]
                terms = list(twist)
                for m in range(1, 9):
                    l = degree(m)
                    terms.append(twist[l] * geo[m, t : t + 1, :] + back[l] * gd[m, t : t + 1, :])
                sums = terms if sums is None else [x + y for x, y in zip(sums, terms, strict=True)]
            for n in range(11):
                sc.cott[n, rs, :] = group_sum(sums[n])
        work(1)
        for r in range(0, 32, 8):
            rs = slice(r, r + 8)
            envs = [[st.env[j, m, rs, :] for m in range(9)] for j in range(k + 1)]
            envds = [[sc.envd[j, m, rs, :] for m in range(9)] for j in range(k + 1)]
            cots = [st.cot[k, n, rs, :] for n in range(11)]
            cotts = [sc.cott[n, rs, :] for n in range(11)]
            _, back = jax.jvp(
                atom_back,
                (envs, (cots[:3], cots[3:])),
                (envds, (cotts[:3], cotts[3:])),
            )
            for j in range(k + 1):
                for m in range(9):
                    if k == LAYERS - 1:
                        sc.et[j, m, rs, :] = back[j][m]
                    else:
                        sc.et[j, m, rs, :] += back[j][m]
        work(1)
        high = [[None] * TILES for _ in range(4)]
        low = [[None] * TILES for _ in range(4)]
        for r in range(0, 32, 16):
            rs = slice(r, r + 16)
            for t in range(TILES):
                ts = tile(t)
                at = sc.et[k, 0, rs, :]
                for m in range(1, 9):
                    at = (
                        at
                        + geo[m, t : t + 1, :] * sc.et[k, m, rs, :]
                        + gd[m, t : t + 1, :] * st.eb[k, m, rs, :]
                    )
                qt = sc.qt[k, rs, ts]
                if k > 0:
                    qt = mix * (sc.qd[k - 1, rs, ts] * st.qb[k, rs, ts] + st.qq[k - 1, rs, ts] * qt)
                pt = at * geo[9, t : t + 1, :] + st.ab[k, rs, ts] * gd[9, t : t + 1, :]
                high[r // 16][t], low[r // 16][t] = split(pt)
                high[2 + r // 16][t], low[2 + r // 16][t] = split(qt)
        high, low = joined(high), joined(low)
        sc.pt[k, 0:64, :] = high
        sc.pt[k, 64:128, :] = low
        if k > 0:
            xt = ahead + product(st.wb_te[k - 1], high, low)
        lt = run + product(st.wb_env[k], high, low)
        single(
            128,
            128,
            lambda k=k: (sc.latd[k], st.pb[k]),
            lambda k=k: (st.latx[k], sc.pt[k]),
            packed(AT_ENV + 32 * k, 32),
        )
        work(2)

    keep_pair(sc.zt, (), lt * st.z1[...] + st.tz[...] * sc.zd[...])
    single(
        2 * FEAT,
        128,
        lambda: (sc.phid[...], st.zb[...]),
        lambda: (st.phi[...], sc.zt[...]),
        packed(AT_EMBED, 9),
    )
    work(len(queue))
    sc.grad[ROWS:PADDED, :] = jnp.zeros((PADDED - ROWS, 128), f32)
    lane = lanes((1, 128))
    amount = 3.0 * live[0, 0].astype(f32)
    sc.grad[ROWS : ROWS + 1, :] = jnp.where(
        lane == 0, jnp.sum(loss), jnp.where(lane == 1, amount, 0.0)
    )
    half = lax.axis_index(pick)
    keep[...] = sc.grad[pl.ds(pl.multiple_of(half * HALF, HALF), HALF), :]
    give[...] = sc.grad[pl.ds(pl.multiple_of((1 - half) * HALF, HALF), HALF), :]


def third_kernel(pick, mine, other, par, first, second, avg, *outs):
    loss, count, norm, new_first, new_second, new_par, low, new_avg = outs
    half = lax.axis_index(pick)
    lower = jnp.where(half == 0, mine[...], other[...])
    upper = jnp.where(half == 0, other[...], mine[...])
    last = ROWS - HALF
    scalars = upper[last : last + 1]
    loss[...] = scalars[:, 0:1]
    amount = scalars[:, 1:2]
    count[...] = amount
    squares = jnp.sum(lower * lower, keepdims=True) + jnp.sum(
        upper[0:last] * upper[0:last], keepdims=True
    )
    length = jnp.sqrt(squares) / amount
    norm[...] = length
    factor = (clip_level / jnp.maximum(length, clip_level)) / amount
    for start, stop, value in ((0, HALF, lower), (HALF, ROWS, upper[0:last])):
        rows = slice(start, stop)
        gradient = value * factor
        one = beta_one * first[rows, :] + (1.0 - beta_one) * gradient
        two = beta_two * second[rows, :] + (1.0 - beta_two) * gradient * gradient
        fixed_one = one / (1.0 - beta_one**STEP)
        fixed_two = two / (1.0 - beta_two**STEP)
        weights = par[rows, :]
        weights = weights - learn_rate * (
            fixed_one / (jnp.sqrt(fixed_two) + epsilon_adam) + decay_rate * weights
        )
        new_first[rows, :] = one
        new_second[rows, :] = two
        new_par[rows, :] = weights
        low[rows, :] = weights.astype(bf16)
        new_avg[rows, :] = average_keep * avg[rows, :] + (1.0 - average_keep) * weights


VMEM = pl.BlockSpec(memory_space=pltpu.VMEM)
HBM = pl.BlockSpec(memory_space=pltpu.HBM)
SMEM = pl.BlockSpec(memory_space=pltpu.SMEM)


def scratch(entries):
    return [pltpu.VMEM(shape, dtype) for _, shape, dtype in entries]


def local(
    ranks,
    params,
    first_moment,
    second_moment,
    average,
    edge_vectors,
    owner_rank,
    neighbour_local,
    centre_species,
    neighbour_species,
    live_atoms,
    target_forces,
):
    shape = jax.ShapeDtypeStruct
    flat = (ROWS, 128)
    par = params.reshape(flat)
    live = live_atoms.reshape(1, 1)
    tall = 3 * ranks + 8
    state = [shape(s, t) for _, s, t in STATE]
    sources = (
        edge_vectors.reshape(3, 8, 128),
        owner_rank.reshape(8, 128),
        neighbour_local.reshape(8, 128),
        neighbour_species.reshape(8, 128),
        centre_species.reshape(1, ATOMS),
        target_forces.reshape(3, 1, ATOMS),
        par,
    )
    pay, *kept = pl.pallas_call(
        functools.partial(first_kernel, ranks, "atoms"),
        out_shape=[shape((ranks, tall, 128), f32), *state],
        in_specs=[SMEM] + [HBM] * 7,
        out_specs=[VMEM] * (1 + len(state)),
        scratch_shapes=[
            *[pltpu.VMEM(x.shape, x.dtype) for x in sources],
            pltpu.SemaphoreType.DMA((7,)),
            pltpu.VMEM((tall, 128), f32),
            pltpu.VMEM((6 * ranks, EDGES), bf16),
            *scratch(SCRATCH_A),
        ],
        compiler_params=pltpu.CompilerParams(vmem_limit_bytes=16 * 2**20),
        name="forward",
    )(live, *sources)
    got = lax.all_to_all(pay, "atoms", split_axis=0, concat_axis=0, tiled=True)
    keep, give, forces = pl.pallas_call(
        functools.partial(second_kernel, ranks, "atoms", "low"),
        out_shape=[shape((HALF, 128), f32), shape((HALF, 128), f32), shape((3, 1, ATOMS), f32)],
        in_specs=[SMEM, VMEM] + [VMEM] * len(state),
        out_specs=[VMEM] * 3,
        scratch_shapes=[
            pltpu.VMEM((4 * ranks, 128), f32),
            pltpu.VMEM((3 * ranks, 128), f32),
            *scratch(SCRATCH_B),
        ],
        compiler_params=pltpu.CompilerParams(vmem_limit_bytes=20 * 2**20),
        name="gradient",
    )(live, got, *kept)
    swap = [(0, 1), (1, 0)]
    axes, size = ("atoms", "high"), ranks * 2
    held = keep + lax.ppermute(give, "low", swap)
    pieces = size * 8 * -(-HALF // (8 * size))
    held = jnp.pad(held, ((0, pieces - HALF), (0, 0))).reshape(size, pieces // size, 128)
    summed = lax.all_to_all(held, axes, split_axis=0, concat_axis=0, tiled=True).sum(0)
    summed = jnp.broadcast_to(summed[None], (size, *summed.shape))
    mine = lax.all_to_all(summed, axes, split_axis=0, concat_axis=0, tiled=True)
    mine = mine.reshape(pieces, 128)[:HALF]
    other = lax.ppermute(mine, "low", swap)
    one, vec = shape((1, 1), f32), shape(flat, f32)
    loss, count, norm, new_first, new_second, new_params, low, new_average = pl.pallas_call(
        functools.partial(third_kernel, "low"),
        out_shape=[one, one, one, vec, vec, vec, shape(flat, bf16), vec],
        in_specs=[VMEM] * 6,
        out_specs=[VMEM] * 8,
        compiler_params=pltpu.CompilerParams(vmem_limit_bytes=16 * 2**20),
        name="update",
    )(
        mine,
        other,
        par,
        first_moment.reshape(flat),
        second_moment.reshape(flat),
        average.reshape(flat),
    )
    return (
        loss.reshape(()),
        count.reshape(()),
        norm.reshape(()),
        forces,
        new_first.reshape(-1),
        new_second.reshape(-1),
        new_params.reshape(-1),
        low.reshape(-1),
        new_average.reshape(-1),
    )


def solution(mesh):
    ranks, groups = mesh.shape["atoms"], mesh.shape["grp"]
    fine = Mesh(mesh.devices.reshape(ranks, groups // 2, 2), ("atoms", "high", "low"))
    grp = ("high", "low")
    in_specs = (
        P(),
        P(),
        P(),
        P(),
        P(None, grp, "atoms"),
        P(grp, "atoms", None),
        P(grp, "atoms"),
        P(grp, "atoms"),
        P(grp, "atoms"),
        P(grp, "atoms"),
        P(None, grp, "atoms"),
    )
    out_specs = (P(), P(), P(), P(None, grp, "atoms"), P(), P(), P(), P(), P())
    return jax.shard_map(
        functools.partial(local, ranks),
        mesh=fine,
        in_specs=in_specs,
        out_specs=out_specs,
        check_vma=False,
    )
```

```python
import functools
import math

import jax
import jax.numpy as jnp
from jax import lax
from jax.experimental import pallas as pl
from jax.experimental.pallas import tpu as pltpu
from jax.sharding import Mesh
from jax.sharding import PartitionSpec as P

LATENT = 64
UNITS = 128
CHANNELS = 32
BASES = 8
SPECIES = 5
LAYERS = 3
STEP = 10
NEI = 32
NPARAM = 89344

cutoff_radius = 5.0
clip_level = 0.01
learn_rate = 0.1
beta_one = 0.9
beta_two = 0.999
epsilon_adam = 1e-08
decay_rate = 0.01
average_keep = 0.99
mix = 0.7071

f32 = jnp.float32
bf16 = jnp.bfloat16

ATOMS = 32
EDGES = 1024
TILES = 8
FEAT = 32

AT_EMBED = 0
AT_ENV = 9
AT_INV = AT_ENV + 96
AT_ONE = AT_INV + 144
AT_TWO = AT_ONE + 192
AT_HEAD = AT_TWO + 192
AT_VEC = AT_HEAD + 64
ROWS = AT_VEC + 1
PADDED = 768
HALF = PADDED // 2

STATE = [
    ("wf_emb", (LATENT, 3 * FEAT), bf16),
    ("wf_first", (64, 192), bf16),
    ("wf_lat", (3, 256, 192), bf16),
    ("wf_io", (3, 128, 288), bf16),
    ("wf_s", (3, 192, 384), bf16),
    ("wf_inv", (3, 64, 288), bf16),
    ("wb_hh", (192, 384), bf16),
    ("wb_h", (3, 160, 384), bf16),
    ("wb_p", (3, 192, 192), bf16),
    ("wb_two", (3, 128, 192), bf16),
    ("whcol", (128, 128), f32),
    ("place", (3, 8, 128), f32),
    ("owner", (8, 128), jnp.int32),
    ("hot", (ATOMS, EDGES), bf16),
    ("geo", (10, 8, 128), f32),
    ("bes", (2, BASES, EDGES), f32),
    ("phi", (2 * FEAT, EDGES), bf16),
    ("latx", (4, 128, EDGES), bf16),
    ("pq", (3, 64, EDGES), f32),
    ("vv", (3, 64, EDGES), f32),
    ("ivx", (3, 192, EDGES), bf16),
    ("sx", (3, 256, EDGES), bf16),
    ("s1", (3, 128, EDGES), f32),
    ("t2", (3, 128, EDGES), f32),
    ("oo", (3, 64, EDGES), f32),
    ("ts", (2, 64, EDGES), f32),
    ("th", (128, EDGES), f32),
    ("lb", (3, 64, EDGES), f32),
    ("ob", (3, 128, EDGES), bf16),
    ("hb", (3, 256, EDGES), bf16),
    ("xb", (3, 128, EDGES), f32),
    ("vb", (3, 96, EDGES), f32),
    ("ab", (3, 32, EDGES), f32),
    ("pb", (3, 128, EDGES), bf16),
    ("qq", (3, 32, EDGES), f32),
    ("qb", (3, 32, EDGES), f32),
    ("z1", (64, EDGES), f32),
    ("tz", (64, EDGES), f32),
    ("zb", (128, EDGES), bf16),
    ("sh", (128, EDGES), f32),
    ("h1", (128, EDGES), f32),
    ("h2", (128, EDGES), f32),
    ("hhb", (256, EDGES), bf16),
    ("env", (3, 9, 32, 128), f32),
    ("eh", (3, 8, 32, 128), f32),
    ("bb", (3, 3, 32, 128), f32),
    ("eb", (3, 9, 32, 128), f32),
    ("cot", (3, 11, 32, 128), f32),
]

SCRATCH_A = [
    ("tmp", (11, 128, 128), f32),
    ("wb_emb", (16, 192), bf16),
    ("ybar", (9, 8, 8, 128), f32),
    ("dbar", (8, 8, 128), f32),
]

SCRATCH_B = [
    ("tmp", (8, 128, 128), f32),
    ("part", (320, 256), f32),
    ("mid", (3, 160, 128), f32),
    ("cdir", (3, 8, 128), f32),
    ("gd", (10, 8, 128), f32),
    ("phid", (2 * FEAT, EDGES), bf16),
    ("zd", (64, EDGES), f32),
    ("latd", (4, 128, EDGES), bf16),
    ("pqd", (3, 64, EDGES), f32),
    ("vvd", (3, 64, EDGES), f32),
    ("qd", (3, 32, EDGES), f32),
    ("ivd", (3, 192, EDGES), bf16),
    ("hd", (3, 128, EDGES), f32),
    ("sd", (3, 256, EDGES), bf16),
    ("envd", (3, 9, 32, 128), f32),
    ("ehd", (3, 8, 32, 128), f32),
    ("bd", (3, 3, 32, 128), f32),
    ("hht", (256, EDGES), bf16),
    ("ot", (3, 128, EDGES), bf16),
    ("ht", (3, 256, EDGES), bf16),
    ("qt", (3, 32, EDGES), f32),
    ("pt", (3, 128, EDGES), bf16),
    ("zt", (128, EDGES), bf16),
    ("et", (3, 9, 32, 128), f32),
    ("cott", (11, 32, 128), f32),
    ("grad", (PADDED, 128), f32),
]


class Refs:
    def __init__(self, entries, refs):
        for (name, _, _), ref in zip(entries, refs, strict=True):
            setattr(self, name, ref)


def split(x):
    high = x.astype(bf16)
    return high, (x - high.astype(f32)).astype(bf16)


def product(weights, high, low):
    return jnp.dot(
        weights, jnp.concatenate([high, low, high], 0), preferred_element_type=f32
    )


def put(ref, rows, columns, value, lead=()):
    high, low = split(value)
    half = ref.shape[-2] // 2
    ref[(*lead, slice(rows, rows + value.shape[0]), columns)] = high
    ref[(*lead, slice(half + rows, half + rows + value.shape[0]), columns)] = low
    return high, low


def pair(ref, columns, lead=()):
    half = ref.shape[-2] // 2
    return ref[(*lead, slice(0, half), columns)], ref[(*lead, slice(half, 2 * half), columns)]


def spin(x, amount):
    return pltpu.roll(x, amount % 128, 1)


def group_sum(x):
    x = x + spin(x, 64)
    return x + spin(x, 32)


def lanes(shape):
    return lax.broadcasted_iota(jnp.int32, shape, len(shape) - 1)


def rows_of(shape):
    return lax.broadcasted_iota(jnp.int32, shape, len(shape) - 2)


def silu_parts(h):
    gate = 1.0 / (1.0 + jnp.exp(-h))
    slope = gate * (1.0 - gate)
    return h * gate, gate + h * slope, slope * (2.0 + h * (1.0 - 2.0 * gate))


def geometry(x, y, z):
    d = jnp.sqrt(x * x + y * y + z * z)
    u, v, w = x / d, y / d, z / d
    s = d / cutoff_radius
    s2 = s * s
    s6 = s2 * s2 * s2
    f = 1.0 - 28.0 * s6 + 48.0 * (s6 * s) - 21.0 * (s6 * s2)
    r3, r5, r15 = math.sqrt(3.0), math.sqrt(5.0), math.sqrt(15.0)
    harmonics = [
        r3 * u,
        r3 * v,
        r3 * w,
        r15 * u * v,
        r15 * v * w,
        0.5 * r5 * (3.0 * w * w - 1.0),
        r15 * u * w,
        0.5 * r15 * (u * u - v * v),
    ]
    return d, f, harmonics


def dots(left, right):
    total = left[0] * right[0]
    for a, b in zip(left[1:], right[1:], strict=True):
        total = total + a * b
    return total


def degree(m):
    return 1 if m <= 3 else 2


def atom_terms(envs):
    if len(envs) == 1:
        (one,) = envs
        zero = jnp.zeros_like(one[0])
        return [one[0], zero, zero], one[1:]
    if len(envs) == 2:
        one, two = envs
        return (
            [2.0 * one[0] * two[0], dots(one[1:4], two[1:4]), dots(one[4:], two[4:])],
            [one[0] * two[m] for m in range(1, 9)],
        )
    one, two, three = envs
    both = one[0] * two[0]
    twice = 2.0 * one[0]
    part = [two[0] * one[m] + twice * two[m] for m in range(1, 9)]
    return (
        [4.0 * both * three[0], dots(part[:3], three[1:4]), dots(part[3:], three[4:])],
        [both * three[m] for m in range(1, 9)],
    )


def atom_back(envs, cots):
    return jax.vjp(atom_terms, envs)[1](cots)[0]


def tile(t):
    return slice(128 * t, 128 * t + 128)


def fold(value):
    total = value[0:8]
    for r in range(8, value.shape[0], 8):
        total = total + value[r : r + 8]
    return total


def unpack(packed, count, tmp):
    half = count // 2
    tmp[pl.ds(0, half, stride=2), :] = packed
    tmp[pl.ds(1, half, stride=2), :] = spin(packed, 64)
    value = tmp[0:count, :]
    return jnp.where(lanes(value.shape) < 64, value, spin(value, 64))


def store_64(ref, lead, doubled, at=0):
    high, low = split(doubled)
    rows = slice(at, at + doubled.shape[0])
    ref[(*lead, rows, slice(0, 128))] = high
    ref[(*lead, rows, slice(128, 192))] = low[:, 0:64]


def store_128(ref, lead, value, at=0):
    high, low = split(value)
    rows = slice(at, at + value.shape[0])
    ref[(*lead, rows, slice(0, 128))] = high
    ref[(*lead, rows, slice(128, 256))] = high
    ref[(*lead, rows, slice(256, 384))] = low


def store_96(ref, lead, value):
    high = value.astype(bf16).astype(f32)
    low = value - high
    high_on, low_on = spin(high, 96), spin(low, 64)
    lane = lanes(value.shape)
    ref[(*lead, slice(None), slice(0, 128))] = jnp.where(lane < 96, high, high_on).astype(bf16)
    ref[(*lead, slice(None), slice(128, 256))] = jnp.where(lane < 64, high_on, low_on).astype(bf16)
    ref[(*lead, slice(None), slice(256, 288))] = low_on[:, 0:32].astype(bf16)


def across(ref, index):
    return jnp.concatenate([ref[index, t : t + 1, :] for t in range(TILES)], 1)


def spread_rows(value):
    return jnp.concatenate([value[t : t + 1] for t in range(TILES)], 1)


def joined(grid):
    return jnp.concatenate([jnp.concatenate(row, 1) for row in grid], 0)


def keep_pair(ref, lead, value):
    high, low = split(value)
    half = value.shape[0]
    ref[(*lead, slice(0, half), slice(None))] = high
    ref[(*lead, slice(half, 2 * half), slice(None))] = low
    return high, low


def both(ref, lead=()):
    half = ref.shape[-2] // 2
    return ref[(*lead, slice(0, half), slice(None))], ref[(*lead, slice(half, 2 * half), slice(None))]


def shares(value):
    total = fold(value)
    return [total[:, tile(t)] for t in range(TILES)]


def tmp_rows(w, start):
    return jnp.concatenate([w[start : start + 2], jnp.zeros((14, 128), f32)], 0)


def weights_product(left, right):
    high, low = split(right)
    return product(left, high, low)


def prepare(par, st, sc):
    def turned(value):
        return value.T

    spare = iter(range(11))

    def doubled(at, count):
        return unpack(par[at : at + count // 2, :], count, sc.tmp.at[next(spare)])

    w = doubled(AT_EMBED, 18)
    w = jnp.concatenate([w[0:16], tmp_rows(w, 16)], 0)
    store_64(sc.wb_emb, (), w[0:16])
    high = w.astype(bf16).astype(f32)
    low = w - high
    turn = jnp.concatenate([high, high, low, jnp.zeros((32, 128), f32)], 0).T[0:64]
    st.wf_emb[...] = turn[:, 0 : 3 * FEAT].astype(bf16)
    envs = []
    for k in range(LAYERS):
        w = doubled(AT_ENV + 32 * k, 64)
        envs.append(w)
        store_64(st.wb_p, (k,), w)
        turn = jnp.concatenate([w, w], 0).T[0:64]
        if k == 0:
            store_64(st.wf_first, (), turn)
        else:
            store_64(st.wf_lat, (k - 1,), turn, 128)
    head = par[AT_HEAD : AT_HEAD + 64, :]
    store_128(st.wb_hh, (), head, 128)
    store_64(st.wf_lat, (2,), jnp.concatenate([head, head], 0).T, 128)
    for k in range(LAYERS):
        one = par[AT_ONE + 64 * k : AT_ONE + 64 * k + 64, :]
        store_128(st.wb_h, (k,), one, 96)
        store_64(st.wf_lat, (k,), jnp.concatenate([one, one], 0).T)
        w = doubled(AT_INV + 48 * k, 96)
        store_96(st.wf_inv, (k,), jnp.concatenate([w, jnp.zeros((32, 128), f32)], 0).T[0:64])
        high, low = split(w)
        w = weights_product(jnp.concatenate([high, low[:, 0:64]], 1), one)
        store_128(st.wb_h, (k,), w)
        store_96(st.wf_io, (k,), jnp.concatenate([w, jnp.zeros((32, 128), f32)], 0).T)
        w = doubled(AT_TWO + 64 * k, 128)
        high, low = split(w)
        left = jnp.concatenate([high, low[:, 0:64]], 1)
        st.wb_two[k] = left
        store_128(st.wf_s, (k,), w.T[0:64])
        if k < LAYERS - 1:
            w = weights_product(left, envs[k + 1])
            store_64(st.wb_p, (k + 1,), w, 64)
            store_128(st.wf_s, (k,), w.T[0:64], 64)
        else:
            w = weights_product(left, head)
            store_128(st.wb_hh, (), w)
            store_128(st.wf_s, (k,), w.T, 64)
    st.whcol[...] = jnp.broadcast_to(par[AT_VEC : AT_VEC + 1, :], (128, 128)).T


def sine_parts(turns):
    whole = jnp.round(turns)
    rest = (turns - whole) * math.pi
    odd = whole - 2.0 * jnp.floor(whole * 0.5)
    sign = 1.0 - 2.0 * odd
    r2 = rest * rest
    sine = 0.0
    for n in (13, 11, 9, 7, 5, 3, 1):
        sine = sine * r2 + (-1.0) ** (n // 2) / math.factorial(n)
    cosine = 0.0
    for n in (14, 12, 10, 8, 6, 4, 2, 0):
        cosine = cosine * r2 + (-1.0) ** (n // 2) / math.factorial(n)
    return sign * rest * sine, sign * cosine


def first_kernel(ranks, axis, live, *refs):
    sources = refs[0:7]
    pay = refs[7]
    st = Refs(STATE, refs[8 : 8 + len(STATE)])
    rest = refs[8 + len(STATE) :]
    vec, own, loc, nsp, cen, tgt, par = rest[0:7]
    sems, payload, scatter = rest[7:10]
    sc = Refs(SCRATCH_A, rest[10:])
    me = lax.axis_index(axis)
    copies = [
        pltpu.make_async_copy(source, target, sems.at[n])
        for n, (source, target) in enumerate(zip(sources, rest[0:7], strict=True))
    ]
    for copy in copies:
        copy.start()
    for copy in copies[:-1]:
        copy.wait()

    order = sc.tmp.at[10]
    code = ((own[...] * 32 + loc[...]) * 8 + nsp[...]).astype(f32)
    for q, value in enumerate((vec[0], vec[1], vec[2], code)):
        for a in range(4):
            order[pl.ds(32 * q + a, 8, stride=4), :] = spin(value, -32 * a)
    turned = order[...].T
    lane = lanes((8, 128))

    def picked(q):
        out = spin(turned[0:8], -32 * q)
        for g in range(1, 4):
            out = jnp.where(lane // 32 == g, spin(turned[8 * g : 8 * g + 8], 32 * (g - q)), out)
        return out

    xyz = [picked(q) for q in range(3)]
    codes = picked(3).astype(jnp.int32)
    for q in range(3):
        st.place[q] = xyz[q]
    local = lax.shift_right_logical(codes, 3) & 31
    owner = lax.shift_right_logical(codes, 8)
    kind = codes & 7
    st.owner[...] = owner
    sc.dbar[0] = jnp.zeros((8, 128), f32)
    sc.dbar[0, 0:1, 0:32] = cen[...].astype(f32)
    centre_kind = group_sum(sc.dbar[0])[0:1].astype(jnp.int32)

    d, f, harmonics = geometry(*xyz)
    geo = st.geo
    geo[0] = f
    for m in range(8):
        geo[m + 1] = harmonics[m]
    geo[9] = f * (1.0 / math.sqrt(NEI))

    orders = (rows_of((8, 128)) + 1).astype(f32)
    inv_d = 1.0 / d
    scale = math.sqrt(2.0 / cutoff_radius)
    tiles = []
    for t in range(TILES):
        row_inv = inv_d[t : t + 1]
        sine, cosine = sine_parts(orders * (d[t : t + 1] / cutoff_radius))
        b = (scale * sine) * row_inv
        slope = (scale * math.pi / cutoff_radius) * orders * cosine * row_inv - b * row_inv
        st.bes[0, :, tile(t)] = b
        st.bes[1, :, tile(t)] = slope
        row = rows_of((FEAT - 8, 128)) + 8
        hot = (row == centre_kind + 8) | (row == kind[t : t + 1] + 13)
        tiles.append(jnp.concatenate([b * f[t : t + 1], hot.astype(f32)], 0))
        st.hot[:, tile(t)] = (rows_of((ATOMS, 128)) == local[t : t + 1]).astype(f32).astype(bf16)
    phi = keep_pair(st.phi, (), jnp.concatenate(tiles, 1))

    copies[-1].wait()
    prepare(par, st, sc)
    fw = spread_rows(f)

    s, s1, s2 = silu_parts(product(st.wf_emb[...], *phi))
    st.z1[...] = s1
    st.tz[...] = s2
    latent = s
    lat = keep_pair(st.latx, (0,), s)
    pq = product(st.wf_first[...], *lat)
    st.pq[0] = pq
    both_of = product(st.wf_lat[0, 0:192, :], *lat)
    base, ahead = both_of[0:128], both_of[128:192]

    for k in range(LAYERS):
        for r in range(0, 32, 16):
            rs = slice(r, r + 16)
            sums = None
            for t in range(TILES):
                a = pq[rs, tile(t)] * geo[9, t : t + 1, :]
                terms = [a] + [a * geo[m, t : t + 1, :] for m in range(1, 9)]
                sums = terms if sums is None else [x + y for x, y in zip(sums, terms, strict=True)]
            for m in range(9):
                st.env[k, m, rs, :] = group_sum(sums[m])
        for r in range(0, 32, 8):
            rs = slice(r, r + 8)
            envs = [[st.env[j, m, rs, :] for m in range(9)] for j in range(k + 1)]
            level, factors = atom_terms(envs)
            for l in range(3):
                st.bb[k, l, rs, :] = level[l]
            for m in range(8):
                st.eh[k, m, rs, :] = factors[m]
        high = [[None] * TILES for _ in range(6)]
        low = [[None] * TILES for _ in range(6)]
        for r in range(0, 32, 16):
            rs = slice(r, r + 16)
            for t in range(TILES):
                ts = tile(t)
                q = pq[32 + r : 48 + r, ts]
                if k > 0:
                    q = mix * st.qq[k - 1, rs, ts] * q
                st.qq[k, rs, ts] = q
                values = [st.bb[k, l, rs, :] for l in range(3)]
                for m in range(1, 9):
                    l = degree(m)
                    values[l] = values[l] + geo[m, t : t + 1, :] * st.eh[k, m - 1, rs, :]
                st.vv[k, rs, ts] = values[1]
                st.vv[k, 32 + r : 48 + r, ts] = values[2]
                for l in range(3):
                    n = 2 * l + r // 16
                    high[n][t], low[n][t] = split(q * values[l])
        high, low = joined(high), joined(low)
        st.ivx[k, 0:96, :] = high
        st.ivx[k, 96:192, :] = low
        h = base + product(st.wf_io[k], high, low)
        s, s1, s2 = silu_parts(h)
        st.s1[k] = s1
        st.t2[k] = s2
        pair_s = keep_pair(st.sx, (k,), s)
        last = k == LAYERS - 1
        both_of = product(st.wf_s[k] if last else st.wf_s[k, 0:128, :], *pair_s)
        o, step = both_of[0:64], both_of[64:]
        if last:
            st.th[...] = step
            hh = ahead + fw * step
        else:
            st.ts[k] = step
            pq = ahead + fw * step
            st.pq[k + 1] = pq
        st.oo[k] = o
        latent = latent + fw * o
        lat = keep_pair(st.latx, (k + 1,), latent)
        if not last:
            both_of = product(st.wf_lat[k + 1] if k + 2 == LAYERS else st.wf_lat[k + 1, 0:192, :], *lat)
            base, ahead = both_of[0:128], both_of[128:]

    s, s1, s2 = silu_parts(hh)
    st.sh[...] = s
    st.h1[...] = s1
    st.h2[...] = s2
    whcol = jnp.concatenate([st.whcol[...]] * TILES, 1)
    back = keep_pair(st.hhb, (), fw * whcol * s1)
    for t, share in enumerate(shares(whcol * s)):
        sc.ybar[0, t] = share
    both_of = product(st.wb_hh[...], *back)
    xb, lb = both_of[0:128], both_of[128:192]

    for k in reversed(range(LAYERS)):
        st.xb[k] = xb
        sb = fw * xb
        pair_h = keep_pair(st.hb, (k,), st.s1[k] * sb)
        st.t2[k] = st.t2[k] * sb
        both_of = product(st.wb_h[k], *pair_h)
        vb, ib = both_of[0:96], both_of[96:160]
        st.vb[k] = vb
        st.lb[k] = lb
        keep_pair(st.ob, (k,), fw * lb)
        for t, share in enumerate(shares(st.oo[k] * lb)):
            sc.ybar[0, t] += share
        run = lb + ib
        if k > 0:
            ahead = product(st.wb_two[k - 1], *split(run))
        for r in range(0, 32, 16):
            rs = slice(r, r + 16)
            sums = None
            for t in range(TILES):
                ts = tile(t)
                q = st.qq[k, rs, ts]
                vs = [vb[32 * l + r : 32 * l + r + 16, ts] for l in range(3)]
                qb = (
                    vs[0] * st.bb[k, 0, rs, :]
                    + vs[1] * st.vv[k, rs, ts]
                    + vs[2] * st.vv[k, 32 + r : 48 + r, ts]
                )
                if k < LAYERS - 1:
                    qb = qb + mix * st.pq[k + 1, 32 + r : 48 + r, ts] * st.qb[k + 1, rs, ts]
                st.qb[k, rs, ts] = qb
                back = [x * q for x in vs]
                terms = list(back)
                for m in range(1, 9):
                    terms.append(back[degree(m)] * geo[m, t : t + 1, :])
                    share = fold(back[degree(m)] * st.eh[k, m - 1, rs, :])
                    if k == LAYERS - 1 and r == 0:
                        sc.ybar[m, t] = share
                    else:
                        sc.ybar[m, t] += share
                sums = terms if sums is None else [x + y for x, y in zip(sums, terms, strict=True)]
            for n in range(11):
                st.cot[k, n, rs, :] = group_sum(sums[n])
        for r in range(0, 32, 8):
            rs = slice(r, r + 8)
            envs = [[st.env[j, m, rs, :] for m in range(9)] for j in range(k + 1)]
            cots = [st.cot[k, n, rs, :] for n in range(11)]
            back = atom_back(envs, (cots[:3], cots[3:]))
            for j in range(k + 1):
                for m in range(9):
                    if k == LAYERS - 1:
                        st.eb[j, m, rs, :] = back[j][m]
                    else:
                        st.eb[j, m, rs, :] += back[j][m]
        high = [[None] * TILES for _ in range(4)]
        low = [[None] * TILES for _ in range(4)]
        for r in range(0, 32, 16):
            rs = slice(r, r + 16)
            for t in range(TILES):
                ts = tile(t)
                p = st.pq[k, rs, ts]
                fs = geo[9, t : t + 1, :]
                a = p * fs
                ab = st.eb[k, 0, rs, :]
                for m in range(1, 9):
                    e = st.eb[k, m, rs, :]
                    ab = ab + geo[m, t : t + 1, :] * e
                    sc.ybar[m, t] += fold(a * e)
                st.ab[k, rs, ts] = ab
                sc.ybar[0, t] += fold((1.0 / math.sqrt(NEI)) * ab * p)
                qb = st.qb[k, rs, ts]
                if k > 0:
                    qb = mix * st.qq[k - 1, rs, ts] * qb
                high[r // 16][t], low[r // 16][t] = split(ab * fs)
                high[2 + r // 16][t], low[2 + r // 16][t] = split(qb)
        high, low = joined(high), joined(low)
        st.pb[k, 0:64, :] = high
        st.pb[k, 64:128, :] = low
        both_of = product(st.wb_p[k] if k > 0 else st.wb_p[k, 0:64, :], high, low)
        lb = run + both_of[0:64]
        if k > 0:
            xb = ahead + both_of[64:192]

    st.tz[...] = st.tz[...] * lb
    pb = product(sc.wb_emb[...], *keep_pair(st.zb, (), st.z1[...] * lb))[0:8]
    for t in range(TILES):
        part = pb[:, tile(t)]
        sc.ybar[0, t] += st.bes[0, :, tile(t)] * part
        sc.dbar[t] = geo[0, t : t + 1, :] * st.bes[1, :, tile(t)] * part

    bars = [jnp.sum(sc.ybar[m], axis=1) for m in range(9)]
    slopes = jax.vjp(geometry, *xyz)[1]((jnp.sum(sc.dbar[...], axis=1), bars[0], bars[1:]))

    for t in range(TILES):
        mine = rows_of((ranks, 128)) == owner[t : t + 1]
        parts = jnp.concatenate([jnp.where(mine, s[t : t + 1], 0.0) for s in slopes], 0)
        high = parts.astype(bf16).astype(f32)
        scatter[:, tile(t)] = jnp.concatenate([high, parts - high], 0).astype(bf16)
    sums = lax.dot_general(
        scatter[...], st.hot[...], (((1,), (1,)), ((), ())), preferred_element_type=f32
    )
    payload[...] = jnp.zeros(payload.shape, f32)
    for q in range(3):
        at = ranks * q
        total = jnp.broadcast_to(jnp.sum(slopes[q], axis=0, keepdims=True), (8, 128))
        total = group_sum(total)[0:1, 0:32]
        part = -(sums[at : at + ranks] + sums[3 * ranks + at : 4 * ranks + at])
        payload[at : at + ranks, 0:32] = part + jnp.where(
            rows_of((ranks, 32)) == me, total, 0.0
        )
    for q in range(3):
        payload[3 * ranks + q : 3 * ranks + q + 1, 0:32] = tgt[q]
    payload[3 * ranks + 3 : 3 * ranks + 4, 0:32] = (lanes((1, 32)) < live[0, 0]).astype(f32)

    def spread(j, carry):
        pay[j] = payload[...]
        return carry

    lax.fori_loop(0, ranks, spread, 0)


def cross(x, y):
    return lax.dot_general(x, y, (((1,), (1,)), ((), ())), preferred_element_type=f32)


def settle(full):
    rows, columns = full.shape[0] // 2, full.shape[1] // 2
    if columns == 64:
        return full[:rows] + (spin(full[:rows], 64) + full[rows:])
    return full[:rows, :columns] + (full[:rows, columns:] + full[rows:, :columns])


def pack(value, tmp):
    count = value.shape[0]
    tmp[0:count, :] = value
    even, odd = tmp[pl.ds(0, count // 2, stride=2), :], tmp[pl.ds(1, count // 2, stride=2), :]
    return jnp.where(lanes(even.shape) < 64, even, spin(odd, 64))


def second_kernel(ranks, axis, pick, live, got, *refs):
    st = Refs(STATE, refs[: len(STATE)])
    keep, give, forces, tm, aim = refs[len(STATE) : len(STATE) + 5]
    sc = Refs(SCRATCH_B, refs[len(STATE) + 5 :])
    me = lax.axis_index(axis)
    geo, gd = st.geo, sc.gd

    total = got[0, 0 : 3 * ranks, :]
    for j in range(1, ranks):
        total = total + got[j, 0 : 3 * ranks, :]
    for j in range(ranks):
        for q in range(4):
            tm[q * ranks + j : q * ranks + j + 1, :] = got[j, 3 * ranks + q : 3 * ranks + q + 1, :]
    mask = tm[3 * ranks : 4 * ranks, :]
    mine = rows_of((ranks, 128)) == me
    loss = jnp.zeros((ranks, 128), f32)
    centre = []
    for q in range(3):
        at = slice(q * ranks, q * ranks + ranks)
        error = mask * (total[at] - tm[at, :])
        loss = loss + jnp.where(mine, error * error, 0.0)
        forces[q] = jnp.sum(jnp.where(mine, total[at], 0.0), axis=0, keepdims=True)[:, 0:32]
        error = 2.0 * error
        aim[at, :] = error
        own = jnp.sum(jnp.where(mine, error, 0.0), axis=0, keepdims=True)
        centre.append(group_sum(jnp.broadcast_to(own, (8, 128)))[0:1])
    aims = aim[...]
    high = aims.astype(bf16).astype(f32)
    stacked = jnp.concatenate([high, aims - high], 0).astype(bf16)[:, 0:32]
    seen = jnp.dot(stacked, st.hot[...], preferred_element_type=f32)
    seen = seen[0 : 3 * ranks] + seen[3 * ranks :]
    for t in range(TILES):
        at_owner = rows_of((ranks, 128)) == st.owner[t : t + 1, :]
        for q in range(3):
            there = jnp.where(at_owner, seen[q * ranks : q * ranks + ranks, tile(t)], 0.0)
            sc.cdir[q, t : t + 1, :] = centre[q] - jnp.sum(there, axis=0, keepdims=True)

    xyz = tuple(st.place[q] for q in range(3))
    ways = tuple(sc.cdir[q] for q in range(3))
    _, (dd, fd, yd) = jax.jvp(geometry, xyz, ways)
    gd[0] = fd
    for m in range(8):
        gd[m + 1] = yd[m]
    gd[9] = fd * (1.0 / math.sqrt(NEI))
    tiles = []
    for t in range(TILES):
        b, slope = st.bes[0, :, tile(t)], st.bes[1, :, tile(t)]
        row = fd[t : t + 1] * b + (geo[0, t : t + 1, :] * dd[t : t + 1]) * slope
        tiles.append(jnp.concatenate([row, jnp.zeros((FEAT - 8, 128), f32)], 0))
    phid = keep_pair(sc.phid, (), jnp.concatenate(tiles, 1))
    fw, fdw = across(geo, 0), spread_rows(fd)

    zd = product(st.wf_emb[...], *phid)
    sc.zd[...] = zd
    latent = st.z1[...] * zd
    lat = keep_pair(sc.latd, (0,), latent)
    pqd = product(st.wf_first[...], *lat)
    sc.pqd[0] = pqd
    both_of = product(st.wf_lat[0, 0:192, :], *lat)
    base, ahead = both_of[0:128], both_of[128:192]

    for k in range(LAYERS):
        for r in range(0, 32, 16):
            rs = slice(r, r + 16)
            sums = None
            for t in range(TILES):
                ts = tile(t)
                p = st.pq[k, rs, ts]
                a = p * geo[9, t : t + 1, :]
                ad = pqd[rs, ts] * geo[9, t : t + 1, :] + p * gd[9, t : t + 1, :]
                terms = [ad] + [
                    ad * geo[m, t : t + 1, :] + a * gd[m, t : t + 1, :] for m in range(1, 9)
                ]
                sums = terms if sums is None else [x + y for x, y in zip(sums, terms, strict=True)]
            for m in range(9):
                sc.envd[k, m, rs, :] = group_sum(sums[m])
        for r in range(0, 32, 8):
            rs = slice(r, r + 8)
            envs = [[st.env[j, m, rs, :] for m in range(9)] for j in range(k + 1)]
            envds = [[sc.envd[j, m, rs, :] for m in range(9)] for j in range(k + 1)]
            _, (level, factors) = jax.jvp(atom_terms, (envs,), (envds,))
            for l in range(3):
                sc.bd[k, l, rs, :] = level[l]
            for m in range(8):
                sc.ehd[k, m, rs, :] = factors[m]
        high = [[None] * TILES for _ in range(6)]
        low = [[None] * TILES for _ in range(6)]
        for r in range(0, 32, 16):
            rs = slice(r, r + 16)
            ru = slice(32 + r, 48 + r)
            for t in range(TILES):
                ts = tile(t)
                qd = pqd[ru, ts]
                if k > 0:
                    qd = mix * (
                        sc.qd[k - 1, rs, ts] * st.pq[k, ru, ts] + st.qq[k - 1, rs, ts] * qd
                    )
                sc.qd[k, rs, ts] = qd
                q = st.qq[k, rs, ts]
                values = [st.bb[k, 0, rs, :], st.vv[k, rs, ts], st.vv[k, ru, ts]]
                moves = [sc.bd[k, l, rs, :] for l in range(3)]
                for m in range(1, 9):
                    l = degree(m)
                    moves[l] = (
                        moves[l]
                        + geo[m, t : t + 1, :] * sc.ehd[k, m - 1, rs, :]
                        + gd[m, t : t + 1, :] * st.eh[k, m - 1, rs, :]
                    )
                sc.vvd[k, rs, ts] = moves[1]
                sc.vvd[k, ru, ts] = moves[2]
                for l in range(3):
                    n = 2 * l + r // 16
                    high[n][t], low[n][t] = split(qd * values[l] + q * moves[l])
        high, low = joined(high), joined(low)
        sc.ivd[k, 0:96, :] = high
        sc.ivd[k, 96:192, :] = low
        hd = base + product(st.wf_io[k], high, low)
        sc.hd[k] = hd
        pair_s = keep_pair(sc.sd, (k,), st.s1[k] * hd)
        last = k == LAYERS - 1
        both_of = product(st.wf_s[k] if last else st.wf_s[k, 0:128, :], *pair_s)
        od, step = both_of[0:64], both_of[64:]
        if last:
            hhd = ahead + fdw * st.th[...] + fw * step
        else:
            pqd = ahead + fdw * st.ts[k] + fw * step
            sc.pqd[k + 1] = pqd
        latent = latent + fdw * st.oo[k] + fw * od
        lat = keep_pair(sc.latd, (k + 1,), latent)
        if not last:
            both_of = product(st.wf_lat[k + 1] if k + 2 == LAYERS else st.wf_lat[k + 1, 0:192, :], *lat)
            base, ahead = both_of[0:128], both_of[128:]

    whcol = jnp.concatenate([st.whcol[...]] * TILES, 1)
    back = keep_pair(sc.hht, (), whcol * (fdw * st.h1[...] + fw * st.h2[...] * hhd))
    both_of = product(st.wb_hh[...], *back)
    xt, lt = both_of[0:128], both_of[128:192]
    part = fw * st.h1[...] * hhd + fdw * st.sh[...]
    vector = part[:, tile(0)]
    for t in range(1, TILES):
        vector = vector + part[:, tile(t)]
    sc.grad[AT_VEC : AT_VEC + 1, :] = jnp.sum(vector.T, axis=0, keepdims=True)

    queue = []
    spare = [0]

    def work(count):
        for _ in range(min(count, len(queue))):
            queue.pop(0)()

    def single(rows, columns, first, second, finish):
        def begin():
            sc.part[0:rows, 0:columns] = cross(*first())

        def end():
            finish(settle(sc.part[0:rows, 0:columns] + cross(*second())))

        queue.extend((begin, end))

    def plain(at, count):
        def finish(value):
            sc.grad[at : at + count, :] = value

        return finish

    def packed(at, count):
        def finish(value):
            spare[0] = (spare[0] + 1) % 8
            sc.grad[at : at + count, :] = pack(value, sc.tmp.at[spare[0]])[0:count]

        return finish

    def middle(k):
        def finish(value):
            sc.mid[k] = value

        return finish

    def split_middle():
        parts = [split(sc.mid[k, 0:96, :]) for k in range(LAYERS)]
        ones = [product(st.wf_inv[k], *parts[k]) for k in range(LAYERS)]
        invs = []
        for k, (high, low) in enumerate(parts):
            inv = cross(jnp.concatenate([high, low, high], 1), st.wb_h[k, 96:160, :])
            invs.append(jnp.concatenate([inv, jnp.zeros((96, 64), f32)], 1))
        for k in range(LAYERS):
            at = AT_ONE + 64 * k
            sc.grad[at : at + 64, :] = sc.mid[k, 96:160, :] + ones[k]
            packed(AT_INV + 48 * k, 48)(invs[k])

    def stack(lat, inv):
        return jnp.concatenate([inv[0:96, :], lat[0:64, :], inv[96:192, :], lat[64:128, :]], 0)

    single(
        128,
        256,
        lambda: (sc.latd[3], st.hhb[...]),
        lambda: (st.latx[3], sc.hht[...]),
        plain(AT_HEAD, 64),
    )

    for k in reversed(range(LAYERS)):
        ht = (fdw * st.xb[k] + fw * xt) * st.s1[k] + st.t2[k] * sc.hd[k]
        pair_h = keep_pair(sc.ht, (k,), ht)
        both_of = product(st.wb_h[k], *pair_h)
        vt, it = both_of[0:96], both_of[96:160]
        keep_pair(sc.ot, (k,), fdw * st.lb[k] + fw * lt)
        run = lt + it
        if k > 0:
            ahead = product(st.wb_two[k - 1], *split(run))
        work(2)
        single(
            320,
            256,
            lambda k=k: (stack(sc.latd[k], sc.ivd[k]), st.hb[k]),
            lambda k=k: (stack(st.latx[k], st.ivx[k]), sc.ht[k]),
            middle(k),
        )
        single(
            256,
            128,
            lambda k=k: (sc.sd[k], st.ob[k]),
            lambda k=k: (st.sx[k], sc.ot[k]),
            packed(AT_TWO + 64 * k, 64),
        )
        for r in range(0, 32, 16):
            rs = slice(r, r + 16)
            ru = slice(32 + r, 48 + r)
            sums = None
            for t in range(TILES):
                ts = tile(t)
                q, qd = st.qq[k, rs, ts], sc.qd[k, rs, ts]
                ls = [slice(32 * l + r, 32 * l + r + 16) for l in range(3)]
                vb = [st.vb[k, s, ts] for s in ls]
                vs = [vt[s, ts] for s in ls]
                qt = (
                    vs[0] * st.bb[k, 0, rs, :]
                    + vs[1] * st.vv[k, rs, ts]
                    + vs[2] * st.vv[k, ru, ts]
                    + vb[0] * sc.bd[k, 0, rs, :]
                    + vb[1] * sc.vvd[k, rs, ts]
                    + vb[2] * sc.vvd[k, ru, ts]
                )
                if k < LAYERS - 1:
                    qt = qt + mix * (
                        sc.pqd[k + 1, ru, ts] * st.qb[k + 1, rs, ts]
                        + st.pq[k + 1, ru, ts] * sc.qt[k + 1, rs, ts]
                    )
                sc.qt[k, rs, ts] = qt
                back = [x * q for x in vb]
                twist = [x * q + y * qd for x, y in zip(vs, vb, strict=True)]
                terms = list(twist)
                for m in range(1, 9):
                    l = degree(m)
                    terms.append(twist[l] * geo[m, t : t + 1, :] + back[l] * gd[m, t : t + 1, :])
                sums = terms if sums is None else [x + y for x, y in zip(sums, terms, strict=True)]
            for n in range(11):
                sc.cott[n, rs, :] = group_sum(sums[n])
        work(1)
        for r in range(0, 32, 8):
            rs = slice(r, r + 8)
            envs = [[st.env[j, m, rs, :] for m in range(9)] for j in range(k + 1)]
            envds = [[sc.envd[j, m, rs, :] for m in range(9)] for j in range(k + 1)]
            cots = [st.cot[k, n, rs, :] for n in range(11)]
            cotts = [sc.cott[n, rs, :] for n in range(11)]
            _, back = jax.jvp(
                atom_back,
                (envs, (cots[:3], cots[3:])),
                (envds, (cotts[:3], cotts[3:])),
            )
            for j in range(k + 1):
                for m in range(9):
                    if k == LAYERS - 1:
                        sc.et[j, m, rs, :] = back[j][m]
                    else:
                        sc.et[j, m, rs, :] += back[j][m]
        work(1)
        high = [[None] * TILES for _ in range(4)]
        low = [[None] * TILES for _ in range(4)]
        for r in range(0, 32, 16):
            rs = slice(r, r + 16)
            for t in range(TILES):
                ts = tile(t)
                at = sc.et[k, 0, rs, :]
                for m in range(1, 9):
                    at = (
                        at
                        + geo[m, t : t + 1, :] * sc.et[k, m, rs, :]
                        + gd[m, t : t + 1, :] * st.eb[k, m, rs, :]
                    )
                qt = sc.qt[k, rs, ts]
                if k > 0:
                    qt = mix * (sc.qd[k - 1, rs, ts] * st.qb[k, rs, ts] + st.qq[k - 1, rs, ts] * qt)
                pt = at * geo[9, t : t + 1, :] + st.ab[k, rs, ts] * gd[9, t : t + 1, :]
                high[r // 16][t], low[r // 16][t] = split(pt)
                high[2 + r // 16][t], low[2 + r // 16][t] = split(qt)
        high, low = joined(high), joined(low)
        sc.pt[k, 0:64, :] = high
        sc.pt[k, 64:128, :] = low
        both_of = product(st.wb_p[k] if k > 0 else st.wb_p[k, 0:64, :], high, low)
        lt = run + both_of[0:64]
        if k > 0:
            xt = ahead + both_of[64:192]
        single(
            128,
            128,
            lambda k=k: (sc.latd[k], st.pb[k]),
            lambda k=k: (st.latx[k], sc.pt[k]),
            packed(AT_ENV + 32 * k, 32),
        )
        work(2)

    keep_pair(sc.zt, (), lt * st.z1[...] + st.tz[...] * sc.zd[...])
    single(
        2 * FEAT,
        128,
        lambda: (sc.phid[...], st.zb[...]),
        lambda: (st.phi[...], sc.zt[...]),
        packed(AT_EMBED, 9),
    )
    work(len(queue))
    split_middle()
    sc.grad[ROWS:PADDED, :] = jnp.zeros((PADDED - ROWS, 128), f32)
    lane = lanes((1, 128))
    amount = 3.0 * live[0, 0].astype(f32)
    sc.grad[ROWS : ROWS + 1, :] = jnp.where(
        lane == 0, jnp.sum(loss), jnp.where(lane == 1, amount, 0.0)
    )
    half = lax.axis_index(pick)
    keep[...] = sc.grad[pl.ds(pl.multiple_of(half * HALF, HALF), HALF), :]
    give[...] = sc.grad[pl.ds(pl.multiple_of((1 - half) * HALF, HALF), HALF), :]


def third_kernel(pick, mine, other, par, first, second, avg, *outs):
    loss, count, norm, new_first, new_second, new_par, low, new_avg = outs
    half = lax.axis_index(pick)
    lower = jnp.where(half == 0, mine[...], other[...])
    upper = jnp.where(half == 0, other[...], mine[...])
    last = ROWS - HALF
    scalars = upper[last : last + 1]
    loss[...] = scalars[:, 0:1]
    amount = scalars[:, 1:2]
    count[...] = amount
    squares = jnp.sum(lower * lower, keepdims=True) + jnp.sum(
        upper[0:last] * upper[0:last], keepdims=True
    )
    length = jnp.sqrt(squares) / amount
    norm[...] = length
    factor = (clip_level / jnp.maximum(length, clip_level)) / amount
    for start, stop, value in ((0, HALF, lower), (HALF, ROWS, upper[0:last])):
        rows = slice(start, stop)
        gradient = value * factor
        one = beta_one * first[rows, :] + (1.0 - beta_one) * gradient
        two = beta_two * second[rows, :] + (1.0 - beta_two) * gradient * gradient
        fixed_one = one / (1.0 - beta_one**STEP)
        fixed_two = two / (1.0 - beta_two**STEP)
        weights = par[rows, :]
        weights = weights - learn_rate * (
            fixed_one / (jnp.sqrt(fixed_two) + epsilon_adam) + decay_rate * weights
        )
        new_first[rows, :] = one
        new_second[rows, :] = two
        new_par[rows, :] = weights
        low[rows, :] = weights.astype(bf16)
        new_avg[rows, :] = average_keep * avg[rows, :] + (1.0 - average_keep) * weights


VMEM = pl.BlockSpec(memory_space=pltpu.VMEM)
HBM = pl.BlockSpec(memory_space=pltpu.HBM)
SMEM = pl.BlockSpec(memory_space=pltpu.SMEM)


def scratch(entries):
    return [pltpu.VMEM(shape, dtype) for _, shape, dtype in entries]


def local(
    ranks,
    params,
    first_moment,
    second_moment,
    average,
    edge_vectors,
    owner_rank,
    neighbour_local,
    centre_species,
    neighbour_species,
    live_atoms,
    target_forces,
):
    shape = jax.ShapeDtypeStruct
    flat = (ROWS, 128)
    par = params.reshape(flat)
    live = live_atoms.reshape(1, 1)
    tall = 3 * ranks + 8
    state = [shape(s, t) for _, s, t in STATE]
    sources = (
        edge_vectors.reshape(3, 8, 128),
        owner_rank.reshape(8, 128),
        neighbour_local.reshape(8, 128),
        neighbour_species.reshape(8, 128),
        centre_species.reshape(1, ATOMS),
        target_forces.reshape(3, 1, ATOMS),
        par,
    )
    pay, *kept = pl.pallas_call(
        functools.partial(first_kernel, ranks, "atoms"),
        out_shape=[shape((ranks, tall, 128), f32), *state],
        in_specs=[SMEM] + [HBM] * 7,
        out_specs=[VMEM] * (1 + len(state)),
        scratch_shapes=[
            *[pltpu.VMEM(x.shape, x.dtype) for x in sources],
            pltpu.SemaphoreType.DMA((7,)),
            pltpu.VMEM((tall, 128), f32),
            pltpu.VMEM((6 * ranks, EDGES), bf16),
            *scratch(SCRATCH_A),
        ],
        compiler_params=pltpu.CompilerParams(vmem_limit_bytes=16 * 2**20),
        name="forward",
    )(live, *[pltpu.with_memory_space_constraint(x, pltpu.HBM) for x in sources])
    got = lax.all_to_all(pay, "atoms", split_axis=0, concat_axis=0, tiled=True)
    keep, give, forces = pl.pallas_call(
        functools.partial(second_kernel, ranks, "atoms", "low"),
        out_shape=[shape((HALF, 128), f32), shape((HALF, 128), f32), shape((3, 1, ATOMS), f32)],
        in_specs=[SMEM, VMEM] + [VMEM] * len(state),
        out_specs=[VMEM] * 3,
        scratch_shapes=[
            pltpu.VMEM((4 * ranks, 128), f32),
            pltpu.VMEM((3 * ranks, 128), f32),
            *scratch(SCRATCH_B),
        ],
        compiler_params=pltpu.CompilerParams(vmem_limit_bytes=20 * 2**20),
        name="gradient",
    )(live, got, *kept)
    swap = [(0, 1), (1, 0)]
    axes, size = ("atoms", "high"), ranks * 2
    held = keep + lax.ppermute(give, "low", swap)
    pieces = size * 8 * -(-HALF // (8 * size))
    held = jnp.pad(held, ((0, pieces - HALF), (0, 0))).reshape(size, pieces // size, 128)
    summed = lax.all_to_all(held, axes, split_axis=0, concat_axis=0, tiled=True).sum(0)
    summed = jnp.broadcast_to(summed[None], (size, *summed.shape))
    mine = lax.all_to_all(summed, axes, split_axis=0, concat_axis=0, tiled=True)
    mine = mine.reshape(pieces, 128)[:HALF]
    other = lax.ppermute(mine, "low", swap)
    one, vec = shape((1, 1), f32), shape(flat, f32)
    loss, count, norm, new_first, new_second, new_params, low, new_average = pl.pallas_call(
        functools.partial(third_kernel, "low"),
        out_shape=[one, one, one, vec, vec, vec, shape(flat, bf16), vec],
        in_specs=[VMEM] * 6,
        out_specs=[VMEM] * 8,
        compiler_params=pltpu.CompilerParams(vmem_limit_bytes=16 * 2**20),
        name="update",
    )(
        mine,
        other,
        par,
        first_moment.reshape(flat),
        second_moment.reshape(flat),
        average.reshape(flat),
    )
    return (
        loss.reshape(()),
        count.reshape(()),
        norm.reshape(()),
        forces,
        new_first.reshape(-1),
        new_second.reshape(-1),
        new_params.reshape(-1),
        low.reshape(-1),
        new_average.reshape(-1),
    )


def solution(mesh):
    ranks, groups = mesh.shape["atoms"], mesh.shape["grp"]
    fine = Mesh(mesh.devices.reshape(ranks, groups // 2, 2), ("atoms", "high", "low"))
    grp = ("high", "low")
    in_specs = (
        P(),
        P(),
        P(),
        P(),
        P(None, grp, "atoms"),
        P(grp, "atoms", None),
        P(grp, "atoms"),
        P(grp, "atoms"),
        P(grp, "atoms"),
        P(grp, "atoms"),
        P(None, grp, "atoms"),
    )
    out_specs = (P(), P(), P(), P(None, grp, "atoms"), P(), P(), P(), P(), P())
    return jax.shard_map(
        functools.partial(local, ranks),
        mesh=fine,
        in_specs=in_specs,
        out_specs=out_specs,
        check_vma=False,
    )
```

```python
import functools
import math

import jax
import jax.numpy as jnp
from jax import lax
from jax.experimental import pallas as pl
from jax.experimental.pallas import tpu as pltpu
from jax.sharding import Mesh
from jax.sharding import PartitionSpec as P

LATENT = 64
UNITS = 128
CHANNELS = 32
BASES = 8
SPECIES = 5
LAYERS = 3
STEP = 10
NEI = 32
NPARAM = 89344

cutoff_radius = 5.0
clip_level = 0.01
learn_rate = 0.1
beta_one = 0.9
beta_two = 0.999
epsilon_adam = 1e-08
decay_rate = 0.01
average_keep = 0.99
mix = 0.7071

f32 = jnp.float32
bf16 = jnp.bfloat16

ATOMS = 32
EDGES = 1024
TILES = 8
FEAT = 32

AT_EMBED = 0
AT_ENV = 9
AT_INV = AT_ENV + 96
AT_ONE = AT_INV + 144
AT_TWO = AT_ONE + 192
AT_HEAD = AT_TWO + 192
AT_VEC = AT_HEAD + 64
ROWS = AT_VEC + 1
PADDED = 768
HALF = PADDED // 2

STATE = [
    ("wf_emb", (LATENT, 3 * FEAT), bf16),
    ("wf_first", (64, 192), bf16),
    ("wf_lat", (3, 256, 192), bf16),
    ("wf_io", (3, 128, 288), bf16),
    ("wf_s", (3, 192, 384), bf16),
    ("wf_inv", (3, 64, 288), bf16),
    ("wb_hh", (192, 384), bf16),
    ("wb_h", (3, 160, 384), bf16),
    ("wb_p", (3, 192, 192), bf16),
    ("wb_two", (3, 128, 192), bf16),
    ("whcol", (128, 128), f32),
    ("place", (3, 8, 128), f32),
    ("owner", (8, 128), jnp.int32),
    ("hot", (ATOMS, EDGES), bf16),
    ("geo", (10, 8, 128), f32),
    ("bes", (2, BASES, EDGES), f32),
    ("phi", (2 * FEAT, EDGES), bf16),
    ("latx", (4, 128, EDGES), bf16),
    ("pq", (3, 64, EDGES), f32),
    ("vv", (3, 64, EDGES), f32),
    ("ivx", (3, 192, EDGES), bf16),
    ("sx", (3, 256, EDGES), bf16),
    ("s1", (3, 128, EDGES), f32),
    ("t2", (3, 128, EDGES), f32),
    ("oo", (3, 64, EDGES), f32),
    ("ts", (2, 64, EDGES), f32),
    ("th", (128, EDGES), f32),
    ("lb", (3, 64, EDGES), f32),
    ("ob", (3, 128, EDGES), bf16),
    ("hb", (3, 256, EDGES), bf16),
    ("xb", (3, 128, EDGES), f32),
    ("vb", (3, 96, EDGES), f32),
    ("ab", (3, 32, EDGES), f32),
    ("pb", (3, 128, EDGES), bf16),
    ("qq", (3, 32, EDGES), f32),
    ("qb", (3, 32, EDGES), f32),
    ("z1", (64, EDGES), f32),
    ("tz", (64, EDGES), f32),
    ("zb", (128, EDGES), bf16),
    ("sh", (128, EDGES), f32),
    ("h1", (128, EDGES), f32),
    ("h2", (128, EDGES), f32),
    ("hhb", (256, EDGES), bf16),
    ("env", (3, 9, 32, 128), f32),
    ("eh", (3, 8, 32, 128), f32),
    ("bb", (3, 3, 32, 128), f32),
    ("eb", (3, 9, 32, 128), f32),
    ("cot", (3, 11, 32, 128), f32),
]

SCRATCH_A = [
    ("tmp", (11, 128, 128), f32),
    ("wb_emb", (16, 192), bf16),
    ("ybar", (9, 8, 8, 128), f32),
    ("dbar", (8, 8, 128), f32),
]

SCRATCH_B = [
    ("tmp", (8, 128, 128), f32),
    ("part", (320, 256), f32),
    ("mid", (3, 160, 128), f32),
    ("cdir", (3, 8, 128), f32),
    ("gd", (10, 8, 128), f32),
    ("phid", (2 * FEAT, EDGES), bf16),
    ("zd", (64, EDGES), f32),
    ("latd", (4, 128, EDGES), bf16),
    ("pqd", (3, 64, EDGES), f32),
    ("vvd", (3, 64, EDGES), f32),
    ("qd", (3, 32, EDGES), f32),
    ("ivd", (3, 192, EDGES), bf16),
    ("hd", (3, 128, EDGES), f32),
    ("sd", (3, 256, EDGES), bf16),
    ("envd", (3, 9, 32, 128), f32),
    ("ehd", (3, 8, 32, 128), f32),
    ("bd", (3, 3, 32, 128), f32),
    ("hht", (256, EDGES), bf16),
    ("ot", (3, 128, EDGES), bf16),
    ("ht", (3, 256, EDGES), bf16),
    ("qt", (3, 32, EDGES), f32),
    ("pt", (3, 128, EDGES), bf16),
    ("zt", (128, EDGES), bf16),
    ("et", (3, 9, 32, 128), f32),
    ("cott", (11, 32, 128), f32),
    ("grad", (PADDED, 128), f32),
]


class Refs:
    def __init__(self, entries, refs):
        for (name, _, _), ref in zip(entries, refs, strict=True):
            setattr(self, name, ref)


def split(x):
    high = x.astype(bf16)
    return high, (x - high.astype(f32)).astype(bf16)


def product(weights, high, low):
    return jnp.dot(
        weights, jnp.concatenate([high, low, high], 0), preferred_element_type=f32
    )


def put(ref, rows, columns, value, lead=()):
    high, low = split(value)
    half = ref.shape[-2] // 2
    ref[(*lead, slice(rows, rows + value.shape[0]), columns)] = high
    ref[(*lead, slice(half + rows, half + rows + value.shape[0]), columns)] = low
    return high, low


def pair(ref, columns, lead=()):
    half = ref.shape[-2] // 2
    return ref[(*lead, slice(0, half), columns)], ref[(*lead, slice(half, 2 * half), columns)]


def spin(x, amount):
    return pltpu.roll(x, amount % 128, 1)


def group_sum(x):
    x = x + spin(x, 64)
    return x + spin(x, 32)


def lanes(shape):
    return lax.broadcasted_iota(jnp.int32, shape, len(shape) - 1)


def rows_of(shape):
    return lax.broadcasted_iota(jnp.int32, shape, len(shape) - 2)


def silu_parts(h):
    gate = 1.0 / (1.0 + jnp.exp(-h))
    slope = gate * (1.0 - gate)
    return h * gate, gate + h * slope, slope * (2.0 + h * (1.0 - 2.0 * gate))


def geometry(x, y, z):
    d = jnp.sqrt(x * x + y * y + z * z)
    u, v, w = x / d, y / d, z / d
    s = d / cutoff_radius
    s2 = s * s
    s6 = s2 * s2 * s2
    f = 1.0 - 28.0 * s6 + 48.0 * (s6 * s) - 21.0 * (s6 * s2)
    r3, r5, r15 = math.sqrt(3.0), math.sqrt(5.0), math.sqrt(15.0)
    harmonics = [
        r3 * u,
        r3 * v,
        r3 * w,
        r15 * u * v,
        r15 * v * w,
        0.5 * r5 * (3.0 * w * w - 1.0),
        r15 * u * w,
        0.5 * r15 * (u * u - v * v),
    ]
    return d, f, harmonics


def dots(left, right):
    total = left[0] * right[0]
    for a, b in zip(left[1:], right[1:], strict=True):
        total = total + a * b
    return total


def degree(m):
    return 1 if m <= 3 else 2


def atom_terms(envs):
    if len(envs) == 1:
        (one,) = envs
        zero = jnp.zeros_like(one[0])
        return [one[0], zero, zero], one[1:]
    if len(envs) == 2:
        one, two = envs
        return (
            [2.0 * one[0] * two[0], dots(one[1:4], two[1:4]), dots(one[4:], two[4:])],
            [one[0] * two[m] for m in range(1, 9)],
        )
    one, two, three = envs
    both = one[0] * two[0]
    twice = 2.0 * one[0]
    part = [two[0] * one[m] + twice * two[m] for m in range(1, 9)]
    return (
        [4.0 * both * three[0], dots(part[:3], three[1:4]), dots(part[3:], three[4:])],
        [both * three[m] for m in range(1, 9)],
    )


def atom_back(envs, cots):
    return jax.vjp(atom_terms, envs)[1](cots)[0]


def tile(t):
    return slice(128 * t, 128 * t + 128)


def fold(value):
    total = value[0:8]
    for r in range(8, value.shape[0], 8):
        total = total + value[r : r + 8]
    return total


def unpack(packed, count, tmp):
    half = count // 2
    tmp[pl.ds(0, half, stride=2), :] = packed
    tmp[pl.ds(1, half, stride=2), :] = spin(packed, 64)
    value = tmp[0:count, :]
    return jnp.where(lanes(value.shape) < 64, value, spin(value, 64))


def store_64(ref, lead, doubled, at=0):
    high, low = split(doubled)
    rows = slice(at, at + doubled.shape[0])
    ref[(*lead, rows, slice(0, 128))] = high
    ref[(*lead, rows, slice(128, 192))] = low[:, 0:64]


def store_128(ref, lead, value, at=0):
    high, low = split(value)
    rows = slice(at, at + value.shape[0])
    ref[(*lead, rows, slice(0, 128))] = high
    ref[(*lead, rows, slice(128, 256))] = high
    ref[(*lead, rows, slice(256, 384))] = low


def store_96(ref, lead, value):
    high = value.astype(bf16).astype(f32)
    low = value - high
    high_on, low_on = spin(high, 96), spin(low, 64)
    lane = lanes(value.shape)
    ref[(*lead, slice(None), slice(0, 128))] = jnp.where(lane < 96, high, high_on).astype(bf16)
    ref[(*lead, slice(None), slice(128, 256))] = jnp.where(lane < 64, high_on, low_on).astype(bf16)
    ref[(*lead, slice(None), slice(256, 288))] = low_on[:, 0:32].astype(bf16)


def across(ref, index):
    return jnp.concatenate([ref[index, t : t + 1, :] for t in range(TILES)], 1)


def spread_rows(value):
    return jnp.concatenate([value[t : t + 1] for t in range(TILES)], 1)


def joined(grid):
    return jnp.concatenate([jnp.concatenate(row, 1) for row in grid], 0)


def keep_pair(ref, lead, value):
    high, low = split(value)
    half = value.shape[0]
    ref[(*lead, slice(0, half), slice(None))] = high
    ref[(*lead, slice(half, 2 * half), slice(None))] = low
    return high, low


def both(ref, lead=()):
    half = ref.shape[-2] // 2
    return ref[(*lead, slice(0, half), slice(None))], ref[(*lead, slice(half, 2 * half), slice(None))]


def shares(value):
    total = fold(value)
    return [total[:, tile(t)] for t in range(TILES)]


def tmp_rows(w, start):
    return jnp.concatenate([w[start : start + 2], jnp.zeros((14, 128), f32)], 0)


def weights_product(left, right):
    high, low = split(right)
    return product(left, high, low)


def prepare(par, st, sc):
    def turned(value):
        return value.T

    spare = iter(range(11))

    def doubled(at, count):
        return unpack(par[at : at + count // 2, :], count, sc.tmp.at[next(spare)])

    w = doubled(AT_EMBED, 18)
    w = jnp.concatenate([w[0:16], tmp_rows(w, 16)], 0)
    store_64(sc.wb_emb, (), w[0:16])
    high = w.astype(bf16).astype(f32)
    low = w - high
    turn = jnp.concatenate([high, high, low, jnp.zeros((32, 128), f32)], 0).T[0:64]
    st.wf_emb[...] = turn[:, 0 : 3 * FEAT].astype(bf16)
    envs = []
    for k in range(LAYERS):
        w = doubled(AT_ENV + 32 * k, 64)
        envs.append(w)
        store_64(st.wb_p, (k,), w)
        turn = jnp.concatenate([w, w], 0).T[0:64]
        if k == 0:
            store_64(st.wf_first, (), turn)
        else:
            store_64(st.wf_lat, (k - 1,), turn, 128)
    head = par[AT_HEAD : AT_HEAD + 64, :]
    store_128(st.wb_hh, (), head, 128)
    store_64(st.wf_lat, (2,), jnp.concatenate([head, head], 0).T, 128)
    for k in range(LAYERS):
        one = par[AT_ONE + 64 * k : AT_ONE + 64 * k + 64, :]
        store_128(st.wb_h, (k,), one, 96)
        store_64(st.wf_lat, (k,), jnp.concatenate([one, one], 0).T)
        w = doubled(AT_INV + 48 * k, 96)
        store_96(st.wf_inv, (k,), jnp.concatenate([w, jnp.zeros((32, 128), f32)], 0).T[0:64])
        high, low = split(w)
        w = weights_product(jnp.concatenate([high, low[:, 0:64]], 1), one)
        store_128(st.wb_h, (k,), w)
        store_96(st.wf_io, (k,), jnp.concatenate([w, jnp.zeros((32, 128), f32)], 0).T)
        w = doubled(AT_TWO + 64 * k, 128)
        high, low = split(w)
        left = jnp.concatenate([high, low[:, 0:64]], 1)
        st.wb_two[k] = left
        store_128(st.wf_s, (k,), w.T[0:64])
        if k < LAYERS - 1:
            w = weights_product(left, envs[k + 1])
            store_64(st.wb_p, (k + 1,), w, 64)
            store_128(st.wf_s, (k,), w.T[0:64], 64)
        else:
            w = weights_product(left, head)
            store_128(st.wb_hh, (), w)
            store_128(st.wf_s, (k,), w.T, 64)
    st.whcol[...] = jnp.broadcast_to(par[AT_VEC : AT_VEC + 1, :], (128, 128)).T


def sine_parts(turns):
    whole = jnp.round(turns)
    rest = (turns - whole) * math.pi
    odd = whole - 2.0 * jnp.floor(whole * 0.5)
    sign = 1.0 - 2.0 * odd
    r2 = rest * rest
    sine = 0.0
    for n in (13, 11, 9, 7, 5, 3, 1):
        sine = sine * r2 + (-1.0) ** (n // 2) / math.factorial(n)
    cosine = 0.0
    for n in (14, 12, 10, 8, 6, 4, 2, 0):
        cosine = cosine * r2 + (-1.0) ** (n // 2) / math.factorial(n)
    return sign * rest * sine, sign * cosine


def first_kernel(ranks, axis, live, *refs):
    sources = refs[0:7]
    pay = refs[7]
    st = Refs(STATE, refs[8 : 8 + len(STATE)])
    rest = refs[8 + len(STATE) :]
    vec, own, loc, nsp, cen, tgt, par = rest[0:7]
    sems, payload, scatter = rest[7:10]
    sc = Refs(SCRATCH_A, rest[10:])
    me = lax.axis_index(axis)
    copies = [
        pltpu.make_async_copy(source, target, sems.at[n])
        for n, (source, target) in enumerate(zip(sources, rest[0:7], strict=True))
    ]
    for copy in copies:
        copy.start()
    for copy in copies[:6]:
        copy.wait()

    order = sc.tmp.at[10]
    code = ((own[...] * 32 + loc[...]) * 8 + nsp[...]).astype(f32)
    for q, value in enumerate((vec[0], vec[1], vec[2], code)):
        for a in range(4):
            order[pl.ds(32 * q + a, 8, stride=4), :] = spin(value, -32 * a)
    turned = order[...].T
    lane = lanes((8, 128))

    def picked(q):
        out = spin(turned[0:8], -32 * q)
        for g in range(1, 4):
            out = jnp.where(lane // 32 == g, spin(turned[8 * g : 8 * g + 8], 32 * (g - q)), out)
        return out

    xyz = [picked(q) for q in range(3)]
    codes = picked(3).astype(jnp.int32)
    for q in range(3):
        st.place[q] = xyz[q]
    local = lax.shift_right_logical(codes, 3) & 31
    owner = lax.shift_right_logical(codes, 8)
    kind = codes & 7
    st.owner[...] = owner
    sc.dbar[0] = jnp.zeros((8, 128), f32)
    sc.dbar[0, 0:1, 0:32] = cen[...].astype(f32)
    centre_kind = group_sum(sc.dbar[0])[0:1].astype(jnp.int32)

    d, f, harmonics = geometry(*xyz)
    geo = st.geo
    geo[0] = f
    for m in range(8):
        geo[m + 1] = harmonics[m]
    geo[9] = f * (1.0 / math.sqrt(NEI))

    orders = (rows_of((8, 128)) + 1).astype(f32)
    inv_d = 1.0 / d
    scale = math.sqrt(2.0 / cutoff_radius)
    tiles = []
    for t in range(TILES):
        row_inv = inv_d[t : t + 1]
        sine, cosine = sine_parts(orders * (d[t : t + 1] / cutoff_radius))
        b = (scale * sine) * row_inv
        slope = (scale * math.pi / cutoff_radius) * orders * cosine * row_inv - b * row_inv
        st.bes[0, :, tile(t)] = b
        st.bes[1, :, tile(t)] = slope
        row = rows_of((FEAT - 8, 128)) + 8
        hot = (row == centre_kind + 8) | (row == kind[t : t + 1] + 13)
        tiles.append(jnp.concatenate([b * f[t : t + 1], hot.astype(f32)], 0))
        st.hot[:, tile(t)] = (rows_of((ATOMS, 128)) == local[t : t + 1]).astype(f32).astype(bf16)
    phi = keep_pair(st.phi, (), jnp.concatenate(tiles, 1))

    copies[6].wait()
    prepare(par, st, sc)
    fw = spread_rows(f)

    s, s1, s2 = silu_parts(product(st.wf_emb[...], *phi))
    st.z1[...] = s1
    st.tz[...] = s2
    latent = s
    lat = keep_pair(st.latx, (0,), s)
    pq = product(st.wf_first[...], *lat)
    st.pq[0] = pq
    both_of = product(st.wf_lat[0, 0:192, :], *lat)
    base, ahead = both_of[0:128], both_of[128:192]

    for k in range(LAYERS):
        for r in range(0, 32, 16):
            rs = slice(r, r + 16)
            sums = None
            for t in range(TILES):
                a = pq[rs, tile(t)] * geo[9, t : t + 1, :]
                terms = [a] + [a * geo[m, t : t + 1, :] for m in range(1, 9)]
                sums = terms if sums is None else [x + y for x, y in zip(sums, terms, strict=True)]
            for m in range(9):
                st.env[k, m, rs, :] = group_sum(sums[m])
        for r in range(0, 32, 8):
            rs = slice(r, r + 8)
            envs = [[st.env[j, m, rs, :] for m in range(9)] for j in range(k + 1)]
            level, factors = atom_terms(envs)
            for l in range(3):
                st.bb[k, l, rs, :] = level[l]
            for m in range(8):
                st.eh[k, m, rs, :] = factors[m]
        high = [[None] * TILES for _ in range(6)]
        low = [[None] * TILES for _ in range(6)]
        for r in range(0, 32, 16):
            rs = slice(r, r + 16)
            for t in range(TILES):
                ts = tile(t)
                q = pq[32 + r : 48 + r, ts]
                if k > 0:
                    q = mix * st.qq[k - 1, rs, ts] * q
                st.qq[k, rs, ts] = q
                values = [st.bb[k, l, rs, :] for l in range(3)]
                for m in range(1, 9):
                    l = degree(m)
                    values[l] = values[l] + geo[m, t : t + 1, :] * st.eh[k, m - 1, rs, :]
                st.vv[k, rs, ts] = values[1]
                st.vv[k, 32 + r : 48 + r, ts] = values[2]
                for l in range(3):
                    n = 2 * l + r // 16
                    high[n][t], low[n][t] = split(q * values[l])
        high, low = joined(high), joined(low)
        st.ivx[k, 0:96, :] = high
        st.ivx[k, 96:192, :] = low
        h = base + product(st.wf_io[k], high, low)
        s, s1, s2 = silu_parts(h)
        st.s1[k] = s1
        st.t2[k] = s2
        pair_s = keep_pair(st.sx, (k,), s)
        last = k == LAYERS - 1
        both_of = product(st.wf_s[k] if last else st.wf_s[k, 0:128, :], *pair_s)
        o, step = both_of[0:64], both_of[64:]
        if last:
            st.th[...] = step
            hh = ahead + fw * step
        else:
            st.ts[k] = step
            pq = ahead + fw * step
            st.pq[k + 1] = pq
        st.oo[k] = o
        latent = latent + fw * o
        lat = keep_pair(st.latx, (k + 1,), latent)
        if not last:
            both_of = product(st.wf_lat[k + 1] if k + 2 == LAYERS else st.wf_lat[k + 1, 0:192, :], *lat)
            base, ahead = both_of[0:128], both_of[128:]

    s, s1, s2 = silu_parts(hh)
    st.sh[...] = s
    st.h1[...] = s1
    st.h2[...] = s2
    whcol = jnp.concatenate([st.whcol[...]] * TILES, 1)
    back = keep_pair(st.hhb, (), fw * whcol * s1)
    for t, share in enumerate(shares(whcol * s)):
        sc.ybar[0, t] = share
    both_of = product(st.wb_hh[...], *back)
    xb, lb = both_of[0:128], both_of[128:192]

    for k in reversed(range(LAYERS)):
        st.xb[k] = xb
        sb = fw * xb
        pair_h = keep_pair(st.hb, (k,), st.s1[k] * sb)
        st.t2[k] = st.t2[k] * sb
        both_of = product(st.wb_h[k], *pair_h)
        vb, ib = both_of[0:96], both_of[96:160]
        st.vb[k] = vb
        st.lb[k] = lb
        keep_pair(st.ob, (k,), fw * lb)
        for t, share in enumerate(shares(st.oo[k] * lb)):
            sc.ybar[0, t] += share
        run = lb + ib
        if k > 0:
            ahead = product(st.wb_two[k - 1], *split(run))
        for r in range(0, 32, 16):
            rs = slice(r, r + 16)
            sums = None
            for t in range(TILES):
                ts = tile(t)
                q = st.qq[k, rs, ts]
                vs = [vb[32 * l + r : 32 * l + r + 16, ts] for l in range(3)]
                qb = (
                    vs[0] * st.bb[k, 0, rs, :]
                    + vs[1] * st.vv[k, rs, ts]
                    + vs[2] * st.vv[k, 32 + r : 48 + r, ts]
                )
                if k < LAYERS - 1:
                    qb = qb + mix * st.pq[k + 1, 32 + r : 48 + r, ts] * st.qb[k + 1, rs, ts]
                st.qb[k, rs, ts] = qb
                back = [x * q for x in vs]
                terms = list(back)
                for m in range(1, 9):
                    terms.append(back[degree(m)] * geo[m, t : t + 1, :])
                    share = fold(back[degree(m)] * st.eh[k, m - 1, rs, :])
                    if k == LAYERS - 1 and r == 0:
                        sc.ybar[m, t] = share
                    else:
                        sc.ybar[m, t] += share
                sums = terms if sums is None else [x + y for x, y in zip(sums, terms, strict=True)]
            for n in range(11):
                st.cot[k, n, rs, :] = group_sum(sums[n])
        for r in range(0, 32, 8):
            rs = slice(r, r + 8)
            envs = [[st.env[j, m, rs, :] for m in range(9)] for j in range(k + 1)]
            cots = [st.cot[k, n, rs, :] for n in range(11)]
            back = atom_back(envs, (cots[:3], cots[3:]))
            for j in range(k + 1):
                for m in range(9):
                    if k == LAYERS - 1:
                        st.eb[j, m, rs, :] = back[j][m]
                    else:
                        st.eb[j, m, rs, :] += back[j][m]
        high = [[None] * TILES for _ in range(4)]
        low = [[None] * TILES for _ in range(4)]
        for r in range(0, 32, 16):
            rs = slice(r, r + 16)
            for t in range(TILES):
                ts = tile(t)
                p = st.pq[k, rs, ts]
                fs = geo[9, t : t + 1, :]
                a = p * fs
                ab = st.eb[k, 0, rs, :]
                for m in range(1, 9):
                    e = st.eb[k, m, rs, :]
                    ab = ab + geo[m, t : t + 1, :] * e
                    sc.ybar[m, t] += fold(a * e)
                st.ab[k, rs, ts] = ab
                sc.ybar[0, t] += fold((1.0 / math.sqrt(NEI)) * ab * p)
                qb = st.qb[k, rs, ts]
                if k > 0:
                    qb = mix * st.qq[k - 1, rs, ts] * qb
                high[r // 16][t], low[r // 16][t] = split(ab * fs)
                high[2 + r // 16][t], low[2 + r // 16][t] = split(qb)
        high, low = joined(high), joined(low)
        st.pb[k, 0:64, :] = high
        st.pb[k, 64:128, :] = low
        both_of = product(st.wb_p[k] if k > 0 else st.wb_p[k, 0:64, :], high, low)
        lb = run + both_of[0:64]
        if k > 0:
            xb = ahead + both_of[64:192]

    st.tz[...] = st.tz[...] * lb
    pb = product(sc.wb_emb[...], *keep_pair(st.zb, (), st.z1[...] * lb))[0:8]
    for t in range(TILES):
        part = pb[:, tile(t)]
        sc.ybar[0, t] += st.bes[0, :, tile(t)] * part
        sc.dbar[t] = geo[0, t : t + 1, :] * st.bes[1, :, tile(t)] * part

    bars = [jnp.sum(sc.ybar[m], axis=1) for m in range(9)]
    slopes = jax.vjp(geometry, *xyz)[1]((jnp.sum(sc.dbar[...], axis=1), bars[0], bars[1:]))

    for t in range(TILES):
        mine = rows_of((ranks, 128)) == owner[t : t + 1]
        parts = jnp.concatenate([jnp.where(mine, s[t : t + 1], 0.0) for s in slopes], 0)
        high = parts.astype(bf16).astype(f32)
        scatter[:, tile(t)] = jnp.concatenate([high, parts - high], 0).astype(bf16)
    sums = lax.dot_general(
        scatter[...], st.hot[...], (((1,), (1,)), ((), ())), preferred_element_type=f32
    )
    payload[...] = jnp.zeros(payload.shape, f32)
    for q in range(3):
        at = ranks * q
        total = jnp.broadcast_to(jnp.sum(slopes[q], axis=0, keepdims=True), (8, 128))
        total = group_sum(total)[0:1, 0:32]
        part = -(sums[at : at + ranks] + sums[3 * ranks + at : 4 * ranks + at])
        payload[at : at + ranks, 0:32] = part + jnp.where(
            rows_of((ranks, 32)) == me, total, 0.0
        )
    for q in range(3):
        payload[3 * ranks + q : 3 * ranks + q + 1, 0:32] = tgt[q]
    payload[3 * ranks + 3 : 3 * ranks + 4, 0:32] = (lanes((1, 32)) < live[0, 0]).astype(f32)

    deep = pay.shape[1]
    packed = payload[0:deep, :]
    for g in range(1, 4):
        packed = packed + spin(payload[g * deep : g * deep + deep, :], 32 * g)
    payload[0:deep, :] = packed

    def spread(j, carry):
        pay[j] = payload[0:deep, :]
        return carry

    lax.fori_loop(0, ranks, spread, 0)


def cross(x, y):
    return lax.dot_general(x, y, (((1,), (1,)), ((), ())), preferred_element_type=f32)


def settle(full):
    rows, columns = full.shape[0] // 2, full.shape[1] // 2
    if columns == 64:
        return full[:rows] + (spin(full[:rows], 64) + full[rows:])
    return full[:rows, :columns] + (full[:rows, columns:] + full[rows:, :columns])


def pack(value, tmp):
    count = value.shape[0]
    tmp[0:count, :] = value
    even, odd = tmp[pl.ds(0, count // 2, stride=2), :], tmp[pl.ds(1, count // 2, stride=2), :]
    return jnp.where(lanes(even.shape) < 64, even, spin(odd, 64))


def second_kernel(ranks, axis, pick, live, got, *refs):
    st = Refs(STATE, refs[: len(STATE)])
    keep, give, forces, tm, aim = refs[len(STATE) : len(STATE) + 5]
    sc = Refs(SCRATCH_B, refs[len(STATE) + 5 :])
    me = lax.axis_index(axis)
    geo, gd = st.geo, sc.gd

    deep = got.shape[1]
    total = got[0]
    for j in range(1, ranks):
        total = total + got[j]
    first = lanes((deep, 128)) < 32
    total = jnp.concatenate([jnp.where(first, spin(total, -32 * g), 0.0) for g in range(4)], 0)
    for j in range(ranks):
        own = got[j, 3 * ranks - 3 * deep : 3 * ranks - 3 * deep + 4, :]
        for q in range(4):
            tm[q * ranks + j : q * ranks + j + 1, :] = own[q : q + 1]
    tm[...] = jnp.where(lanes((4 * ranks, 128)) < 32, spin(tm[...], -96), 0.0)
    mask = tm[3 * ranks : 4 * ranks, :]
    mine = rows_of((ranks, 128)) == me
    loss = jnp.zeros((ranks, 128), f32)
    centre = []
    for q in range(3):
        at = slice(q * ranks, q * ranks + ranks)
        error = mask * (total[at] - tm[at, :])
        loss = loss + jnp.where(mine, error * error, 0.0)
        forces[q] = jnp.sum(jnp.where(mine, total[at], 0.0), axis=0, keepdims=True)[:, 0:32]
        error = 2.0 * error
        aim[at, :] = error
        own = jnp.sum(jnp.where(mine, error, 0.0), axis=0, keepdims=True)
        centre.append(group_sum(jnp.broadcast_to(own, (8, 128)))[0:1])
    aims = aim[...]
    high = aims.astype(bf16).astype(f32)
    stacked = jnp.concatenate([high, aims - high], 0).astype(bf16)[:, 0:32]
    seen = jnp.dot(stacked, st.hot[...], preferred_element_type=f32)
    seen = seen[0 : 3 * ranks] + seen[3 * ranks :]
    for t in range(TILES):
        at_owner = rows_of((ranks, 128)) == st.owner[t : t + 1, :]
        for q in range(3):
            there = jnp.where(at_owner, seen[q * ranks : q * ranks + ranks, tile(t)], 0.0)
            sc.cdir[q, t : t + 1, :] = centre[q] - jnp.sum(there, axis=0, keepdims=True)

    xyz = tuple(st.place[q] for q in range(3))
    ways = tuple(sc.cdir[q] for q in range(3))
    _, (dd, fd, yd) = jax.jvp(geometry, xyz, ways)
    gd[0] = fd
    for m in range(8):
        gd[m + 1] = yd[m]
    gd[9] = fd * (1.0 / math.sqrt(NEI))
    tiles = []
    for t in range(TILES):
        b, slope = st.bes[0, :, tile(t)], st.bes[1, :, tile(t)]
        row = fd[t : t + 1] * b + (geo[0, t : t + 1, :] * dd[t : t + 1]) * slope
        tiles.append(jnp.concatenate([row, jnp.zeros((FEAT - 8, 128), f32)], 0))
    phid = keep_pair(sc.phid, (), jnp.concatenate(tiles, 1))
    fw, fdw = across(geo, 0), spread_rows(fd)

    zd = product(st.wf_emb[...], *phid)
    sc.zd[...] = zd
    latent = st.z1[...] * zd
    lat = keep_pair(sc.latd, (0,), latent)
    pqd = product(st.wf_first[...], *lat)
    sc.pqd[0] = pqd
    both_of = product(st.wf_lat[0, 0:192, :], *lat)
    base, ahead = both_of[0:128], both_of[128:192]

    for k in range(LAYERS):
        for r in range(0, 32, 16):
            rs = slice(r, r + 16)
            sums = None
            for t in range(TILES):
                ts = tile(t)
                p = st.pq[k, rs, ts]
                a = p * geo[9, t : t + 1, :]
                ad = pqd[rs, ts] * geo[9, t : t + 1, :] + p * gd[9, t : t + 1, :]
                terms = [ad] + [
                    ad * geo[m, t : t + 1, :] + a * gd[m, t : t + 1, :] for m in range(1, 9)
                ]
                sums = terms if sums is None else [x + y for x, y in zip(sums, terms, strict=True)]
            for m in range(9):
                sc.envd[k, m, rs, :] = group_sum(sums[m])
        for r in range(0, 32, 8):
            rs = slice(r, r + 8)
            envs = [[st.env[j, m, rs, :] for m in range(9)] for j in range(k + 1)]
            envds = [[sc.envd[j, m, rs, :] for m in range(9)] for j in range(k + 1)]
            _, (level, factors) = jax.jvp(atom_terms, (envs,), (envds,))
            for l in range(3):
                sc.bd[k, l, rs, :] = level[l]
            for m in range(8):
                sc.ehd[k, m, rs, :] = factors[m]
        high = [[None] * TILES for _ in range(6)]
        low = [[None] * TILES for _ in range(6)]
        for r in range(0, 32, 16):
            rs = slice(r, r + 16)
            ru = slice(32 + r, 48 + r)
            for t in range(TILES):
                ts = tile(t)
                qd = pqd[ru, ts]
                if k > 0:
                    qd = mix * (
                        sc.qd[k - 1, rs, ts] * st.pq[k, ru, ts] + st.qq[k - 1, rs, ts] * qd
                    )
                sc.qd[k, rs, ts] = qd
                q = st.qq[k, rs, ts]
                values = [st.bb[k, 0, rs, :], st.vv[k, rs, ts], st.vv[k, ru, ts]]
                moves = [sc.bd[k, l, rs, :] for l in range(3)]
                for m in range(1, 9):
                    l = degree(m)
                    moves[l] = (
                        moves[l]
                        + geo[m, t : t + 1, :] * sc.ehd[k, m - 1, rs, :]
                        + gd[m, t : t + 1, :] * st.eh[k, m - 1, rs, :]
                    )
                sc.vvd[k, rs, ts] = moves[1]
                sc.vvd[k, ru, ts] = moves[2]
                for l in range(3):
                    n = 2 * l + r // 16
                    high[n][t], low[n][t] = split(qd * values[l] + q * moves[l])
        high, low = joined(high), joined(low)
        sc.ivd[k, 0:96, :] = high
        sc.ivd[k, 96:192, :] = low
        hd = base + product(st.wf_io[k], high, low)
        sc.hd[k] = hd
        pair_s = keep_pair(sc.sd, (k,), st.s1[k] * hd)
        last = k == LAYERS - 1
        both_of = product(st.wf_s[k] if last else st.wf_s[k, 0:128, :], *pair_s)
        od, step = both_of[0:64], both_of[64:]
        if last:
            hhd = ahead + fdw * st.th[...] + fw * step
        else:
            pqd = ahead + fdw * st.ts[k] + fw * step
            sc.pqd[k + 1] = pqd
        latent = latent + fdw * st.oo[k] + fw * od
        lat = keep_pair(sc.latd, (k + 1,), latent)
        if not last:
            both_of = product(st.wf_lat[k + 1] if k + 2 == LAYERS else st.wf_lat[k + 1, 0:192, :], *lat)
            base, ahead = both_of[0:128], both_of[128:]

    whcol = jnp.concatenate([st.whcol[...]] * TILES, 1)
    back = keep_pair(sc.hht, (), whcol * (fdw * st.h1[...] + fw * st.h2[...] * hhd))
    both_of = product(st.wb_hh[...], *back)
    xt, lt = both_of[0:128], both_of[128:192]
    part = fw * st.h1[...] * hhd + fdw * st.sh[...]
    vector = part[:, tile(0)]
    for t in range(1, TILES):
        vector = vector + part[:, tile(t)]
    sc.grad[AT_VEC : AT_VEC + 1, :] = jnp.sum(vector.T, axis=0, keepdims=True)

    queue = []
    spare = [0]

    def work(count):
        for _ in range(min(count, len(queue))):
            queue.pop(0)()

    def single(rows, columns, first, second, finish):
        def begin():
            sc.part[0:rows, 0:columns] = cross(*first())

        def end():
            finish(settle(sc.part[0:rows, 0:columns] + cross(*second())))

        queue.extend((begin, end))

    def plain(at, count):
        def finish(value):
            sc.grad[at : at + count, :] = value

        return finish

    def packed(at, count):
        def finish(value):
            spare[0] = (spare[0] + 1) % 8
            sc.grad[at : at + count, :] = pack(value, sc.tmp.at[spare[0]])[0:count]

        return finish

    def middle(k):
        def finish(value):
            sc.mid[k] = value

        return finish

    def middle_products():
        parts = [split(sc.mid[k, 0:96, :]) for k in range(LAYERS)]
        ones = [product(st.wf_inv[k], *parts[k]) for k in range(LAYERS)]
        invs = []
        for k, (high, low) in enumerate(parts):
            inv = cross(jnp.concatenate([high, low, high], 1), st.wb_h[k, 96:160, :])
            invs.append(jnp.concatenate([inv, jnp.zeros((96, 64), f32)], 1))
        return ones, invs

    def finish_middle(ones, invs):
        for k in range(LAYERS):
            at = AT_ONE + 64 * k
            sc.grad[at : at + 64, :] = sc.mid[k, 96:160, :] + ones[k]
            packed(AT_INV + 48 * k, 48)(invs[k])

    def stack(lat, inv):
        return jnp.concatenate([inv[0:96, :], lat[0:64, :], inv[96:192, :], lat[64:128, :]], 0)

    single(
        128,
        256,
        lambda: (sc.latd[3], st.hhb[...]),
        lambda: (st.latx[3], sc.hht[...]),
        plain(AT_HEAD, 64),
    )

    for k in reversed(range(LAYERS)):
        ht = (fdw * st.xb[k] + fw * xt) * st.s1[k] + st.t2[k] * sc.hd[k]
        pair_h = keep_pair(sc.ht, (k,), ht)
        both_of = product(st.wb_h[k], *pair_h)
        vt, it = both_of[0:96], both_of[96:160]
        keep_pair(sc.ot, (k,), fdw * st.lb[k] + fw * lt)
        run = lt + it
        if k > 0:
            ahead = product(st.wb_two[k - 1], *split(run))
        work(2)
        single(
            320,
            256,
            lambda k=k: (stack(sc.latd[k], sc.ivd[k]), st.hb[k]),
            lambda k=k: (stack(st.latx[k], st.ivx[k]), sc.ht[k]),
            middle(k),
        )
        single(
            256,
            128,
            lambda k=k: (sc.sd[k], st.ob[k]),
            lambda k=k: (st.sx[k], sc.ot[k]),
            packed(AT_TWO + 64 * k, 64),
        )
        for r in range(0, 32, 16):
            rs = slice(r, r + 16)
            ru = slice(32 + r, 48 + r)
            sums = None
            for t in range(TILES):
                ts = tile(t)
                q, qd = st.qq[k, rs, ts], sc.qd[k, rs, ts]
                ls = [slice(32 * l + r, 32 * l + r + 16) for l in range(3)]
                vb = [st.vb[k, s, ts] for s in ls]
                vs = [vt[s, ts] for s in ls]
                qt = (
                    vs[0] * st.bb[k, 0, rs, :]
                    + vs[1] * st.vv[k, rs, ts]
                    + vs[2] * st.vv[k, ru, ts]
                    + vb[0] * sc.bd[k, 0, rs, :]
                    + vb[1] * sc.vvd[k, rs, ts]
                    + vb[2] * sc.vvd[k, ru, ts]
                )
                if k < LAYERS - 1:
                    qt = qt + mix * (
                        sc.pqd[k + 1, ru, ts] * st.qb[k + 1, rs, ts]
                        + st.pq[k + 1, ru, ts] * sc.qt[k + 1, rs, ts]
                    )
                sc.qt[k, rs, ts] = qt
                back = [x * q for x in vb]
                twist = [x * q + y * qd for x, y in zip(vs, vb, strict=True)]
                terms = list(twist)
                for m in range(1, 9):
                    l = degree(m)
                    terms.append(twist[l] * geo[m, t : t + 1, :] + back[l] * gd[m, t : t + 1, :])
                sums = terms if sums is None else [x + y for x, y in zip(sums, terms, strict=True)]
            for n in range(11):
                sc.cott[n, rs, :] = group_sum(sums[n])
        work(1)
        for r in range(0, 32, 8):
            rs = slice(r, r + 8)
            envs = [[st.env[j, m, rs, :] for m in range(9)] for j in range(k + 1)]
            envds = [[sc.envd[j, m, rs, :] for m in range(9)] for j in range(k + 1)]
            cots = [st.cot[k, n, rs, :] for n in range(11)]
            cotts = [sc.cott[n, rs, :] for n in range(11)]
            _, back = jax.jvp(
                atom_back,
                (envs, (cots[:3], cots[3:])),
                (envds, (cotts[:3], cotts[3:])),
            )
            for j in range(k + 1):
                for m in range(9):
                    if k == LAYERS - 1:
                        sc.et[j, m, rs, :] = back[j][m]
                    else:
                        sc.et[j, m, rs, :] += back[j][m]
        work(1)
        high = [[None] * TILES for _ in range(4)]
        low = [[None] * TILES for _ in range(4)]
        for r in range(0, 32, 16):
            rs = slice(r, r + 16)
            for t in range(TILES):
                ts = tile(t)
                at = sc.et[k, 0, rs, :]
                for m in range(1, 9):
                    at = (
                        at
                        + geo[m, t : t + 1, :] * sc.et[k, m, rs, :]
                        + gd[m, t : t + 1, :] * st.eb[k, m, rs, :]
                    )
                qt = sc.qt[k, rs, ts]
                if k > 0:
                    qt = mix * (sc.qd[k - 1, rs, ts] * st.qb[k, rs, ts] + st.qq[k - 1, rs, ts] * qt)
                pt = at * geo[9, t : t + 1, :] + st.ab[k, rs, ts] * gd[9, t : t + 1, :]
                high[r // 16][t], low[r // 16][t] = split(pt)
                high[2 + r // 16][t], low[2 + r // 16][t] = split(qt)
        high, low = joined(high), joined(low)
        sc.pt[k, 0:64, :] = high
        sc.pt[k, 64:128, :] = low
        both_of = product(st.wb_p[k] if k > 0 else st.wb_p[k, 0:64, :], high, low)
        lt = run + both_of[0:64]
        if k > 0:
            xt = ahead + both_of[64:192]
        single(
            128,
            128,
            lambda k=k: (sc.latd[k], st.pb[k]),
            lambda k=k: (st.latx[k], sc.pt[k]),
            packed(AT_ENV + 32 * k, 32),
        )
        work(2)

    keep_pair(sc.zt, (), lt * st.z1[...] + st.tz[...] * sc.zd[...])
    single(
        2 * FEAT,
        128,
        lambda: (sc.phid[...], st.zb[...]),
        lambda: (st.phi[...], sc.zt[...]),
        packed(AT_EMBED, 9),
    )
    work(len(queue))
    finish_middle(*middle_products())
    sc.grad[ROWS:PADDED, :] = jnp.zeros((PADDED - ROWS, 128), f32)
    lane = lanes((1, 128))
    amount = 3.0 * live[0, 0].astype(f32)
    sc.grad[ROWS : ROWS + 1, :] = jnp.where(
        lane == 0, jnp.sum(loss), jnp.where(lane == 1, amount, 0.0)
    )
    half = lax.axis_index(pick)
    keep[...] = sc.grad[pl.ds(pl.multiple_of(half * HALF, HALF), HALF), :]
    give[...] = sc.grad[pl.ds(pl.multiple_of((1 - half) * HALF, HALF), HALF), :]


def third_kernel(pick, mine, other, par, first, second, avg, *outs):
    loss, count, norm, new_first, new_second, new_par, low, new_avg = outs
    half = lax.axis_index(pick)
    lower = jnp.where(half == 0, mine[...], other[...])
    upper = jnp.where(half == 0, other[...], mine[...])
    last = ROWS - HALF
    scalars = upper[last : last + 1]
    loss[...] = scalars[:, 0:1]
    amount = scalars[:, 1:2]
    count[...] = amount
    squares = jnp.sum(lower * lower, keepdims=True) + jnp.sum(
        upper[0:last] * upper[0:last], keepdims=True
    )
    length = jnp.sqrt(squares) / amount
    norm[...] = length
    factor = (clip_level / jnp.maximum(length, clip_level)) / amount
    for start, stop, value in ((0, HALF, lower), (HALF, ROWS, upper[0:last])):
        rows = slice(start, stop)
        gradient = value * factor
        one = beta_one * first[rows, :] + (1.0 - beta_one) * gradient
        two = beta_two * second[rows, :] + (1.0 - beta_two) * gradient * gradient
        fixed_one = one / (1.0 - beta_one**STEP)
        fixed_two = two / (1.0 - beta_two**STEP)
        weights = par[rows, :]
        weights = weights - learn_rate * (
            fixed_one / (jnp.sqrt(fixed_two) + epsilon_adam) + decay_rate * weights
        )
        new_first[rows, :] = one
        new_second[rows, :] = two
        new_par[rows, :] = weights
        low[rows, :] = weights.astype(bf16)
        new_avg[rows, :] = average_keep * avg[rows, :] + (1.0 - average_keep) * weights


VMEM = pl.BlockSpec(memory_space=pltpu.VMEM)
HBM = pl.BlockSpec(memory_space=pltpu.HBM)
SMEM = pl.BlockSpec(memory_space=pltpu.SMEM)


def scratch(entries):
    return [pltpu.VMEM(shape, dtype) for _, shape, dtype in entries]


def local(
    ranks,
    params,
    first_moment,
    second_moment,
    average,
    edge_vectors,
    owner_rank,
    neighbour_local,
    centre_species,
    neighbour_species,
    live_atoms,
    target_forces,
):
    shape = jax.ShapeDtypeStruct
    flat = (ROWS, 128)
    par = params.reshape(flat)
    live = live_atoms.reshape(1, 1)
    tall = 32 * -(-(3 * ranks + 4) // 32)
    state = [shape(s, t) for _, s, t in STATE]
    sources = (
        edge_vectors.reshape(3, 8, 128),
        owner_rank.reshape(8, 128),
        neighbour_local.reshape(8, 128),
        neighbour_species.reshape(8, 128),
        centre_species.reshape(1, ATOMS),
        target_forces.reshape(3, 1, ATOMS),
        par,
    )
    pay, *kept = pl.pallas_call(
        functools.partial(first_kernel, ranks, "atoms"),
        out_shape=[shape((ranks, tall // 4, 128), f32), *state],
        in_specs=[SMEM] + [HBM] * 7,
        out_specs=[VMEM] * (1 + len(state)),
        scratch_shapes=[
            *[pltpu.VMEM(x.shape, x.dtype) for x in sources],
            pltpu.SemaphoreType.DMA((7,)),
            pltpu.VMEM((tall, 128), f32),
            pltpu.VMEM((6 * ranks, EDGES), bf16),
            *scratch(SCRATCH_A),
        ],
        compiler_params=pltpu.CompilerParams(vmem_limit_bytes=16 * 2**20),
        name="forward",
    )(live, *[pltpu.with_memory_space_constraint(x, pltpu.HBM) for x in sources])
    got = lax.all_to_all(pay, "atoms", split_axis=0, concat_axis=0, tiled=True)
    keep, give, forces = pl.pallas_call(
        functools.partial(second_kernel, ranks, "atoms", "low"),
        out_shape=[shape((HALF, 128), f32), shape((HALF, 128), f32), shape((3, 1, ATOMS), f32)],
        in_specs=[SMEM, VMEM] + [VMEM] * len(state),
        out_specs=[VMEM] * 3,
        scratch_shapes=[
            pltpu.VMEM((4 * ranks, 128), f32),
            pltpu.VMEM((3 * ranks, 128), f32),
            *scratch(SCRATCH_B),
        ],
        compiler_params=pltpu.CompilerParams(vmem_limit_bytes=20 * 2**20),
        name="gradient",
    )(live, got, *kept)
    swap = [(0, 1), (1, 0)]
    axes, size = ("atoms", "high"), ranks * 2
    held = keep + lax.ppermute(give, "low", swap)
    pieces = size * 8 * -(-HALF // (8 * size))
    held = jnp.pad(held, ((0, pieces - HALF), (0, 0))).reshape(size, pieces // size, 128)
    summed = lax.all_to_all(held, axes, split_axis=0, concat_axis=0, tiled=True).sum(0)
    summed = jnp.broadcast_to(summed[None], (size, *summed.shape))
    mine = lax.all_to_all(summed, axes, split_axis=0, concat_axis=0, tiled=True)
    mine = mine.reshape(pieces, 128)[:HALF]
    other = lax.ppermute(mine, "low", swap)
    one, vec = shape((1, 1), f32), shape(flat, f32)
    loss, count, norm, new_first, new_second, new_params, low, new_average = pl.pallas_call(
        functools.partial(third_kernel, "low"),
        out_shape=[one, one, one, vec, vec, vec, shape(flat, bf16), vec],
        in_specs=[VMEM] * 6,
        out_specs=[VMEM] * 8,
        compiler_params=pltpu.CompilerParams(vmem_limit_bytes=16 * 2**20),
        name="update",
    )(
        mine,
        other,
        par,
        first_moment.reshape(flat),
        second_moment.reshape(flat),
        average.reshape(flat),
    )
    return (
        loss.reshape(()),
        count.reshape(()),
        norm.reshape(()),
        forces,
        new_first.reshape(-1),
        new_second.reshape(-1),
        new_params.reshape(-1),
        low.reshape(-1),
        new_average.reshape(-1),
    )


def solution(mesh):
    ranks, groups = mesh.shape["atoms"], mesh.shape["grp"]
    fine = Mesh(mesh.devices.reshape(ranks, groups // 2, 2), ("atoms", "high", "low"))
    grp = ("high", "low")
    in_specs = (
        P(),
        P(),
        P(),
        P(),
        P(None, grp, "atoms"),
        P(grp, "atoms", None),
        P(grp, "atoms"),
        P(grp, "atoms"),
        P(grp, "atoms"),
        P(grp, "atoms"),
        P(None, grp, "atoms"),
    )
    out_specs = (P(), P(), P(), P(None, grp, "atoms"), P(), P(), P(), P(), P())
    return jax.shard_map(
        functools.partial(local, ranks),
        mesh=fine,
        in_specs=in_specs,
        out_specs=out_specs,
        check_vma=False,
    )
```

```python
import functools
import math

import jax
import jax.numpy as jnp
from jax import lax
from jax.experimental import pallas as pl
from jax.experimental.pallas import tpu as pltpu
from jax.sharding import Mesh
from jax.sharding import PartitionSpec as P

LATENT = 64
UNITS = 128
CHANNELS = 32
BASES = 8
SPECIES = 5
LAYERS = 3
STEP = 10
NEI = 32
NPARAM = 89344

cutoff_radius = 5.0
clip_level = 0.01
learn_rate = 0.1
beta_one = 0.9
beta_two = 0.999
epsilon_adam = 1e-08
decay_rate = 0.01
average_keep = 0.99
mix = 0.7071

f32 = jnp.float32
bf16 = jnp.bfloat16

ATOMS = 32
EDGES = 1024
TILES = 8
FEAT = 32

AT_EMBED = 0
AT_ENV = 9
AT_INV = AT_ENV + 96
AT_ONE = AT_INV + 144
AT_TWO = AT_ONE + 192
AT_HEAD = AT_TWO + 192
AT_VEC = AT_HEAD + 64
ROWS = AT_VEC + 1
PADDED = 768
HALF = PADDED // 2

STATE = [
    ("wf_emb", (LATENT, 3 * FEAT), bf16),
    ("wf_first", (64, 192), bf16),
    ("wf_lat", (3, 256, 192), bf16),
    ("wf_io", (3, 128, 288), bf16),
    ("wf_s", (3, 192, 384), bf16),
    ("wf_inv", (3, 64, 288), bf16),
    ("wb_hh", (192, 384), bf16),
    ("wb_h", (3, 160, 384), bf16),
    ("wb_p", (3, 192, 192), bf16),
    ("wb_two", (3, 128, 192), bf16),
    ("whcol", (128, 128), f32),
    ("place", (3, 8, 128), f32),
    ("owner", (8, 128), jnp.int32),
    ("hot", (ATOMS, EDGES), bf16),
    ("geo", (10, 8, 128), f32),
    ("bes", (2, BASES, EDGES), f32),
    ("phi", (2 * FEAT, EDGES), bf16),
    ("latx", (4, 128, EDGES), bf16),
    ("pq", (3, 64, EDGES), f32),
    ("vv", (3, 64, EDGES), f32),
    ("ivx", (3, 192, EDGES), bf16),
    ("sx", (3, 256, EDGES), bf16),
    ("s1", (3, 128, EDGES), f32),
    ("t2", (3, 128, EDGES), f32),
    ("oo", (3, 64, EDGES), f32),
    ("ts", (2, 64, EDGES), f32),
    ("th", (128, EDGES), f32),
    ("lb", (3, 64, EDGES), f32),
    ("ob", (3, 128, EDGES), bf16),
    ("hb", (3, 256, EDGES), bf16),
    ("xb", (3, 128, EDGES), f32),
    ("vb", (3, 96, EDGES), f32),
    ("ab", (3, 32, EDGES), f32),
    ("pb", (3, 128, EDGES), bf16),
    ("qq", (3, 32, EDGES), f32),
    ("qb", (3, 32, EDGES), f32),
    ("z1", (64, EDGES), f32),
    ("tz", (64, EDGES), f32),
    ("zb", (128, EDGES), bf16),
    ("sh", (128, EDGES), f32),
    ("h1", (128, EDGES), f32),
    ("h2", (128, EDGES), f32),
    ("hhb", (256, EDGES), bf16),
    ("env", (3, 9, 32, 128), f32),
    ("eh", (3, 8, 32, 128), f32),
    ("bb", (3, 3, 32, 128), f32),
    ("eb", (3, 9, 32, 128), f32),
    ("cot", (3, 11, 32, 128), f32),
]

SCRATCH_A = [
    ("tmp", (11, 128, 128), f32),
    ("wb_emb", (16, 192), bf16),
    ("ybar", (9, 8, 8, 128), f32),
    ("dbar", (8, 8, 128), f32),
]

SCRATCH_B = [
    ("tmp", (8, 128, 128), f32),
    ("part", (320, 256), f32),
    ("mid", (3, 160, 128), f32),
    ("cdir", (3, 8, 128), f32),
    ("gd", (10, 8, 128), f32),
    ("phid", (2 * FEAT, EDGES), bf16),
    ("zd", (64, EDGES), f32),
    ("latd", (4, 128, EDGES), bf16),
    ("pqd", (3, 64, EDGES), f32),
    ("vvd", (3, 64, EDGES), f32),
    ("qd", (3, 32, EDGES), f32),
    ("ivd", (3, 192, EDGES), bf16),
    ("hd", (3, 128, EDGES), f32),
    ("sd", (3, 256, EDGES), bf16),
    ("envd", (3, 9, 32, 128), f32),
    ("ehd", (3, 8, 32, 128), f32),
    ("bd", (3, 3, 32, 128), f32),
    ("hht", (256, EDGES), bf16),
    ("ot", (3, 128, EDGES), bf16),
    ("ht", (3, 256, EDGES), bf16),
    ("qt", (3, 32, EDGES), f32),
    ("pt", (3, 128, EDGES), bf16),
    ("zt", (128, EDGES), bf16),
    ("et", (3, 9, 32, 128), f32),
    ("cott", (11, 32, 128), f32),
    ("grad", (PADDED, 128), f32),
]


class Refs:
    def __init__(self, entries, refs):
        for (name, _, _), ref in zip(entries, refs, strict=True):
            setattr(self, name, ref)


def split(x):
    high = x.astype(bf16)
    return high, (x - high.astype(f32)).astype(bf16)


def product(weights, high, low):
    return jnp.dot(
        weights, jnp.concatenate([high, low, high], 0), preferred_element_type=f32
    )


def put(ref, rows, columns, value, lead=()):
    high, low = split(value)
    half = ref.shape[-2] // 2
    ref[(*lead, slice(rows, rows + value.shape[0]), columns)] = high
    ref[(*lead, slice(half + rows, half + rows + value.shape[0]), columns)] = low
    return high, low


def pair(ref, columns, lead=()):
    half = ref.shape[-2] // 2
    return ref[(*lead, slice(0, half), columns)], ref[(*lead, slice(half, 2 * half), columns)]


def spin(x, amount):
    return pltpu.roll(x, amount % 128, 1)


def group_sum(x):
    x = x + spin(x, 64)
    return x + spin(x, 32)


def lanes(shape):
    return lax.broadcasted_iota(jnp.int32, shape, len(shape) - 1)


def rows_of(shape):
    return lax.broadcasted_iota(jnp.int32, shape, len(shape) - 2)


def silu_parts(h):
    gate = 1.0 / (1.0 + jnp.exp(-h))
    slope = gate * (1.0 - gate)
    return h * gate, gate + h * slope, slope * (2.0 + h * (1.0 - 2.0 * gate))


def geometry(x, y, z):
    d = jnp.sqrt(x * x + y * y + z * z)
    u, v, w = x / d, y / d, z / d
    s = d / cutoff_radius
    s2 = s * s
    s6 = s2 * s2 * s2
    f = 1.0 - 28.0 * s6 + 48.0 * (s6 * s) - 21.0 * (s6 * s2)
    r3, r5, r15 = math.sqrt(3.0), math.sqrt(5.0), math.sqrt(15.0)
    harmonics = [
        r3 * u,
        r3 * v,
        r3 * w,
        r15 * u * v,
        r15 * v * w,
        0.5 * r5 * (3.0 * w * w - 1.0),
        r15 * u * w,
        0.5 * r15 * (u * u - v * v),
    ]
    return d, f, harmonics


def dots(left, right):
    total = left[0] * right[0]
    for a, b in zip(left[1:], right[1:], strict=True):
        total = total + a * b
    return total


def degree(m):
    return 1 if m <= 3 else 2


def atom_terms(envs):
    if len(envs) == 1:
        (one,) = envs
        zero = jnp.zeros_like(one[0])
        return [one[0], zero, zero], one[1:]
    if len(envs) == 2:
        one, two = envs
        return (
            [2.0 * one[0] * two[0], dots(one[1:4], two[1:4]), dots(one[4:], two[4:])],
            [one[0] * two[m] for m in range(1, 9)],
        )
    one, two, three = envs
    both = one[0] * two[0]
    twice = 2.0 * one[0]
    part = [two[0] * one[m] + twice * two[m] for m in range(1, 9)]
    return (
        [4.0 * both * three[0], dots(part[:3], three[1:4]), dots(part[3:], three[4:])],
        [both * three[m] for m in range(1, 9)],
    )


def atom_back(envs, cots):
    return jax.vjp(atom_terms, envs)[1](cots)[0]


def tile(t):
    return slice(128 * t, 128 * t + 128)


def fold(value):
    total = value[0:8]
    for r in range(8, value.shape[0], 8):
        total = total + value[r : r + 8]
    return total


def unpack(packed, count, tmp):
    half = count // 2
    tmp[pl.ds(0, half, stride=2), :] = packed
    tmp[pl.ds(1, half, stride=2), :] = spin(packed, 64)
    value = tmp[0:count, :]
    return jnp.where(lanes(value.shape) < 64, value, spin(value, 64))


def store_64(ref, lead, doubled, at=0):
    high, low = split(doubled)
    rows = slice(at, at + doubled.shape[0])
    ref[(*lead, rows, slice(0, 128))] = high
    ref[(*lead, rows, slice(128, 192))] = low[:, 0:64]


def store_128(ref, lead, value, at=0):
    high, low = split(value)
    rows = slice(at, at + value.shape[0])
    ref[(*lead, rows, slice(0, 128))] = high
    ref[(*lead, rows, slice(128, 256))] = high
    ref[(*lead, rows, slice(256, 384))] = low


def store_96(ref, lead, value):
    high = value.astype(bf16).astype(f32)
    low = value - high
    high_on, low_on = spin(high, 96), spin(low, 64)
    lane = lanes(value.shape)
    ref[(*lead, slice(None), slice(0, 128))] = jnp.where(lane < 96, high, high_on).astype(bf16)
    ref[(*lead, slice(None), slice(128, 256))] = jnp.where(lane < 64, high_on, low_on).astype(bf16)
    ref[(*lead, slice(None), slice(256, 288))] = low_on[:, 0:32].astype(bf16)


def across(ref, index):
    return jnp.concatenate([ref[index, t : t + 1, :] for t in range(TILES)], 1)


def spread_rows(value):
    return jnp.concatenate([value[t : t + 1] for t in range(TILES)], 1)


def joined(grid):
    return jnp.concatenate([jnp.concatenate(row, 1) for row in grid], 0)


def keep_pair(ref, lead, value):
    high, low = split(value)
    half = value.shape[0]
    ref[(*lead, slice(0, half), slice(None))] = high
    ref[(*lead, slice(half, 2 * half), slice(None))] = low
    return high, low


def both(ref, lead=()):
    half = ref.shape[-2] // 2
    return ref[(*lead, slice(0, half), slice(None))], ref[(*lead, slice(half, 2 * half), slice(None))]


def shares(value):
    total = fold(value)
    return [total[:, tile(t)] for t in range(TILES)]


def tmp_rows(w, start):
    return jnp.concatenate([w[start : start + 2], jnp.zeros((14, 128), f32)], 0)


def weights_product(left, right):
    high, low = split(right)
    return product(left, high, low)


def prepare(par, st, sc):
    def turned(value):
        return value.T

    spare = iter(range(11))

    def doubled(at, count):
        return unpack(par[at : at + count // 2, :], count, sc.tmp.at[next(spare)])

    w = doubled(AT_EMBED, 18)
    w = jnp.concatenate([w[0:16], tmp_rows(w, 16)], 0)
    store_64(sc.wb_emb, (), w[0:16])
    high = w.astype(bf16).astype(f32)
    low = w - high
    turn = jnp.concatenate([high, high, low, jnp.zeros((32, 128), f32)], 0).T[0:64]
    st.wf_emb[...] = turn[:, 0 : 3 * FEAT].astype(bf16)
    envs = []
    for k in range(LAYERS):
        w = doubled(AT_ENV + 32 * k, 64)
        envs.append(w)
        store_64(st.wb_p, (k,), w)
        turn = jnp.concatenate([w, w], 0).T[0:64]
        if k == 0:
            store_64(st.wf_first, (), turn)
        else:
            store_64(st.wf_lat, (k - 1,), turn, 128)
    head = par[AT_HEAD : AT_HEAD + 64, :]
    store_128(st.wb_hh, (), head, 128)
    store_64(st.wf_lat, (2,), jnp.concatenate([head, head], 0).T, 128)
    for k in range(LAYERS):
        one = par[AT_ONE + 64 * k : AT_ONE + 64 * k + 64, :]
        store_128(st.wb_h, (k,), one, 96)
        store_64(st.wf_lat, (k,), jnp.concatenate([one, one], 0).T)
        w = doubled(AT_INV + 48 * k, 96)
        store_96(st.wf_inv, (k,), jnp.concatenate([w, jnp.zeros((32, 128), f32)], 0).T[0:64])
        high, low = split(w)
        w = weights_product(jnp.concatenate([high, low[:, 0:64]], 1), one)
        store_128(st.wb_h, (k,), w)
        store_96(st.wf_io, (k,), jnp.concatenate([w, jnp.zeros((32, 128), f32)], 0).T)
        w = doubled(AT_TWO + 64 * k, 128)
        high, low = split(w)
        left = jnp.concatenate([high, low[:, 0:64]], 1)
        st.wb_two[k] = left
        store_128(st.wf_s, (k,), w.T[0:64])
        if k < LAYERS - 1:
            w = weights_product(left, envs[k + 1])
            store_64(st.wb_p, (k + 1,), w, 64)
            store_128(st.wf_s, (k,), w.T[0:64], 64)
        else:
            w = weights_product(left, head)
            store_128(st.wb_hh, (), w)
            store_128(st.wf_s, (k,), w.T, 64)
    st.whcol[...] = jnp.broadcast_to(par[AT_VEC : AT_VEC + 1, :], (128, 128)).T


def sine_parts(turns):
    whole = jnp.round(turns)
    rest = (turns - whole) * math.pi
    odd = whole - 2.0 * jnp.floor(whole * 0.5)
    sign = 1.0 - 2.0 * odd
    r2 = rest * rest
    sine = 0.0
    for n in (13, 11, 9, 7, 5, 3, 1):
        sine = sine * r2 + (-1.0) ** (n // 2) / math.factorial(n)
    cosine = 0.0
    for n in (14, 12, 10, 8, 6, 4, 2, 0):
        cosine = cosine * r2 + (-1.0) ** (n // 2) / math.factorial(n)
    return sign * rest * sine, sign * cosine


def first_kernel(ranks, axis, live, *refs):
    sources = refs[0:7]
    pay = refs[7]
    st = Refs(STATE, refs[8 : 8 + len(STATE)])
    rest = refs[8 + len(STATE) :]
    vec, own, loc, nsp, cen, tgt, par = rest[0:7]
    sems, payload, scatter = rest[7:10]
    sc = Refs(SCRATCH_A, rest[10:])
    me = 2 * lax.axis_index(axis[0]) + lax.axis_index(axis[1])
    copies = [
        pltpu.make_async_copy(source, target, sems.at[n])
        for n, (source, target) in enumerate(zip(sources, rest[0:7], strict=True))
    ]
    for copy in copies:
        copy.start()
    for copy in copies[:6]:
        copy.wait()

    order = sc.tmp.at[10]
    code = ((own[...] * 32 + loc[...]) * 8 + nsp[...]).astype(f32)
    for q, value in enumerate((vec[0], vec[1], vec[2], code)):
        for a in range(4):
            order[pl.ds(32 * q + a, 8, stride=4), :] = spin(value, -32 * a)
    turned = order[...].T
    lane = lanes((8, 128))

    def picked(q):
        out = spin(turned[0:8], -32 * q)
        for g in range(1, 4):
            out = jnp.where(lane // 32 == g, spin(turned[8 * g : 8 * g + 8], 32 * (g - q)), out)
        return out

    xyz = [picked(q) for q in range(3)]
    codes = picked(3).astype(jnp.int32)
    for q in range(3):
        st.place[q] = xyz[q]
    local = lax.shift_right_logical(codes, 3) & 31
    owner = lax.shift_right_logical(codes, 8)
    kind = codes & 7
    st.owner[...] = owner
    sc.dbar[0] = jnp.zeros((8, 128), f32)
    sc.dbar[0, 0:1, 0:32] = cen[...].astype(f32)
    centre_kind = group_sum(sc.dbar[0])[0:1].astype(jnp.int32)

    d, f, harmonics = geometry(*xyz)
    geo = st.geo
    geo[0] = f
    for m in range(8):
        geo[m + 1] = harmonics[m]
    geo[9] = f * (1.0 / math.sqrt(NEI))

    orders = (rows_of((8, 128)) + 1).astype(f32)
    inv_d = 1.0 / d
    scale = math.sqrt(2.0 / cutoff_radius)
    tiles = []
    for t in range(TILES):
        row_inv = inv_d[t : t + 1]
        sine, cosine = sine_parts(orders * (d[t : t + 1] / cutoff_radius))
        b = (scale * sine) * row_inv
        slope = (scale * math.pi / cutoff_radius) * orders * cosine * row_inv - b * row_inv
        st.bes[0, :, tile(t)] = b
        st.bes[1, :, tile(t)] = slope
        row = rows_of((FEAT - 8, 128)) + 8
        hot = (row == centre_kind + 8) | (row == kind[t : t + 1] + 13)
        tiles.append(jnp.concatenate([b * f[t : t + 1], hot.astype(f32)], 0))
        st.hot[:, tile(t)] = (rows_of((ATOMS, 128)) == local[t : t + 1]).astype(f32).astype(bf16)
    phi = keep_pair(st.phi, (), jnp.concatenate(tiles, 1))

    copies[6].wait()
    prepare(par, st, sc)
    fw = spread_rows(f)

    s, s1, s2 = silu_parts(product(st.wf_emb[...], *phi))
    st.z1[...] = s1
    st.tz[...] = s2
    latent = s
    lat = keep_pair(st.latx, (0,), s)
    pq = product(st.wf_first[...], *lat)
    st.pq[0] = pq
    both_of = product(st.wf_lat[0, 0:192, :], *lat)
    base, ahead = both_of[0:128], both_of[128:192]

    for k in range(LAYERS):
        for r in range(0, 32, 16):
            rs = slice(r, r + 16)
            sums = None
            for t in range(TILES):
                a = pq[rs, tile(t)] * geo[9, t : t + 1, :]
                terms = [a] + [a * geo[m, t : t + 1, :] for m in range(1, 9)]
                sums = terms if sums is None else [x + y for x, y in zip(sums, terms, strict=True)]
            for m in range(9):
                st.env[k, m, rs, :] = group_sum(sums[m])
        for r in range(0, 32, 8):
            rs = slice(r, r + 8)
            envs = [[st.env[j, m, rs, :] for m in range(9)] for j in range(k + 1)]
            level, factors = atom_terms(envs)
            for l in range(3):
                st.bb[k, l, rs, :] = level[l]
            for m in range(8):
                st.eh[k, m, rs, :] = factors[m]
        high = [[None] * TILES for _ in range(6)]
        low = [[None] * TILES for _ in range(6)]
        for r in range(0, 32, 16):
            rs = slice(r, r + 16)
            for t in range(TILES):
                ts = tile(t)
                q = pq[32 + r : 48 + r, ts]
                if k > 0:
                    q = mix * st.qq[k - 1, rs, ts] * q
                st.qq[k, rs, ts] = q
                values = [st.bb[k, l, rs, :] for l in range(3)]
                for m in range(1, 9):
                    l = degree(m)
                    values[l] = values[l] + geo[m, t : t + 1, :] * st.eh[k, m - 1, rs, :]
                st.vv[k, rs, ts] = values[1]
                st.vv[k, 32 + r : 48 + r, ts] = values[2]
                for l in range(3):
                    n = 2 * l + r // 16
                    high[n][t], low[n][t] = split(q * values[l])
        high, low = joined(high), joined(low)
        st.ivx[k, 0:96, :] = high
        st.ivx[k, 96:192, :] = low
        h = base + product(st.wf_io[k], high, low)
        s, s1, s2 = silu_parts(h)
        st.s1[k] = s1
        st.t2[k] = s2
        pair_s = keep_pair(st.sx, (k,), s)
        last = k == LAYERS - 1
        both_of = product(st.wf_s[k] if last else st.wf_s[k, 0:128, :], *pair_s)
        o, step = both_of[0:64], both_of[64:]
        if last:
            st.th[...] = step
            hh = ahead + fw * step
        else:
            st.ts[k] = step
            pq = ahead + fw * step
            st.pq[k + 1] = pq
        st.oo[k] = o
        latent = latent + fw * o
        lat = keep_pair(st.latx, (k + 1,), latent)
        if not last:
            both_of = product(st.wf_lat[k + 1] if k + 2 == LAYERS else st.wf_lat[k + 1, 0:192, :], *lat)
            base, ahead = both_of[0:128], both_of[128:]

    s, s1, s2 = silu_parts(hh)
    st.sh[...] = s
    st.h1[...] = s1
    st.h2[...] = s2
    whcol = jnp.concatenate([st.whcol[...]] * TILES, 1)
    back = keep_pair(st.hhb, (), fw * whcol * s1)
    for t, share in enumerate(shares(whcol * s)):
        sc.ybar[0, t] = share
    both_of = product(st.wb_hh[...], *back)
    xb, lb = both_of[0:128], both_of[128:192]

    for k in reversed(range(LAYERS)):
        st.xb[k] = xb
        sb = fw * xb
        pair_h = keep_pair(st.hb, (k,), st.s1[k] * sb)
        st.t2[k] = st.t2[k] * sb
        both_of = product(st.wb_h[k], *pair_h)
        vb, ib = both_of[0:96], both_of[96:160]
        st.vb[k] = vb
        st.lb[k] = lb
        keep_pair(st.ob, (k,), fw * lb)
        for t, share in enumerate(shares(st.oo[k] * lb)):
            sc.ybar[0, t] += share
        run = lb + ib
        if k > 0:
            ahead = product(st.wb_two[k - 1], *split(run))
        for r in range(0, 32, 16):
            rs = slice(r, r + 16)
            sums = None
            for t in range(TILES):
                ts = tile(t)
                q = st.qq[k, rs, ts]
                vs = [vb[32 * l + r : 32 * l + r + 16, ts] for l in range(3)]
                qb = (
                    vs[0] * st.bb[k, 0, rs, :]
                    + vs[1] * st.vv[k, rs, ts]
                    + vs[2] * st.vv[k, 32 + r : 48 + r, ts]
                )
                if k < LAYERS - 1:
                    qb = qb + mix * st.pq[k + 1, 32 + r : 48 + r, ts] * st.qb[k + 1, rs, ts]
                st.qb[k, rs, ts] = qb
                back = [x * q for x in vs]
                terms = list(back)
                for m in range(1, 9):
                    terms.append(back[degree(m)] * geo[m, t : t + 1, :])
                    share = fold(back[degree(m)] * st.eh[k, m - 1, rs, :])
                    if k == LAYERS - 1 and r == 0:
                        sc.ybar[m, t] = share
                    else:
                        sc.ybar[m, t] += share
                sums = terms if sums is None else [x + y for x, y in zip(sums, terms, strict=True)]
            for n in range(11):
                st.cot[k, n, rs, :] = group_sum(sums[n])
        for r in range(0, 32, 8):
            rs = slice(r, r + 8)
            envs = [[st.env[j, m, rs, :] for m in range(9)] for j in range(k + 1)]
            cots = [st.cot[k, n, rs, :] for n in range(11)]
            back = atom_back(envs, (cots[:3], cots[3:]))
            for j in range(k + 1):
                for m in range(9):
                    if k == LAYERS - 1:
                        st.eb[j, m, rs, :] = back[j][m]
                    else:
                        st.eb[j, m, rs, :] += back[j][m]
        high = [[None] * TILES for _ in range(4)]
        low = [[None] * TILES for _ in range(4)]
        for r in range(0, 32, 16):
            rs = slice(r, r + 16)
            for t in range(TILES):
                ts = tile(t)
                p = st.pq[k, rs, ts]
                fs = geo[9, t : t + 1, :]
                a = p * fs
                ab = st.eb[k, 0, rs, :]
                for m in range(1, 9):
                    e = st.eb[k, m, rs, :]
                    ab = ab + geo[m, t : t + 1, :] * e
                    sc.ybar[m, t] += fold(a * e)
                st.ab[k, rs, ts] = ab
                sc.ybar[0, t] += fold((1.0 / math.sqrt(NEI)) * ab * p)
                qb = st.qb[k, rs, ts]
                if k > 0:
                    qb = mix * st.qq[k - 1, rs, ts] * qb
                high[r // 16][t], low[r // 16][t] = split(ab * fs)
                high[2 + r // 16][t], low[2 + r // 16][t] = split(qb)
        high, low = joined(high), joined(low)
        st.pb[k, 0:64, :] = high
        st.pb[k, 64:128, :] = low
        both_of = product(st.wb_p[k] if k > 0 else st.wb_p[k, 0:64, :], high, low)
        lb = run + both_of[0:64]
        if k > 0:
            xb = ahead + both_of[64:192]

    st.tz[...] = st.tz[...] * lb
    pb = product(sc.wb_emb[...], *keep_pair(st.zb, (), st.z1[...] * lb))[0:8]
    for t in range(TILES):
        part = pb[:, tile(t)]
        sc.ybar[0, t] += st.bes[0, :, tile(t)] * part
        sc.dbar[t] = geo[0, t : t + 1, :] * st.bes[1, :, tile(t)] * part

    bars = [jnp.sum(sc.ybar[m], axis=1) for m in range(9)]
    slopes = jax.vjp(geometry, *xyz)[1]((jnp.sum(sc.dbar[...], axis=1), bars[0], bars[1:]))

    for t in range(TILES):
        mine = rows_of((ranks, 128)) == owner[t : t + 1]
        parts = jnp.concatenate([jnp.where(mine, s[t : t + 1], 0.0) for s in slopes], 0)
        high = parts.astype(bf16).astype(f32)
        scatter[:, tile(t)] = jnp.concatenate([high, parts - high], 0).astype(bf16)
    sums = lax.dot_general(
        scatter[...], st.hot[...], (((1,), (1,)), ((), ())), preferred_element_type=f32
    )
    payload[...] = jnp.zeros(payload.shape, f32)
    for q in range(3):
        at = ranks * q
        total = jnp.broadcast_to(jnp.sum(slopes[q], axis=0, keepdims=True), (8, 128))
        total = group_sum(total)[0:1, 0:32]
        part = -(sums[at : at + ranks] + sums[3 * ranks + at : 4 * ranks + at])
        payload[at : at + ranks, 0:32] = part + jnp.where(
            rows_of((ranks, 32)) == me, total, 0.0
        )
    for q in range(3):
        payload[3 * ranks + q : 3 * ranks + q + 1, 0:32] = tgt[q]
    payload[3 * ranks + 3 : 3 * ranks + 4, 0:32] = (lanes((1, 32)) < live[0, 0]).astype(f32)

    deep = pay.shape[1]
    packed = payload[0:deep, :]
    for g in range(1, 4):
        packed = packed + spin(payload[g * deep : g * deep + deep, :], 32 * g)
    payload[0:deep, :] = packed

    def spread(j, carry):
        pay[j] = payload[0:deep, :]
        return carry

    lax.fori_loop(0, ranks, spread, 0)


def cross(x, y):
    return lax.dot_general(x, y, (((1,), (1,)), ((), ())), preferred_element_type=f32)


def settle(full):
    rows, columns = full.shape[0] // 2, full.shape[1] // 2
    if columns == 64:
        return full[:rows] + (spin(full[:rows], 64) + full[rows:])
    return full[:rows, :columns] + (full[:rows, columns:] + full[rows:, :columns])


def pack(value, tmp):
    count = value.shape[0]
    tmp[0:count, :] = value
    even, odd = tmp[pl.ds(0, count // 2, stride=2), :], tmp[pl.ds(1, count // 2, stride=2), :]
    return jnp.where(lanes(even.shape) < 64, even, spin(odd, 64))


def second_kernel(ranks, axis, pick, live, got, *refs):
    st = Refs(STATE, refs[: len(STATE)])
    keep, give, forces, tm, aim = refs[len(STATE) : len(STATE) + 5]
    sc = Refs(SCRATCH_B, refs[len(STATE) + 5 :])
    me = 2 * lax.axis_index(axis[0]) + lax.axis_index(axis[1])
    geo, gd = st.geo, sc.gd

    deep = got.shape[1]
    total = got[0]
    for j in range(1, ranks):
        total = total + got[j]
    first = lanes((deep, 128)) < 32
    total = jnp.concatenate([jnp.where(first, spin(total, -32 * g), 0.0) for g in range(4)], 0)
    for j in range(ranks):
        own = got[j, 3 * ranks - 3 * deep : 3 * ranks - 3 * deep + 4, :]
        for q in range(4):
            tm[q * ranks + j : q * ranks + j + 1, :] = own[q : q + 1]
    tm[...] = jnp.where(lanes((4 * ranks, 128)) < 32, spin(tm[...], -96), 0.0)
    mask = tm[3 * ranks : 4 * ranks, :]
    mine = rows_of((ranks, 128)) == me
    loss = jnp.zeros((ranks, 128), f32)
    centre = []
    for q in range(3):
        at = slice(q * ranks, q * ranks + ranks)
        error = mask * (total[at] - tm[at, :])
        loss = loss + jnp.where(mine, error * error, 0.0)
        forces[q] = jnp.sum(jnp.where(mine, total[at], 0.0), axis=0, keepdims=True)[:, 0:32]
        error = 2.0 * error
        aim[at, :] = error
        own = jnp.sum(jnp.where(mine, error, 0.0), axis=0, keepdims=True)
        centre.append(group_sum(jnp.broadcast_to(own, (8, 128)))[0:1])
    aims = aim[...]
    high = aims.astype(bf16).astype(f32)
    stacked = jnp.concatenate([high, aims - high], 0).astype(bf16)[:, 0:32]
    seen = jnp.dot(stacked, st.hot[...], preferred_element_type=f32)
    seen = seen[0 : 3 * ranks] + seen[3 * ranks :]
    for t in range(TILES):
        at_owner = rows_of((ranks, 128)) == st.owner[t : t + 1, :]
        for q in range(3):
            there = jnp.where(at_owner, seen[q * ranks : q * ranks + ranks, tile(t)], 0.0)
            sc.cdir[q, t : t + 1, :] = centre[q] - jnp.sum(there, axis=0, keepdims=True)

    xyz = tuple(st.place[q] for q in range(3))
    ways = tuple(sc.cdir[q] for q in range(3))
    _, (dd, fd, yd) = jax.jvp(geometry, xyz, ways)
    gd[0] = fd
    for m in range(8):
        gd[m + 1] = yd[m]
    gd[9] = fd * (1.0 / math.sqrt(NEI))
    tiles = []
    for t in range(TILES):
        b, slope = st.bes[0, :, tile(t)], st.bes[1, :, tile(t)]
        row = fd[t : t + 1] * b + (geo[0, t : t + 1, :] * dd[t : t + 1]) * slope
        tiles.append(jnp.concatenate([row, jnp.zeros((FEAT - 8, 128), f32)], 0))
    phid = keep_pair(sc.phid, (), jnp.concatenate(tiles, 1))
    fw, fdw = across(geo, 0), spread_rows(fd)

    zd = product(st.wf_emb[...], *phid)
    sc.zd[...] = zd
    latent = st.z1[...] * zd
    lat = keep_pair(sc.latd, (0,), latent)
    pqd = product(st.wf_first[...], *lat)
    sc.pqd[0] = pqd
    both_of = product(st.wf_lat[0, 0:192, :], *lat)
    base, ahead = both_of[0:128], both_of[128:192]

    for k in range(LAYERS):
        for r in range(0, 32, 16):
            rs = slice(r, r + 16)
            sums = None
            for t in range(TILES):
                ts = tile(t)
                p = st.pq[k, rs, ts]
                a = p * geo[9, t : t + 1, :]
                ad = pqd[rs, ts] * geo[9, t : t + 1, :] + p * gd[9, t : t + 1, :]
                terms = [ad] + [
                    ad * geo[m, t : t + 1, :] + a * gd[m, t : t + 1, :] for m in range(1, 9)
                ]
                sums = terms if sums is None else [x + y for x, y in zip(sums, terms, strict=True)]
            for m in range(9):
                sc.envd[k, m, rs, :] = group_sum(sums[m])
        for r in range(0, 32, 8):
            rs = slice(r, r + 8)
            envs = [[st.env[j, m, rs, :] for m in range(9)] for j in range(k + 1)]
            envds = [[sc.envd[j, m, rs, :] for m in range(9)] for j in range(k + 1)]
            _, (level, factors) = jax.jvp(atom_terms, (envs,), (envds,))
            for l in range(3):
                sc.bd[k, l, rs, :] = level[l]
            for m in range(8):
                sc.ehd[k, m, rs, :] = factors[m]
        high = [[None] * TILES for _ in range(6)]
        low = [[None] * TILES for _ in range(6)]
        for r in range(0, 32, 16):
            rs = slice(r, r + 16)
            ru = slice(32 + r, 48 + r)
            for t in range(TILES):
                ts = tile(t)
                qd = pqd[ru, ts]
                if k > 0:
                    qd = mix * (
                        sc.qd[k - 1, rs, ts] * st.pq[k, ru, ts] + st.qq[k - 1, rs, ts] * qd
                    )
                sc.qd[k, rs, ts] = qd
                q = st.qq[k, rs, ts]
                values = [st.bb[k, 0, rs, :], st.vv[k, rs, ts], st.vv[k, ru, ts]]
                moves = [sc.bd[k, l, rs, :] for l in range(3)]
                for m in range(1, 9):
                    l = degree(m)
                    moves[l] = (
                        moves[l]
                        + geo[m, t : t + 1, :] * sc.ehd[k, m - 1, rs, :]
                        + gd[m, t : t + 1, :] * st.eh[k, m - 1, rs, :]
                    )
                sc.vvd[k, rs, ts] = moves[1]
                sc.vvd[k, ru, ts] = moves[2]
                for l in range(3):
                    n = 2 * l + r // 16
                    high[n][t], low[n][t] = split(qd * values[l] + q * moves[l])
        high, low = joined(high), joined(low)
        sc.ivd[k, 0:96, :] = high
        sc.ivd[k, 96:192, :] = low
        hd = base + product(st.wf_io[k], high, low)
        sc.hd[k] = hd
        pair_s = keep_pair(sc.sd, (k,), st.s1[k] * hd)
        last = k == LAYERS - 1
        both_of = product(st.wf_s[k] if last else st.wf_s[k, 0:128, :], *pair_s)
        od, step = both_of[0:64], both_of[64:]
        if last:
            hhd = ahead + fdw * st.th[...] + fw * step
        else:
            pqd = ahead + fdw * st.ts[k] + fw * step
            sc.pqd[k + 1] = pqd
        latent = latent + fdw * st.oo[k] + fw * od
        lat = keep_pair(sc.latd, (k + 1,), latent)
        if not last:
            both_of = product(st.wf_lat[k + 1] if k + 2 == LAYERS else st.wf_lat[k + 1, 0:192, :], *lat)
            base, ahead = both_of[0:128], both_of[128:]

    whcol = jnp.concatenate([st.whcol[...]] * TILES, 1)
    back = keep_pair(sc.hht, (), whcol * (fdw * st.h1[...] + fw * st.h2[...] * hhd))
    both_of = product(st.wb_hh[...], *back)
    xt, lt = both_of[0:128], both_of[128:192]
    part = fw * st.h1[...] * hhd + fdw * st.sh[...]
    vector = part[:, tile(0)]
    for t in range(1, TILES):
        vector = vector + part[:, tile(t)]
    sc.grad[AT_VEC : AT_VEC + 1, :] = jnp.sum(vector.T, axis=0, keepdims=True)

    queue = []
    spare = [0]

    def work(count):
        for _ in range(min(count, len(queue))):
            queue.pop(0)()

    def single(rows, columns, first, second, finish):
        def begin():
            sc.part[0:rows, 0:columns] = cross(*first())

        def end():
            finish(settle(sc.part[0:rows, 0:columns] + cross(*second())))

        queue.extend((begin, end))

    def plain(at, count):
        def finish(value):
            sc.grad[at : at + count, :] = value

        return finish

    def packed(at, count):
        def finish(value):
            spare[0] = (spare[0] + 1) % 8
            sc.grad[at : at + count, :] = pack(value, sc.tmp.at[spare[0]])[0:count]

        return finish

    def middle(k):
        def finish(value):
            sc.mid[k] = value

        return finish

    def middle_products():
        parts = [split(sc.mid[k, 0:96, :]) for k in range(LAYERS)]
        ones = [product(st.wf_inv[k], *parts[k]) for k in range(LAYERS)]
        invs = []
        for k, (high, low) in enumerate(parts):
            inv = cross(jnp.concatenate([high, low, high], 1), st.wb_h[k, 96:160, :])
            invs.append(jnp.concatenate([inv, jnp.zeros((96, 64), f32)], 1))
        return ones, invs

    def finish_middle(ones, invs):
        for k in range(LAYERS):
            at = AT_ONE + 64 * k
            sc.grad[at : at + 64, :] = sc.mid[k, 96:160, :] + ones[k]
            packed(AT_INV + 48 * k, 48)(invs[k])

    def stack(lat, inv):
        return jnp.concatenate([inv[0:96, :], lat[0:64, :], inv[96:192, :], lat[64:128, :]], 0)

    single(
        128,
        256,
        lambda: (sc.latd[3], st.hhb[...]),
        lambda: (st.latx[3], sc.hht[...]),
        plain(AT_HEAD, 64),
    )

    for k in reversed(range(LAYERS)):
        ht = (fdw * st.xb[k] + fw * xt) * st.s1[k] + st.t2[k] * sc.hd[k]
        pair_h = keep_pair(sc.ht, (k,), ht)
        both_of = product(st.wb_h[k], *pair_h)
        vt, it = both_of[0:96], both_of[96:160]
        keep_pair(sc.ot, (k,), fdw * st.lb[k] + fw * lt)
        run = lt + it
        if k > 0:
            ahead = product(st.wb_two[k - 1], *split(run))
        work(2)
        single(
            320,
            256,
            lambda k=k: (stack(sc.latd[k], sc.ivd[k]), st.hb[k]),
            lambda k=k: (stack(st.latx[k], st.ivx[k]), sc.ht[k]),
            middle(k),
        )
        single(
            256,
            128,
            lambda k=k: (sc.sd[k], st.ob[k]),
            lambda k=k: (st.sx[k], sc.ot[k]),
            packed(AT_TWO + 64 * k, 64),
        )
        for r in range(0, 32, 16):
            rs = slice(r, r + 16)
            ru = slice(32 + r, 48 + r)
            sums = None
            for t in range(TILES):
                ts = tile(t)
                q, qd = st.qq[k, rs, ts], sc.qd[k, rs, ts]
                ls = [slice(32 * l + r, 32 * l + r + 16) for l in range(3)]
                vb = [st.vb[k, s, ts] for s in ls]
                vs = [vt[s, ts] for s in ls]
                qt = (
                    vs[0] * st.bb[k, 0, rs, :]
                    + vs[1] * st.vv[k, rs, ts]
                    + vs[2] * st.vv[k, ru, ts]
                    + vb[0] * sc.bd[k, 0, rs, :]
                    + vb[1] * sc.vvd[k, rs, ts]
                    + vb[2] * sc.vvd[k, ru, ts]
                )
                if k < LAYERS - 1:
                    qt = qt + mix * (
                        sc.pqd[k + 1, ru, ts] * st.qb[k + 1, rs, ts]
                        + st.pq[k + 1, ru, ts] * sc.qt[k + 1, rs, ts]
                    )
                sc.qt[k, rs, ts] = qt
                back = [x * q for x in vb]
                twist = [x * q + y * qd for x, y in zip(vs, vb, strict=True)]
                terms = list(twist)
                for m in range(1, 9):
                    l = degree(m)
                    terms.append(twist[l] * geo[m, t : t + 1, :] + back[l] * gd[m, t : t + 1, :])
                sums = terms if sums is None else [x + y for x, y in zip(sums, terms, strict=True)]
            for n in range(11):
                sc.cott[n, rs, :] = group_sum(sums[n])
        work(1)
        for r in range(0, 32, 8):
            rs = slice(r, r + 8)
            envs = [[st.env[j, m, rs, :] for m in range(9)] for j in range(k + 1)]
            envds = [[sc.envd[j, m, rs, :] for m in range(9)] for j in range(k + 1)]
            cots = [st.cot[k, n, rs, :] for n in range(11)]
            cotts = [sc.cott[n, rs, :] for n in range(11)]
            _, back = jax.jvp(
                atom_back,
                (envs, (cots[:3], cots[3:])),
                (envds, (cotts[:3], cotts[3:])),
            )
            for j in range(k + 1):
                for m in range(9):
                    if k == LAYERS - 1:
                        sc.et[j, m, rs, :] = back[j][m]
                    else:
                        sc.et[j, m, rs, :] += back[j][m]
        work(1)
        high = [[None] * TILES for _ in range(4)]
        low = [[None] * TILES for _ in range(4)]
        for r in range(0, 32, 16):
            rs = slice(r, r + 16)
            for t in range(TILES):
                ts = tile(t)
                at = sc.et[k, 0, rs, :]
                for m in range(1, 9):
                    at = (
                        at
                        + geo[m, t : t + 1, :] * sc.et[k, m, rs, :]
                        + gd[m, t : t + 1, :] * st.eb[k, m, rs, :]
                    )
                qt = sc.qt[k, rs, ts]
                if k > 0:
                    qt = mix * (sc.qd[k - 1, rs, ts] * st.qb[k, rs, ts] + st.qq[k - 1, rs, ts] * qt)
                pt = at * geo[9, t : t + 1, :] + st.ab[k, rs, ts] * gd[9, t : t + 1, :]
                high[r // 16][t], low[r // 16][t] = split(pt)
                high[2 + r // 16][t], low[2 + r // 16][t] = split(qt)
        high, low = joined(high), joined(low)
        sc.pt[k, 0:64, :] = high
        sc.pt[k, 64:128, :] = low
        both_of = product(st.wb_p[k] if k > 0 else st.wb_p[k, 0:64, :], high, low)
        lt = run + both_of[0:64]
        if k > 0:
            xt = ahead + both_of[64:192]
        single(
            128,
            128,
            lambda k=k: (sc.latd[k], st.pb[k]),
            lambda k=k: (st.latx[k], sc.pt[k]),
            packed(AT_ENV + 32 * k, 32),
        )
        work(2)

    keep_pair(sc.zt, (), lt * st.z1[...] + st.tz[...] * sc.zd[...])
    single(
        2 * FEAT,
        128,
        lambda: (sc.phid[...], st.zb[...]),
        lambda: (st.phi[...], sc.zt[...]),
        packed(AT_EMBED, 9),
    )
    work(len(queue))
    finish_middle(*middle_products())
    sc.grad[ROWS:PADDED, :] = jnp.zeros((PADDED - ROWS, 128), f32)
    lane = lanes((1, 128))
    amount = 3.0 * live[0, 0].astype(f32)
    sc.grad[ROWS : ROWS + 1, :] = jnp.where(
        lane == 0, jnp.sum(loss), jnp.where(lane == 1, amount, 0.0)
    )
    half = lax.axis_index(pick)
    keep[...] = sc.grad[pl.ds(pl.multiple_of(half * HALF, HALF), HALF), :]
    give[...] = sc.grad[pl.ds(pl.multiple_of((1 - half) * HALF, HALF), HALF), :]


def third_kernel(pick, mine, other, par, first, second, avg, *outs):
    loss, count, norm, new_first, new_second, new_par, low, new_avg, order = outs
    half = lax.axis_index(pick)
    spot = 2 * lax.axis_index("near") + lax.axis_index("high")
    for k in range(4):
        order[half, spot ^ k] = mine[k]
        order[1 - half, spot ^ k] = other[k]
    lower = jnp.concatenate([order[0, k] for k in range(4)], 0)
    upper = jnp.concatenate([order[1, k] for k in range(4)], 0)
    last = ROWS - HALF
    scalars = upper[last : last + 1]
    loss[...] = scalars[:, 0:1]
    amount = scalars[:, 1:2]
    count[...] = amount
    squares = jnp.sum(lower * lower, keepdims=True) + jnp.sum(
        upper[0:last] * upper[0:last], keepdims=True
    )
    length = jnp.sqrt(squares) / amount
    norm[...] = length
    factor = (clip_level / jnp.maximum(length, clip_level)) / amount
    for start, stop, value in ((0, HALF, lower), (HALF, ROWS, upper[0:last])):
        rows = slice(start, stop)
        gradient = value * factor
        one = beta_one * first[rows, :] + (1.0 - beta_one) * gradient
        two = beta_two * second[rows, :] + (1.0 - beta_two) * gradient * gradient
        fixed_one = one / (1.0 - beta_one**STEP)
        fixed_two = two / (1.0 - beta_two**STEP)
        weights = par[rows, :]
        weights = weights - learn_rate * (
            fixed_one / (jnp.sqrt(fixed_two) + epsilon_adam) + decay_rate * weights
        )
        new_first[rows, :] = one
        new_second[rows, :] = two
        new_par[rows, :] = weights
        low[rows, :] = weights.astype(bf16)
        new_avg[rows, :] = average_keep * avg[rows, :] + (1.0 - average_keep) * weights


ATOM_AXES = ("far", "near")
PLANE = ("near", "high")
VMEM = pl.BlockSpec(memory_space=pltpu.VMEM)
HBM = pl.BlockSpec(memory_space=pltpu.HBM)
SMEM = pl.BlockSpec(memory_space=pltpu.SMEM)


def scratch(entries):
    return [pltpu.VMEM(shape, dtype) for _, shape, dtype in entries]


def local(
    ranks,
    params,
    first_moment,
    second_moment,
    average,
    edge_vectors,
    owner_rank,
    neighbour_local,
    centre_species,
    neighbour_species,
    live_atoms,
    target_forces,
):
    shape = jax.ShapeDtypeStruct
    flat = (ROWS, 128)
    par = params.reshape(flat)
    live = live_atoms.reshape(1, 1)
    tall = 32 * -(-(3 * ranks + 4) // 32)
    state = [shape(s, t) for _, s, t in STATE]
    sources = (
        edge_vectors.reshape(3, 8, 128),
        owner_rank.reshape(8, 128),
        neighbour_local.reshape(8, 128),
        neighbour_species.reshape(8, 128),
        centre_species.reshape(1, ATOMS),
        target_forces.reshape(3, 1, ATOMS),
        par,
    )
    pay, *kept = pl.pallas_call(
        functools.partial(first_kernel, ranks, ATOM_AXES),
        out_shape=[shape((ranks, tall // 4, 128), f32), *state],
        in_specs=[SMEM] + [HBM] * 7,
        out_specs=[VMEM] * (1 + len(state)),
        scratch_shapes=[
            *[pltpu.VMEM(x.shape, x.dtype) for x in sources],
            pltpu.SemaphoreType.DMA((7,)),
            pltpu.VMEM((tall, 128), f32),
            pltpu.VMEM((6 * ranks, EDGES), bf16),
            *scratch(SCRATCH_A),
        ],
        compiler_params=pltpu.CompilerParams(vmem_limit_bytes=16 * 2**20),
        name="forward",
    )(live, *[pltpu.with_memory_space_constraint(x, pltpu.HBM) for x in sources])
    got = lax.all_to_all(pay, ATOM_AXES, split_axis=0, concat_axis=0, tiled=True)
    keep, give, forces = pl.pallas_call(
        functools.partial(second_kernel, ranks, ATOM_AXES, "low"),
        out_shape=[shape((HALF, 128), f32), shape((HALF, 128), f32), shape((3, 1, ATOMS), f32)],
        in_specs=[SMEM, VMEM] + [VMEM] * len(state),
        out_specs=[VMEM] * 3,
        scratch_shapes=[
            pltpu.VMEM((4 * ranks, 128), f32),
            pltpu.VMEM((3 * ranks, 128), f32),
            *scratch(SCRATCH_B),
        ],
        compiler_params=pltpu.CompilerParams(vmem_limit_bytes=20 * 2**20),
        name="gradient",
    )(live, got, *kept)
    swap = [(0, 1), (1, 0)]
    held = (keep + lax.ppermute(give, "low", swap)).reshape(4, HALF // 4, 128)
    spot = 2 * lax.axis_index("near") + lax.axis_index("high")
    across_plane = [[(i, i ^ k) for i in range(4)] for k in (1, 2, 3)]
    part = lax.dynamic_index_in_dim(held, spot, 0, False)
    for k in (1, 2, 3):
        piece = lax.dynamic_index_in_dim(held, spot ^ k, 0, False)
        part = part + lax.ppermute(piece, PLANE, across_plane[k - 1])
    far = ranks // 2
    if far == 4:
        one, two, three = (lax.ppermute(part, "far", [(i, i ^ k) for i in range(4)]) for k in (1, 2, 3))
        whole = (part + one) + (two + three)
    else:
        whole = jnp.broadcast_to(part[None], (far, *part.shape))
        whole = lax.all_to_all(whole, "far", split_axis=0, concat_axis=0, tiled=True).sum(0)
    mine = jnp.stack([whole] + [lax.ppermute(whole, PLANE, p) for p in across_plane])
    other = lax.ppermute(mine, "low", swap)
    one, vec = shape((1, 1), f32), shape(flat, f32)
    loss, count, norm, new_first, new_second, new_params, low, new_average = pl.pallas_call(
        functools.partial(third_kernel, "low"),
        out_shape=[one, one, one, vec, vec, vec, shape(flat, bf16), vec],
        in_specs=[VMEM] * 6,
        out_specs=[VMEM] * 8,
        scratch_shapes=[pltpu.VMEM((2, 4, HALF // 4, 128), f32)],
        compiler_params=pltpu.CompilerParams(vmem_limit_bytes=16 * 2**20),
        name="update",
    )(
        mine,
        other,
        par,
        first_moment.reshape(flat),
        second_moment.reshape(flat),
        average.reshape(flat),
    )
    return (
        loss.reshape(()),
        count.reshape(()),
        norm.reshape(()),
        forces,
        new_first.reshape(-1),
        new_second.reshape(-1),
        new_params.reshape(-1),
        low.reshape(-1),
        new_average.reshape(-1),
    )


def solution(mesh):
    ranks, groups = mesh.shape["atoms"], mesh.shape["grp"]
    shape = (ranks // 2, 2, groups // 2, 2)
    fine = Mesh(mesh.devices.reshape(shape), ("far", "near", "high", "low"))
    grp, atoms = ("high", "low"), ATOM_AXES
    in_specs = (
        P(),
        P(),
        P(),
        P(),
        P(None, grp, atoms),
        P(grp, atoms, None),
        P(grp, atoms),
        P(grp, atoms),
        P(grp, atoms),
        P(grp, atoms),
        P(None, grp, atoms),
    )
    out_specs = (P(), P(), P(), P(None, grp, atoms), P(), P(), P(), P(), P())
    return jax.shard_map(
        functools.partial(local, ranks),
        mesh=fine,
        in_specs=in_specs,
        out_specs=out_specs,
        check_vma=False,
    )
```

```python
import functools
import math

import jax
import jax.numpy as jnp
from jax import lax
from jax.experimental import pallas as pl
from jax.experimental.pallas import tpu as pltpu
from jax.sharding import Mesh
from jax.sharding import PartitionSpec as P

LATENT = 64
UNITS = 128
CHANNELS = 32
BASES = 8
SPECIES = 5
LAYERS = 3
STEP = 10
NEI = 32
NPARAM = 89344

cutoff_radius = 5.0
clip_level = 0.01
learn_rate = 0.1
beta_one = 0.9
beta_two = 0.999
epsilon_adam = 1e-08
decay_rate = 0.01
average_keep = 0.99
mix = 0.7071

f32 = jnp.float32
bf16 = jnp.bfloat16

ATOMS = 32
EDGES = 1024
TILES = 8
FEAT = 32

AT_EMBED = 0
AT_ENV = 9
AT_INV = AT_ENV + 96
AT_ONE = AT_INV + 144
AT_TWO = AT_ONE + 192
AT_HEAD = AT_TWO + 192
AT_VEC = AT_HEAD + 64
ROWS = AT_VEC + 1
PADDED = 704
HALF = PADDED // 2

STATE = [
    ("wf_emb", (LATENT, 3 * FEAT), bf16),
    ("wf_first", (64, 192), bf16),
    ("wf_lat", (3, 256, 192), bf16),
    ("wf_io", (3, 128, 288), bf16),
    ("wf_s", (3, 192, 384), bf16),
    ("wf_inv", (3, 64, 288), bf16),
    ("wb_hh", (192, 384), bf16),
    ("wb_h", (3, 160, 384), bf16),
    ("wb_p", (3, 192, 192), bf16),
    ("wb_two", (3, 128, 192), bf16),
    ("whcol", (128, 128), f32),
    ("place", (3, 8, 128), f32),
    ("owner", (8, 128), jnp.int32),
    ("hot", (ATOMS, EDGES), bf16),
    ("geo", (10, 8, 128), f32),
    ("bes", (2, BASES, EDGES), f32),
    ("phi", (2 * FEAT, EDGES), bf16),
    ("latx", (4, 128, EDGES), bf16),
    ("pq", (3, 64, EDGES), f32),
    ("vv", (3, 64, EDGES), f32),
    ("ivx", (3, 192, EDGES), bf16),
    ("sx", (3, 256, EDGES), bf16),
    ("s1", (3, 128, EDGES), f32),
    ("t2", (3, 128, EDGES), f32),
    ("oo", (3, 64, EDGES), f32),
    ("ts", (2, 64, EDGES), f32),
    ("th", (128, EDGES), f32),
    ("lb", (3, 64, EDGES), f32),
    ("ob", (3, 128, EDGES), bf16),
    ("hb", (3, 256, EDGES), bf16),
    ("xb", (3, 128, EDGES), f32),
    ("vb", (3, 96, EDGES), f32),
    ("ab", (3, 32, EDGES), f32),
    ("pb", (3, 128, EDGES), bf16),
    ("qq", (3, 32, EDGES), f32),
    ("qb", (3, 32, EDGES), f32),
    ("z1", (64, EDGES), f32),
    ("tz", (64, EDGES), f32),
    ("zb", (128, EDGES), bf16),
    ("sh", (128, EDGES), f32),
    ("h1", (128, EDGES), f32),
    ("h2", (128, EDGES), f32),
    ("hhb", (256, EDGES), bf16),
    ("env", (3, 9, 32, 128), f32),
    ("eh", (3, 8, 32, 128), f32),
    ("bb", (3, 3, 32, 128), f32),
    ("eb", (3, 9, 32, 128), f32),
    ("cot", (3, 11, 32, 128), f32),
]

SCRATCH_A = [
    ("tmp", (11, 128, 128), f32),
    ("wb_emb", (16, 192), bf16),
    ("ybar", (9, 8, 8, 128), f32),
    ("dbar", (8, 8, 128), f32),
]

SCRATCH_B = [
    ("tmp", (8, 128, 128), f32),
    ("part", (320, 256), f32),
    ("mid", (3, 160, 128), f32),
    ("cdir", (3, 8, 128), f32),
    ("gd", (10, 8, 128), f32),
    ("phid", (2 * FEAT, EDGES), bf16),
    ("zd", (64, EDGES), f32),
    ("latd", (4, 128, EDGES), bf16),
    ("pqd", (3, 64, EDGES), f32),
    ("vvd", (3, 64, EDGES), f32),
    ("qd", (3, 32, EDGES), f32),
    ("ivd", (3, 192, EDGES), bf16),
    ("hd", (3, 128, EDGES), f32),
    ("sd", (3, 256, EDGES), bf16),
    ("envd", (3, 9, 32, 128), f32),
    ("ehd", (3, 8, 32, 128), f32),
    ("bd", (3, 3, 32, 128), f32),
    ("hht", (256, EDGES), bf16),
    ("ot", (3, 128, EDGES), bf16),
    ("ht", (3, 256, EDGES), bf16),
    ("qt", (3, 32, EDGES), f32),
    ("pt", (3, 128, EDGES), bf16),
    ("zt", (128, EDGES), bf16),
    ("et", (3, 9, 32, 128), f32),
    ("cott", (11, 32, 128), f32),
    ("grad", (PADDED, 128), f32),
]


class Refs:
    def __init__(self, entries, refs):
        for (name, _, _), ref in zip(entries, refs, strict=True):
            setattr(self, name, ref)


def split(x):
    high = x.astype(bf16)
    return high, (x - high.astype(f32)).astype(bf16)


def product(weights, high, low):
    return jnp.dot(
        weights, jnp.concatenate([high, low, high], 0), preferred_element_type=f32
    )


def put(ref, rows, columns, value, lead=()):
    high, low = split(value)
    half = ref.shape[-2] // 2
    ref[(*lead, slice(rows, rows + value.shape[0]), columns)] = high
    ref[(*lead, slice(half + rows, half + rows + value.shape[0]), columns)] = low
    return high, low


def pair(ref, columns, lead=()):
    half = ref.shape[-2] // 2
    return ref[(*lead, slice(0, half), columns)], ref[(*lead, slice(half, 2 * half), columns)]


def spin(x, amount):
    return pltpu.roll(x, amount % 128, 1)


def group_sum(x):
    x = x + spin(x, 64)
    return x + spin(x, 32)


def lanes(shape):
    return lax.broadcasted_iota(jnp.int32, shape, len(shape) - 1)


def rows_of(shape):
    return lax.broadcasted_iota(jnp.int32, shape, len(shape) - 2)


def silu_parts(h):
    gate = 1.0 / (1.0 + jnp.exp(-h))
    slope = gate * (1.0 - gate)
    return h * gate, gate + h * slope, slope * (2.0 + h * (1.0 - 2.0 * gate))


def geometry(x, y, z):
    d = jnp.sqrt(x * x + y * y + z * z)
    u, v, w = x / d, y / d, z / d
    s = d / cutoff_radius
    s2 = s * s
    s6 = s2 * s2 * s2
    f = 1.0 - 28.0 * s6 + 48.0 * (s6 * s) - 21.0 * (s6 * s2)
    r3, r5, r15 = math.sqrt(3.0), math.sqrt(5.0), math.sqrt(15.0)
    harmonics = [
        r3 * u,
        r3 * v,
        r3 * w,
        r15 * u * v,
        r15 * v * w,
        0.5 * r5 * (3.0 * w * w - 1.0),
        r15 * u * w,
        0.5 * r15 * (u * u - v * v),
    ]
    return d, f, harmonics


def dots(left, right):
    total = left[0] * right[0]
    for a, b in zip(left[1:], right[1:], strict=True):
        total = total + a * b
    return total


def degree(m):
    return 1 if m <= 3 else 2


def atom_terms(envs):
    if len(envs) == 1:
        (one,) = envs
        zero = jnp.zeros_like(one[0])
        return [one[0], zero, zero], one[1:]
    if len(envs) == 2:
        one, two = envs
        return (
            [2.0 * one[0] * two[0], dots(one[1:4], two[1:4]), dots(one[4:], two[4:])],
            [one[0] * two[m] for m in range(1, 9)],
        )
    one, two, three = envs
    both = one[0] * two[0]
    twice = 2.0 * one[0]
    part = [two[0] * one[m] + twice * two[m] for m in range(1, 9)]
    return (
        [4.0 * both * three[0], dots(part[:3], three[1:4]), dots(part[3:], three[4:])],
        [both * three[m] for m in range(1, 9)],
    )


def atom_back(envs, cots):
    return jax.vjp(atom_terms, envs)[1](cots)[0]


def tile(t):
    return slice(128 * t, 128 * t + 128)


def fold(value):
    total = value[0:8]
    for r in range(8, value.shape[0], 8):
        total = total + value[r : r + 8]
    return total


def unpack(packed, count, tmp):
    half = count // 2
    tmp[pl.ds(0, half, stride=2), :] = packed
    tmp[pl.ds(1, half, stride=2), :] = spin(packed, 64)
    value = tmp[0:count, :]
    return jnp.where(lanes(value.shape) < 64, value, spin(value, 64))


def store_64(ref, lead, doubled, at=0):
    high, low = split(doubled)
    rows = slice(at, at + doubled.shape[0])
    ref[(*lead, rows, slice(0, 128))] = high
    ref[(*lead, rows, slice(128, 192))] = low[:, 0:64]


def store_128(ref, lead, value, at=0):
    high, low = split(value)
    rows = slice(at, at + value.shape[0])
    ref[(*lead, rows, slice(0, 128))] = high
    ref[(*lead, rows, slice(128, 256))] = high
    ref[(*lead, rows, slice(256, 384))] = low


def store_96(ref, lead, value):
    high = value.astype(bf16).astype(f32)
    low = value - high
    high_on, low_on = spin(high, 96), spin(low, 64)
    lane = lanes(value.shape)
    ref[(*lead, slice(None), slice(0, 128))] = jnp.where(lane < 96, high, high_on).astype(bf16)
    ref[(*lead, slice(None), slice(128, 256))] = jnp.where(lane < 64, high_on, low_on).astype(bf16)
    ref[(*lead, slice(None), slice(256, 288))] = low_on[:, 0:32].astype(bf16)


def across(ref, index):
    return jnp.concatenate([ref[index, t : t + 1, :] for t in range(TILES)], 1)


def spread_rows(value):
    return jnp.concatenate([value[t : t + 1] for t in range(TILES)], 1)


def joined(grid):
    return jnp.concatenate([jnp.concatenate(row, 1) for row in grid], 0)


def keep_pair(ref, lead, value):
    high, low = split(value)
    half = value.shape[0]
    ref[(*lead, slice(0, half), slice(None))] = high
    ref[(*lead, slice(half, 2 * half), slice(None))] = low
    return high, low


def both(ref, lead=()):
    half = ref.shape[-2] // 2
    return ref[(*lead, slice(0, half), slice(None))], ref[(*lead, slice(half, 2 * half), slice(None))]


def shares(value):
    total = fold(value)
    return [total[:, tile(t)] for t in range(TILES)]


def tmp_rows(w, start):
    return jnp.concatenate([w[start : start + 2], jnp.zeros((14, 128), f32)], 0)


def weights_product(left, right):
    high, low = split(right)
    return product(left, high, low)


def prepare(par, st, sc):
    def turned(value):
        return value.T

    spare = iter(range(11))

    def doubled(at, count):
        return unpack(par[at : at + count // 2, :], count, sc.tmp.at[next(spare)])

    w = doubled(AT_EMBED, 18)
    w = jnp.concatenate([w[0:16], tmp_rows(w, 16)], 0)
    store_64(sc.wb_emb, (), w[0:16])
    high = w.astype(bf16).astype(f32)
    low = w - high
    turn = jnp.concatenate([high, high, low, jnp.zeros((32, 128), f32)], 0).T[0:64]
    st.wf_emb[...] = turn[:, 0 : 3 * FEAT].astype(bf16)
    envs = []
    for k in range(LAYERS):
        w = doubled(AT_ENV + 32 * k, 64)
        envs.append(w)
        store_64(st.wb_p, (k,), w)
        turn = jnp.concatenate([w, w], 0).T[0:64]
        if k == 0:
            store_64(st.wf_first, (), turn)
        else:
            store_64(st.wf_lat, (k - 1,), turn, 128)
    head = par[AT_HEAD : AT_HEAD + 64, :]
    store_128(st.wb_hh, (), head, 128)
    store_64(st.wf_lat, (2,), jnp.concatenate([head, head], 0).T, 128)
    for k in range(LAYERS):
        one = par[AT_ONE + 64 * k : AT_ONE + 64 * k + 64, :]
        store_128(st.wb_h, (k,), one, 96)
        store_64(st.wf_lat, (k,), jnp.concatenate([one, one], 0).T)
        w = doubled(AT_INV + 48 * k, 96)
        store_96(st.wf_inv, (k,), jnp.concatenate([w, jnp.zeros((32, 128), f32)], 0).T[0:64])
        high, low = split(w)
        w = weights_product(jnp.concatenate([high, low[:, 0:64]], 1), one)
        store_128(st.wb_h, (k,), w)
        store_96(st.wf_io, (k,), jnp.concatenate([w, jnp.zeros((32, 128), f32)], 0).T)
        w = doubled(AT_TWO + 64 * k, 128)
        high, low = split(w)
        left = jnp.concatenate([high, low[:, 0:64]], 1)
        st.wb_two[k] = left
        store_128(st.wf_s, (k,), w.T[0:64])
        if k < LAYERS - 1:
            w = weights_product(left, envs[k + 1])
            store_64(st.wb_p, (k + 1,), w, 64)
            store_128(st.wf_s, (k,), w.T[0:64], 64)
        else:
            w = weights_product(left, head)
            store_128(st.wb_hh, (), w)
            store_128(st.wf_s, (k,), w.T, 64)
    st.whcol[...] = jnp.broadcast_to(par[AT_VEC : AT_VEC + 1, :], (128, 128)).T


def sine_parts(turns):
    whole = jnp.round(turns)
    rest = (turns - whole) * math.pi
    odd = whole - 2.0 * jnp.floor(whole * 0.5)
    sign = 1.0 - 2.0 * odd
    r2 = rest * rest
    sine = 0.0
    for n in (13, 11, 9, 7, 5, 3, 1):
        sine = sine * r2 + (-1.0) ** (n // 2) / math.factorial(n)
    cosine = 0.0
    for n in (14, 12, 10, 8, 6, 4, 2, 0):
        cosine = cosine * r2 + (-1.0) ** (n // 2) / math.factorial(n)
    return sign * rest * sine, sign * cosine


def first_kernel(ranks, axis, live, *refs):
    sources = refs[0:7]
    pay = refs[7]
    st = Refs(STATE, refs[8 : 8 + len(STATE)])
    rest = refs[8 + len(STATE) :]
    vec, own, loc, nsp, cen, tgt, par = rest[0:7]
    sems, payload, scatter = rest[7:10]
    sc = Refs(SCRATCH_A, rest[10:])
    me = 2 * lax.axis_index(axis[0]) + lax.axis_index(axis[1])
    copies = [
        pltpu.make_async_copy(source, target, sems.at[n])
        for n, (source, target) in enumerate(zip(sources, rest[0:7], strict=True))
    ]
    for copy in copies:
        copy.start()
    for copy in copies[:6]:
        copy.wait()

    order = sc.tmp.at[10]
    code = ((own[...] * 32 + loc[...]) * 8 + nsp[...]).astype(f32)
    for q, value in enumerate((vec[0], vec[1], vec[2], code)):
        for a in range(4):
            order[pl.ds(32 * q + a, 8, stride=4), :] = spin(value, -32 * a)
    turned = order[...].T
    lane = lanes((8, 128))

    def picked(q):
        out = spin(turned[0:8], -32 * q)
        for g in range(1, 4):
            out = jnp.where(lane // 32 == g, spin(turned[8 * g : 8 * g + 8], 32 * (g - q)), out)
        return out

    xyz = [picked(q) for q in range(3)]
    codes = picked(3).astype(jnp.int32)
    for q in range(3):
        st.place[q] = xyz[q]
    local = lax.shift_right_logical(codes, 3) & 31
    owner = lax.shift_right_logical(codes, 8)
    kind = codes & 7
    st.owner[...] = owner
    sc.dbar[0] = jnp.zeros((8, 128), f32)
    sc.dbar[0, 0:1, 0:32] = cen[...].astype(f32)
    centre_kind = group_sum(sc.dbar[0])[0:1].astype(jnp.int32)

    d, f, harmonics = geometry(*xyz)
    geo = st.geo
    geo[0] = f
    for m in range(8):
        geo[m + 1] = harmonics[m]
    geo[9] = f * (1.0 / math.sqrt(NEI))

    orders = (rows_of((8, 128)) + 1).astype(f32)
    inv_d = 1.0 / d
    scale = math.sqrt(2.0 / cutoff_radius)
    tiles = []
    for t in range(TILES):
        row_inv = inv_d[t : t + 1]
        sine, cosine = sine_parts(orders * (d[t : t + 1] / cutoff_radius))
        b = (scale * sine) * row_inv
        slope = (scale * math.pi / cutoff_radius) * orders * cosine * row_inv - b * row_inv
        st.bes[0, :, tile(t)] = b
        st.bes[1, :, tile(t)] = slope
        row = rows_of((FEAT - 8, 128)) + 8
        hot = (row == centre_kind + 8) | (row == kind[t : t + 1] + 13)
        tiles.append(jnp.concatenate([b * f[t : t + 1], hot.astype(f32)], 0))
        st.hot[:, tile(t)] = (rows_of((ATOMS, 128)) == local[t : t + 1]).astype(f32).astype(bf16)
    phi = keep_pair(st.phi, (), jnp.concatenate(tiles, 1))

    copies[6].wait()
    prepare(par, st, sc)
    fw = spread_rows(f)

    s, s1, s2 = silu_parts(product(st.wf_emb[...], *phi))
    st.z1[...] = s1
    st.tz[...] = s2
    latent = s
    lat = keep_pair(st.latx, (0,), s)
    pq = product(st.wf_first[...], *lat)
    st.pq[0] = pq
    both_of = product(st.wf_lat[0, 0:192, :], *lat)
    base, ahead = both_of[0:128], both_of[128:192]

    for k in range(LAYERS):
        for r in range(0, 32, 16):
            rs = slice(r, r + 16)
            sums = None
            for t in range(TILES):
                a = pq[rs, tile(t)] * geo[9, t : t + 1, :]
                terms = [a] + [a * geo[m, t : t + 1, :] for m in range(1, 9)]
                sums = terms if sums is None else [x + y for x, y in zip(sums, terms, strict=True)]
            for m in range(9):
                st.env[k, m, rs, :] = group_sum(sums[m])
        for r in range(0, 32, 8):
            rs = slice(r, r + 8)
            envs = [[st.env[j, m, rs, :] for m in range(9)] for j in range(k + 1)]
            level, factors = atom_terms(envs)
            for l in range(3):
                st.bb[k, l, rs, :] = level[l]
            for m in range(8):
                st.eh[k, m, rs, :] = factors[m]
        high = [[None] * TILES for _ in range(6)]
        low = [[None] * TILES for _ in range(6)]
        for r in range(0, 32, 16):
            rs = slice(r, r + 16)
            for t in range(TILES):
                ts = tile(t)
                q = pq[32 + r : 48 + r, ts]
                if k > 0:
                    q = mix * st.qq[k - 1, rs, ts] * q
                st.qq[k, rs, ts] = q
                values = [st.bb[k, l, rs, :] for l in range(3)]
                for m in range(1, 9):
                    l = degree(m)
                    values[l] = values[l] + geo[m, t : t + 1, :] * st.eh[k, m - 1, rs, :]
                st.vv[k, rs, ts] = values[1]
                st.vv[k, 32 + r : 48 + r, ts] = values[2]
                for l in range(3):
                    n = 2 * l + r // 16
                    high[n][t], low[n][t] = split(q * values[l])
        high, low = joined(high), joined(low)
        st.ivx[k, 0:96, :] = high
        st.ivx[k, 96:192, :] = low
        h = base + product(st.wf_io[k], high, low)
        s, s1, s2 = silu_parts(h)
        st.s1[k] = s1
        st.t2[k] = s2
        pair_s = keep_pair(st.sx, (k,), s)
        last = k == LAYERS - 1
        both_of = product(st.wf_s[k] if last else st.wf_s[k, 0:128, :], *pair_s)
        o, step = both_of[0:64], both_of[64:]
        if last:
            st.th[...] = step
            hh = ahead + fw * step
        else:
            st.ts[k] = step
            pq = ahead + fw * step
            st.pq[k + 1] = pq
        st.oo[k] = o
        latent = latent + fw * o
        lat = keep_pair(st.latx, (k + 1,), latent)
        if not last:
            both_of = product(st.wf_lat[k + 1] if k + 2 == LAYERS else st.wf_lat[k + 1, 0:192, :], *lat)
            base, ahead = both_of[0:128], both_of[128:]

    s, s1, s2 = silu_parts(hh)
    st.sh[...] = s
    st.h1[...] = s1
    st.h2[...] = s2
    whcol = jnp.concatenate([st.whcol[...]] * TILES, 1)
    back = keep_pair(st.hhb, (), fw * whcol * s1)
    for t, share in enumerate(shares(whcol * s)):
        sc.ybar[0, t] = share
    both_of = product(st.wb_hh[...], *back)
    xb, lb = both_of[0:128], both_of[128:192]

    for k in reversed(range(LAYERS)):
        st.xb[k] = xb
        sb = fw * xb
        pair_h = keep_pair(st.hb, (k,), st.s1[k] * sb)
        st.t2[k] = st.t2[k] * sb
        both_of = product(st.wb_h[k], *pair_h)
        vb, ib = both_of[0:96], both_of[96:160]
        st.vb[k] = vb
        st.lb[k] = lb
        keep_pair(st.ob, (k,), fw * lb)
        for t, share in enumerate(shares(st.oo[k] * lb)):
            sc.ybar[0, t] += share
        run = lb + ib
        if k > 0:
            ahead = product(st.wb_two[k - 1], *split(run))
        for r in range(0, 32, 16):
            rs = slice(r, r + 16)
            sums = None
            for t in range(TILES):
                ts = tile(t)
                q = st.qq[k, rs, ts]
                vs = [vb[32 * l + r : 32 * l + r + 16, ts] for l in range(3)]
                qb = (
                    vs[0] * st.bb[k, 0, rs, :]
                    + vs[1] * st.vv[k, rs, ts]
                    + vs[2] * st.vv[k, 32 + r : 48 + r, ts]
                )
                if k < LAYERS - 1:
                    qb = qb + mix * st.pq[k + 1, 32 + r : 48 + r, ts] * st.qb[k + 1, rs, ts]
                st.qb[k, rs, ts] = qb
                back = [x * q for x in vs]
                terms = list(back)
                for m in range(1, 9):
                    terms.append(back[degree(m)] * geo[m, t : t + 1, :])
                    share = fold(back[degree(m)] * st.eh[k, m - 1, rs, :])
                    if k == LAYERS - 1 and r == 0:
                        sc.ybar[m, t] = share
                    else:
                        sc.ybar[m, t] += share
                sums = terms if sums is None else [x + y for x, y in zip(sums, terms, strict=True)]
            for n in range(11):
                st.cot[k, n, rs, :] = group_sum(sums[n])
        for r in range(0, 32, 8):
            rs = slice(r, r + 8)
            envs = [[st.env[j, m, rs, :] for m in range(9)] for j in range(k + 1)]
            cots = [st.cot[k, n, rs, :] for n in range(11)]
            back = atom_back(envs, (cots[:3], cots[3:]))
            for j in range(k + 1):
                for m in range(9):
                    if k == LAYERS - 1:
                        st.eb[j, m, rs, :] = back[j][m]
                    else:
                        st.eb[j, m, rs, :] += back[j][m]
        high = [[None] * TILES for _ in range(4)]
        low = [[None] * TILES for _ in range(4)]
        for r in range(0, 32, 16):
            rs = slice(r, r + 16)
            for t in range(TILES):
                ts = tile(t)
                p = st.pq[k, rs, ts]
                fs = geo[9, t : t + 1, :]
                a = p * fs
                ab = st.eb[k, 0, rs, :]
                for m in range(1, 9):
                    e = st.eb[k, m, rs, :]
                    ab = ab + geo[m, t : t + 1, :] * e
                    sc.ybar[m, t] += fold(a * e)
                st.ab[k, rs, ts] = ab
                sc.ybar[0, t] += fold((1.0 / math.sqrt(NEI)) * ab * p)
                qb = st.qb[k, rs, ts]
                if k > 0:
                    qb = mix * st.qq[k - 1, rs, ts] * qb
                high[r // 16][t], low[r // 16][t] = split(ab * fs)
                high[2 + r // 16][t], low[2 + r // 16][t] = split(qb)
        high, low = joined(high), joined(low)
        st.pb[k, 0:64, :] = high
        st.pb[k, 64:128, :] = low
        both_of = product(st.wb_p[k] if k > 0 else st.wb_p[k, 0:64, :], high, low)
        lb = run + both_of[0:64]
        if k > 0:
            xb = ahead + both_of[64:192]

    st.tz[...] = st.tz[...] * lb
    pb = product(sc.wb_emb[...], *keep_pair(st.zb, (), st.z1[...] * lb))[0:8]
    for t in range(TILES):
        part = pb[:, tile(t)]
        sc.ybar[0, t] += st.bes[0, :, tile(t)] * part
        sc.dbar[t] = geo[0, t : t + 1, :] * st.bes[1, :, tile(t)] * part

    bars = [jnp.sum(sc.ybar[m], axis=1) for m in range(9)]
    slopes = jax.vjp(geometry, *xyz)[1]((jnp.sum(sc.dbar[...], axis=1), bars[0], bars[1:]))

    for t in range(TILES):
        mine = rows_of((ranks, 128)) == owner[t : t + 1]
        parts = jnp.concatenate([jnp.where(mine, s[t : t + 1], 0.0) for s in slopes], 0)
        high = parts.astype(bf16).astype(f32)
        scatter[:, tile(t)] = jnp.concatenate([high, parts - high], 0).astype(bf16)
    sums = lax.dot_general(
        scatter[...], st.hot[...], (((1,), (1,)), ((), ())), preferred_element_type=f32
    )
    payload[...] = jnp.zeros(payload.shape, f32)
    for q in range(3):
        at = ranks * q
        total = jnp.broadcast_to(jnp.sum(slopes[q], axis=0, keepdims=True), (8, 128))
        total = group_sum(total)[0:1, 0:32]
        part = -(sums[at : at + ranks] + sums[3 * ranks + at : 4 * ranks + at])
        payload[at : at + ranks, 0:32] = part + jnp.where(
            rows_of((ranks, 32)) == me, total, 0.0
        )
    for q in range(3):
        payload[3 * ranks + q : 3 * ranks + q + 1, 0:32] = tgt[q]
    payload[3 * ranks + 3 : 3 * ranks + 4, 0:32] = (lanes((1, 32)) < live[0, 0]).astype(f32)

    deep = pay.shape[1]
    packed = payload[0:deep, :]
    for g in range(1, 4):
        packed = packed + spin(payload[g * deep : g * deep + deep, :], 32 * g)
    payload[0:deep, :] = packed

    def spread(j, carry):
        pay[j] = payload[0:deep, :]
        return carry

    lax.fori_loop(0, ranks, spread, 0)


def cross(x, y):
    return lax.dot_general(x, y, (((1,), (1,)), ((), ())), preferred_element_type=f32)


def settle(full):
    rows, columns = full.shape[0] // 2, full.shape[1] // 2
    if columns == 64:
        return full[:rows] + (spin(full[:rows], 64) + full[rows:])
    return full[:rows, :columns] + (full[:rows, columns:] + full[rows:, :columns])


def pack(value, tmp):
    count = value.shape[0]
    tmp[0:count, :] = value
    even, odd = tmp[pl.ds(0, count // 2, stride=2), :], tmp[pl.ds(1, count // 2, stride=2), :]
    return jnp.where(lanes(even.shape) < 64, even, spin(odd, 64))


def second_kernel(ranks, axis, pick, live, got, *refs):
    st = Refs(STATE, refs[: len(STATE)])
    keep, give, forces, tm, aim = refs[len(STATE) : len(STATE) + 5]
    sc = Refs(SCRATCH_B, refs[len(STATE) + 5 :])
    me = 2 * lax.axis_index(axis[0]) + lax.axis_index(axis[1])
    geo, gd = st.geo, sc.gd

    deep = got.shape[1]
    total = got[0]
    for j in range(1, ranks):
        total = total + got[j]
    first = lanes((deep, 128)) < 32
    total = jnp.concatenate([jnp.where(first, spin(total, -32 * g), 0.0) for g in range(4)], 0)
    for j in range(ranks):
        own = got[j, 3 * ranks - 3 * deep : 3 * ranks - 3 * deep + 4, :]
        for q in range(4):
            tm[q * ranks + j : q * ranks + j + 1, :] = own[q : q + 1]
    tm[...] = jnp.where(lanes((4 * ranks, 128)) < 32, spin(tm[...], -96), 0.0)
    mask = tm[3 * ranks : 4 * ranks, :]
    mine = rows_of((ranks, 128)) == me
    loss = jnp.zeros((ranks, 128), f32)
    centre = []
    for q in range(3):
        at = slice(q * ranks, q * ranks + ranks)
        error = mask * (total[at] - tm[at, :])
        loss = loss + jnp.where(mine, error * error, 0.0)
        forces[q] = jnp.sum(jnp.where(mine, total[at], 0.0), axis=0, keepdims=True)[:, 0:32]
        error = 2.0 * error
        aim[at, :] = error
        own = jnp.sum(jnp.where(mine, error, 0.0), axis=0, keepdims=True)
        centre.append(group_sum(jnp.broadcast_to(own, (8, 128)))[0:1])
    aims = aim[...]
    high = aims.astype(bf16).astype(f32)
    stacked = jnp.concatenate([high, aims - high], 0).astype(bf16)[:, 0:32]
    seen = jnp.dot(stacked, st.hot[...], preferred_element_type=f32)
    seen = seen[0 : 3 * ranks] + seen[3 * ranks :]
    for t in range(TILES):
        at_owner = rows_of((ranks, 128)) == st.owner[t : t + 1, :]
        for q in range(3):
            there = jnp.where(at_owner, seen[q * ranks : q * ranks + ranks, tile(t)], 0.0)
            sc.cdir[q, t : t + 1, :] = centre[q] - jnp.sum(there, axis=0, keepdims=True)

    xyz = tuple(st.place[q] for q in range(3))
    ways = tuple(sc.cdir[q] for q in range(3))
    _, (dd, fd, yd) = jax.jvp(geometry, xyz, ways)
    gd[0] = fd
    for m in range(8):
        gd[m + 1] = yd[m]
    gd[9] = fd * (1.0 / math.sqrt(NEI))
    tiles = []
    for t in range(TILES):
        b, slope = st.bes[0, :, tile(t)], st.bes[1, :, tile(t)]
        row = fd[t : t + 1] * b + (geo[0, t : t + 1, :] * dd[t : t + 1]) * slope
        tiles.append(jnp.concatenate([row, jnp.zeros((FEAT - 8, 128), f32)], 0))
    phid = keep_pair(sc.phid, (), jnp.concatenate(tiles, 1))
    fw, fdw = across(geo, 0), spread_rows(fd)

    zd = product(st.wf_emb[...], *phid)
    sc.zd[...] = zd
    latent = st.z1[...] * zd
    lat = keep_pair(sc.latd, (0,), latent)
    pqd = product(st.wf_first[...], *lat)
    sc.pqd[0] = pqd
    both_of = product(st.wf_lat[0, 0:192, :], *lat)
    base, ahead = both_of[0:128], both_of[128:192]

    for k in range(LAYERS):
        for r in range(0, 32, 16):
            rs = slice(r, r + 16)
            sums = None
            for t in range(TILES):
                ts = tile(t)
                p = st.pq[k, rs, ts]
                a = p * geo[9, t : t + 1, :]
                ad = pqd[rs, ts] * geo[9, t : t + 1, :] + p * gd[9, t : t + 1, :]
                terms = [ad] + [
                    ad * geo[m, t : t + 1, :] + a * gd[m, t : t + 1, :] for m in range(1, 9)
                ]
                sums = terms if sums is None else [x + y for x, y in zip(sums, terms, strict=True)]
            for m in range(9):
                sc.envd[k, m, rs, :] = group_sum(sums[m])
        for r in range(0, 32, 8):
            rs = slice(r, r + 8)
            envs = [[st.env[j, m, rs, :] for m in range(9)] for j in range(k + 1)]
            envds = [[sc.envd[j, m, rs, :] for m in range(9)] for j in range(k + 1)]
            _, (level, factors) = jax.jvp(atom_terms, (envs,), (envds,))
            for l in range(3):
                sc.bd[k, l, rs, :] = level[l]
            for m in range(8):
                sc.ehd[k, m, rs, :] = factors[m]
        high = [[None] * TILES for _ in range(6)]
        low = [[None] * TILES for _ in range(6)]
        for r in range(0, 32, 16):
            rs = slice(r, r + 16)
            ru = slice(32 + r, 48 + r)
            for t in range(TILES):
                ts = tile(t)
                qd = pqd[ru, ts]
                if k > 0:
                    qd = mix * (
                        sc.qd[k - 1, rs, ts] * st.pq[k, ru, ts] + st.qq[k - 1, rs, ts] * qd
                    )
                sc.qd[k, rs, ts] = qd
                q = st.qq[k, rs, ts]
                values = [st.bb[k, 0, rs, :], st.vv[k, rs, ts], st.vv[k, ru, ts]]
                moves = [sc.bd[k, l, rs, :] for l in range(3)]
                for m in range(1, 9):
                    l = degree(m)
                    moves[l] = (
                        moves[l]
                        + geo[m, t : t + 1, :] * sc.ehd[k, m - 1, rs, :]
                        + gd[m, t : t + 1, :] * st.eh[k, m - 1, rs, :]
                    )
                sc.vvd[k, rs, ts] = moves[1]
                sc.vvd[k, ru, ts] = moves[2]
                for l in range(3):
                    n = 2 * l + r // 16
                    high[n][t], low[n][t] = split(qd * values[l] + q * moves[l])
        high, low = joined(high), joined(low)
        sc.ivd[k, 0:96, :] = high
        sc.ivd[k, 96:192, :] = low
        hd = base + product(st.wf_io[k], high, low)
        sc.hd[k] = hd
        pair_s = keep_pair(sc.sd, (k,), st.s1[k] * hd)
        last = k == LAYERS - 1
        both_of = product(st.wf_s[k] if last else st.wf_s[k, 0:128, :], *pair_s)
        od, step = both_of[0:64], both_of[64:]
        if last:
            hhd = ahead + fdw * st.th[...] + fw * step
        else:
            pqd = ahead + fdw * st.ts[k] + fw * step
            sc.pqd[k + 1] = pqd
        latent = latent + fdw * st.oo[k] + fw * od
        lat = keep_pair(sc.latd, (k + 1,), latent)
        if not last:
            both_of = product(st.wf_lat[k + 1] if k + 2 == LAYERS else st.wf_lat[k + 1, 0:192, :], *lat)
            base, ahead = both_of[0:128], both_of[128:]

    whcol = jnp.concatenate([st.whcol[...]] * TILES, 1)
    back = keep_pair(sc.hht, (), whcol * (fdw * st.h1[...] + fw * st.h2[...] * hhd))
    both_of = product(st.wb_hh[...], *back)
    xt, lt = both_of[0:128], both_of[128:192]
    part = fw * st.h1[...] * hhd + fdw * st.sh[...]
    vector = part[:, tile(0)]
    for t in range(1, TILES):
        vector = vector + part[:, tile(t)]
    sc.grad[AT_VEC : AT_VEC + 1, :] = jnp.sum(vector.T, axis=0, keepdims=True)

    queue = []
    spare = [0]

    def work(count):
        for _ in range(min(count, len(queue))):
            queue.pop(0)()

    def single(rows, columns, first, second, finish):
        def begin():
            sc.part[0:rows, 0:columns] = cross(*first())

        def end():
            finish(settle(sc.part[0:rows, 0:columns] + cross(*second())))

        queue.extend((begin, end))

    def plain(at, count):
        def finish(value):
            sc.grad[at : at + count, :] = value

        return finish

    def packed(at, count):
        def finish(value):
            spare[0] = (spare[0] + 1) % 8
            sc.grad[at : at + count, :] = pack(value, sc.tmp.at[spare[0]])[0:count]

        return finish

    def middle(k):
        def finish(value):
            sc.mid[k] = value

        return finish

    def middle_products():
        parts = [split(sc.mid[k, 0:96, :]) for k in range(LAYERS)]
        ones = [product(st.wf_inv[k], *parts[k]) for k in range(LAYERS)]
        invs = []
        for k, (high, low) in enumerate(parts):
            inv = cross(jnp.concatenate([high, low, high], 1), st.wb_h[k, 96:160, :])
            invs.append(jnp.concatenate([inv, jnp.zeros((96, 64), f32)], 1))
        return ones, invs

    def finish_middle(ones, invs):
        for k in range(LAYERS):
            at = AT_ONE + 64 * k
            sc.grad[at : at + 64, :] = sc.mid[k, 96:160, :] + ones[k]
            packed(AT_INV + 48 * k, 48)(invs[k])

    def stack(lat, inv):
        return jnp.concatenate([inv[0:96, :], lat[0:64, :], inv[96:192, :], lat[64:128, :]], 0)

    single(
        128,
        256,
        lambda: (sc.latd[3], st.hhb[...]),
        lambda: (st.latx[3], sc.hht[...]),
        plain(AT_HEAD, 64),
    )

    for k in reversed(range(LAYERS)):
        ht = (fdw * st.xb[k] + fw * xt) * st.s1[k] + st.t2[k] * sc.hd[k]
        pair_h = keep_pair(sc.ht, (k,), ht)
        both_of = product(st.wb_h[k], *pair_h)
        vt, it = both_of[0:96], both_of[96:160]
        keep_pair(sc.ot, (k,), fdw * st.lb[k] + fw * lt)
        run = lt + it
        if k > 0:
            ahead = product(st.wb_two[k - 1], *split(run))
        work(2)
        single(
            320,
            256,
            lambda k=k: (stack(sc.latd[k], sc.ivd[k]), st.hb[k]),
            lambda k=k: (stack(st.latx[k], st.ivx[k]), sc.ht[k]),
            middle(k),
        )
        single(
            256,
            128,
            lambda k=k: (sc.sd[k], st.ob[k]),
            lambda k=k: (st.sx[k], sc.ot[k]),
            packed(AT_TWO + 64 * k, 64),
        )
        for r in range(0, 32, 16):
            rs = slice(r, r + 16)
            ru = slice(32 + r, 48 + r)
            sums = None
            for t in range(TILES):
                ts = tile(t)
                q, qd = st.qq[k, rs, ts], sc.qd[k, rs, ts]
                ls = [slice(32 * l + r, 32 * l + r + 16) for l in range(3)]
                vb = [st.vb[k, s, ts] for s in ls]
                vs = [vt[s, ts] for s in ls]
                qt = (
                    vs[0] * st.bb[k, 0, rs, :]
                    + vs[1] * st.vv[k, rs, ts]
                    + vs[2] * st.vv[k, ru, ts]
                    + vb[0] * sc.bd[k, 0, rs, :]
                    + vb[1] * sc.vvd[k, rs, ts]
                    + vb[2] * sc.vvd[k, ru, ts]
                )
                if k < LAYERS - 1:
                    qt = qt + mix * (
                        sc.pqd[k + 1, ru, ts] * st.qb[k + 1, rs, ts]
                        + st.pq[k + 1, ru, ts] * sc.qt[k + 1, rs, ts]
                    )
                sc.qt[k, rs, ts] = qt
                back = [x * q for x in vb]
                twist = [x * q + y * qd for x, y in zip(vs, vb, strict=True)]
                terms = list(twist)
                for m in range(1, 9):
                    l = degree(m)
                    terms.append(twist[l] * geo[m, t : t + 1, :] + back[l] * gd[m, t : t + 1, :])
                sums = terms if sums is None else [x + y for x, y in zip(sums, terms, strict=True)]
            for n in range(11):
                sc.cott[n, rs, :] = group_sum(sums[n])
        work(1)
        for r in range(0, 32, 8):
            rs = slice(r, r + 8)
            envs = [[st.env[j, m, rs, :] for m in range(9)] for j in range(k + 1)]
            envds = [[sc.envd[j, m, rs, :] for m in range(9)] for j in range(k + 1)]
            cots = [st.cot[k, n, rs, :] for n in range(11)]
            cotts = [sc.cott[n, rs, :] for n in range(11)]
            _, back = jax.jvp(
                atom_back,
                (envs, (cots[:3], cots[3:])),
                (envds, (cotts[:3], cotts[3:])),
            )
            for j in range(k + 1):
                for m in range(9):
                    if k == LAYERS - 1:
                        sc.et[j, m, rs, :] = back[j][m]
                    else:
                        sc.et[j, m, rs, :] += back[j][m]
        work(1)
        high = [[None] * TILES for _ in range(4)]
        low = [[None] * TILES for _ in range(4)]
        for r in range(0, 32, 16):
            rs = slice(r, r + 16)
            for t in range(TILES):
                ts = tile(t)
                at = sc.et[k, 0, rs, :]
                for m in range(1, 9):
                    at = (
                        at
                        + geo[m, t : t + 1, :] * sc.et[k, m, rs, :]
                        + gd[m, t : t + 1, :] * st.eb[k, m, rs, :]
                    )
                qt = sc.qt[k, rs, ts]
                if k > 0:
                    qt = mix * (sc.qd[k - 1, rs, ts] * st.qb[k, rs, ts] + st.qq[k - 1, rs, ts] * qt)
                pt = at * geo[9, t : t + 1, :] + st.ab[k, rs, ts] * gd[9, t : t + 1, :]
                high[r // 16][t], low[r // 16][t] = split(pt)
                high[2 + r // 16][t], low[2 + r // 16][t] = split(qt)
        high, low = joined(high), joined(low)
        sc.pt[k, 0:64, :] = high
        sc.pt[k, 64:128, :] = low
        both_of = product(st.wb_p[k] if k > 0 else st.wb_p[k, 0:64, :], high, low)
        lt = run + both_of[0:64]
        if k > 0:
            xt = ahead + both_of[64:192]
        single(
            128,
            128,
            lambda k=k: (sc.latd[k], st.pb[k]),
            lambda k=k: (st.latx[k], sc.pt[k]),
            packed(AT_ENV + 32 * k, 32),
        )
        work(2)

    keep_pair(sc.zt, (), lt * st.z1[...] + st.tz[...] * sc.zd[...])
    single(
        2 * FEAT,
        128,
        lambda: (sc.phid[...], st.zb[...]),
        lambda: (st.phi[...], sc.zt[...]),
        packed(AT_EMBED, 9),
    )
    work(len(queue))
    finish_middle(*middle_products())
    sc.grad[ROWS:PADDED, :] = jnp.zeros((PADDED - ROWS, 128), f32)
    lane = lanes((1, 128))
    amount = 3.0 * live[0, 0].astype(f32)
    sc.grad[ROWS : ROWS + 1, :] = jnp.where(
        lane == 0, jnp.sum(loss), jnp.where(lane == 1, amount, 0.0)
    )
    half = lax.axis_index(pick)
    keep[...] = sc.grad[pl.ds(pl.multiple_of(half * HALF, HALF), HALF), :]
    give[...] = sc.grad[pl.ds(pl.multiple_of((1 - half) * HALF, HALF), HALF), :]


def third_kernel(pick, mine, other, par, first, second, avg, *outs):
    loss, count, norm, new_first, new_second, new_par, low, new_avg, order = outs
    half = lax.axis_index(pick)
    spot = 2 * lax.axis_index("near") + lax.axis_index("high")
    for k in range(4):
        order[half, spot ^ k] = mine[k]
        order[1 - half, spot ^ k] = other[k]
    lower = jnp.concatenate([order[0, k] for k in range(4)], 0)
    upper = jnp.concatenate([order[1, k] for k in range(4)], 0)
    last = ROWS - HALF
    scalars = upper[last : last + 1]
    loss[...] = scalars[:, 0:1]
    amount = scalars[:, 1:2]
    count[...] = amount
    squares = jnp.sum(lower * lower, keepdims=True) + jnp.sum(
        upper[0:last] * upper[0:last], keepdims=True
    )
    length = jnp.sqrt(squares) / amount
    norm[...] = length
    factor = (clip_level / jnp.maximum(length, clip_level)) / amount
    for start, stop, value in ((0, HALF, lower), (HALF, ROWS, upper[0:last])):
        rows = slice(start, stop)
        gradient = value * factor
        one = beta_one * first[rows, :] + (1.0 - beta_one) * gradient
        two = beta_two * second[rows, :] + (1.0 - beta_two) * gradient * gradient
        fixed_one = one / (1.0 - beta_one**STEP)
        fixed_two = two / (1.0 - beta_two**STEP)
        weights = par[rows, :]
        weights = weights - learn_rate * (
            fixed_one / (jnp.sqrt(fixed_two) + epsilon_adam) + decay_rate * weights
        )
        new_first[rows, :] = one
        new_second[rows, :] = two
        new_par[rows, :] = weights
        low[rows, :] = weights.astype(bf16)
        new_avg[rows, :] = average_keep * avg[rows, :] + (1.0 - average_keep) * weights


ATOM_AXES = ("far", "near")
PLANE = ("near", "high")
VMEM = pl.BlockSpec(memory_space=pltpu.VMEM)
HBM = pl.BlockSpec(memory_space=pltpu.HBM)
SMEM = pl.BlockSpec(memory_space=pltpu.SMEM)


def scratch(entries):
    return [pltpu.VMEM(shape, dtype) for _, shape, dtype in entries]


def local(
    ranks,
    params,
    first_moment,
    second_moment,
    average,
    edge_vectors,
    owner_rank,
    neighbour_local,
    centre_species,
    neighbour_species,
    live_atoms,
    target_forces,
):
    shape = jax.ShapeDtypeStruct
    flat = (ROWS, 128)
    par = params.reshape(flat)
    live = live_atoms.reshape(1, 1)
    tall = 32 * -(-(3 * ranks + 4) // 32)
    state = [shape(s, t) for _, s, t in STATE]
    sources = (
        edge_vectors.reshape(3, 8, 128),
        owner_rank.reshape(8, 128),
        neighbour_local.reshape(8, 128),
        neighbour_species.reshape(8, 128),
        centre_species.reshape(1, ATOMS),
        target_forces.reshape(3, 1, ATOMS),
        par,
    )
    pay, *kept = pl.pallas_call(
        functools.partial(first_kernel, ranks, ATOM_AXES),
        out_shape=[shape((ranks, tall // 4, 128), f32), *state],
        in_specs=[SMEM] + [HBM] * 7,
        out_specs=[VMEM] * (1 + len(state)),
        scratch_shapes=[
            *[pltpu.VMEM(x.shape, x.dtype) for x in sources],
            pltpu.SemaphoreType.DMA((7,)),
            pltpu.VMEM((tall, 128), f32),
            pltpu.VMEM((6 * ranks, EDGES), bf16),
            *scratch(SCRATCH_A),
        ],
        compiler_params=pltpu.CompilerParams(vmem_limit_bytes=16 * 2**20),
        name="forward",
    )(live, *[pltpu.with_memory_space_constraint(x, pltpu.HBM) for x in sources])
    got = lax.all_to_all(pay, ATOM_AXES, split_axis=0, concat_axis=0, tiled=True)
    keep, give, forces = pl.pallas_call(
        functools.partial(second_kernel, ranks, ATOM_AXES, "low"),
        out_shape=[shape((HALF, 128), f32), shape((HALF, 128), f32), shape((3, 1, ATOMS), f32)],
        in_specs=[SMEM, VMEM] + [VMEM] * len(state),
        out_specs=[VMEM] * 3,
        scratch_shapes=[
            pltpu.VMEM((4 * ranks, 128), f32),
            pltpu.VMEM((3 * ranks, 128), f32),
            *scratch(SCRATCH_B),
        ],
        compiler_params=pltpu.CompilerParams(vmem_limit_bytes=20 * 2**20),
        name="gradient",
    )(live, got, *kept)
    swap = [(0, 1), (1, 0)]
    held = (keep + lax.ppermute(give, "low", swap)).reshape(4, HALF // 4, 128)
    spot = 2 * lax.axis_index("near") + lax.axis_index("high")
    across_plane = [[(i, i ^ k) for i in range(4)] for k in (1, 2, 3)]
    part = lax.dynamic_index_in_dim(held, spot, 0, False)
    for k in (1, 2, 3):
        piece = lax.dynamic_index_in_dim(held, spot ^ k, 0, False)
        part = part + lax.ppermute(piece, PLANE, across_plane[k - 1])
    far = ranks // 2
    if far == 4:
        one, two, three = (lax.ppermute(part, "far", [(i, i ^ k) for i in range(4)]) for k in (1, 2, 3))
        whole = (part + one) + (two + three)
    else:
        whole = jnp.broadcast_to(part[None], (far, *part.shape))
        whole = lax.all_to_all(whole, "far", split_axis=0, concat_axis=0, tiled=True).sum(0)
    mine = jnp.stack([whole] + [lax.ppermute(whole, PLANE, p) for p in across_plane])
    other = lax.ppermute(mine, "low", swap)
    one, vec = shape((1, 1), f32), shape(flat, f32)
    loss, count, norm, new_first, new_second, new_params, low, new_average = pl.pallas_call(
        functools.partial(third_kernel, "low"),
        out_shape=[one, one, one, vec, vec, vec, shape(flat, bf16), vec],
        in_specs=[VMEM] * 6,
        out_specs=[VMEM] * 8,
        scratch_shapes=[pltpu.VMEM((2, 4, HALF // 4, 128), f32)],
        compiler_params=pltpu.CompilerParams(vmem_limit_bytes=16 * 2**20),
        name="update",
    )(
        mine,
        other,
        par,
        first_moment.reshape(flat),
        second_moment.reshape(flat),
        average.reshape(flat),
    )
    return (
        loss.reshape(()),
        count.reshape(()),
        norm.reshape(()),
        forces,
        new_first.reshape(-1),
        new_second.reshape(-1),
        new_params.reshape(-1),
        low.reshape(-1),
        new_average.reshape(-1),
    )


def solution(mesh):
    ranks, groups = mesh.shape["atoms"], mesh.shape["grp"]
    shape = (ranks // 2, 2, groups // 2, 2)
    fine = Mesh(mesh.devices.reshape(shape), ("far", "near", "high", "low"))
    grp, atoms = ("high", "low"), ATOM_AXES
    in_specs = (
        P(),
        P(),
        P(),
        P(),
        P(None, grp, atoms),
        P(grp, atoms, None),
        P(grp, atoms),
        P(grp, atoms),
        P(grp, atoms),
        P(grp, atoms),
        P(None, grp, atoms),
    )
    out_specs = (P(), P(), P(), P(None, grp, atoms), P(), P(), P(), P(), P())
    return jax.shard_map(
        functools.partial(local, ranks),
        mesh=fine,
        in_specs=in_specs,
        out_specs=out_specs,
        check_vma=False,
    )
```
